32 devices in a mesh: tau: 2 (over y), aux: 4 (over z), orb: 2 (over x), sub: 2 (over core).
Axes of the slice: x: 2, y: 2, z: 4, core: 2. Of those that a mesh axis runs over, the one named last changes fastest.
Arguments:
- three_center: float32 [4, 2, 2, 64, 4096], P('aux', 'orb', None, None, 'sub'), may hold values from -6 to 6
- occupied_green: float32 [256, 128], P(('tau', 'orb')), parts along dimension 0, may hold values from -0.5 to 0.5
- virtual_green: float32 [256, 128], P(('tau', 'orb')), parts along dimension 0, may hold values from -0.5 to 0.5
- block_list: int32 [2, 2], P('orb'), may hold values from 0 to 1
Outputs:
- chi_values: float32 [512, 256], P(('tau', 'aux', 'orb', 'sub')), parts along dimension 0
The draws below stay inside these ranges and needn't reach their ends.
There are 2 independent parts, one for each index of `tau`. The reference program is written for one: setup_inputs(seed, part) draws one part's arguments, and reference() takes and returns one part's arrays. A program takes and returns all parts, laid end to end along the dimension named above; an argument that names none is the same for every part. Nothing has to cross between parts.
All inputs are finite; a program needn't handle non-finite values.
Results may differ from the reference program's by a relative error of at most 0.0001.
Values sent between devices are 32-bit elements; how exact they have to be, the bound alone decides.
No kernel may reach another device: no remote copies, remote signals or barrier semaphores. Data moves between devices by JAX's collectives and lax.ppermute only.
A program may use at most 64 MiB of HBM per device.

```python
import math
import jax
import jax.numpy as jnp
from jax import lax

OB = 64
AB = 64
KB = 2
NOB = 2
NORB = 128
NAB = 4
NAUXF = 256


def plant(entries, key, least, largest):
    longest = entries.shape.index(max(entries.shape))
    spots = []
    for shift in (0, 1):
        where = [jax.random.randint(jax.random.fold_in(key, axis), (), 0, length) for axis, length in enumerate(entries.shape)]
        where[longest] = (where[longest] + shift) % entries.shape[longest]
        spots.append(tuple(where))
    return entries.at[spots[0]].set(least).at[spots[1]].set(largest)


def level_of(rng, shape, split, smallest, top_value):
    def one(axis_at, blocks):
        draws = jax.random.uniform(jax.random.fold_in(jax.random.fold_in(rng, 6), axis_at), (blocks,), jnp.float32, smallest / len(split), top_value / len(split))
        return jnp.repeat(jnp.exp(draws), shape[axis_at] // blocks).reshape((-1,) + (1,) * (len(shape) - axis_at - 1))

    factor_of = one(*split[0])
    for cut in split[1:]:
        factor_of = factor_of * one(*cut)
    return factor_of


def gaussian(own_key, shape, spread, limit, pieces=(), kind=jnp.bfloat16):
    level = level_of(own_key, shape, pieces, -0.22, 0.18) if pieces else 1.0
    result = jax.random.normal(own_key, shape, jnp.float32) * spread * level
    return jnp.minimum(jnp.maximum(result, -limit), limit).astype(kind)


def setup_inputs(seed: int = 0, part: int = 0) -> dict:
    keys = jax.random.split(jax.random.key(seed), 5)
    part_splits = jax.random.split(jax.random.fold_in(keys[4], part), 5)
    return {
        "three_center": gaussian(keys[0], (NAB, NOB, KB, OB, AB * OB), 1.0, 6.0, ((0, 4), (1, 2), (4, 2)), jnp.float32),
        "occupied_green": gaussian(part_splits[1], (NORB, NORB), (KB * OB) ** -0.5, 0.5, ((0, 2),), jnp.float32),
        "virtual_green": gaussian(part_splits[2], (NORB, NORB), NORB ** -0.5, 0.5, ((0, 2),), jnp.float32),
        "block_list": plant(jax.random.randint(keys[3], (NOB, KB), 0, NOB), jax.random.fold_in(keys[3], 1), 0, NOB - 1).astype(jnp.int32),
    }


def reference(three_center, occupied_green, virtual_green, block_list):
    tensor = three_center.reshape(NAB, NOB, KB, OB, AB, OB)
    occ_cols = jnp.take(occupied_green.reshape(NORB, NOB, OB), block_list.reshape(-1), axis=1)
    occ_cols = occ_cols.reshape(NORB, NOB, KB, OB)
    virt_blocks = virtual_green.reshape(NOB, OB, NOB, OB)
    scale = -2.0 / math.sqrt(NORB * KB * OB)

    def block_step(total, index):
        occ_rows = lax.dynamic_slice_in_dim(occ_cols, index * OB, OB, 0)
        middle = jnp.einsum('lnkm,ankmpw->lnapw', occ_rows, tensor, precision=lax.Precision.HIGHEST)
        chosen = jnp.take(virt_blocks, block_list[index], axis=2)
        product = jnp.einsum('lnapw,nwks->lapks', middle, chosen, precision=lax.Precision.HIGHEST)
        own_blocks = jnp.take(tensor, index, axis=1)
        partial_chi = jnp.einsum('lapks,bksql->apbq', product, own_blocks, precision=lax.Precision.HIGHEST)
        return (total + partial_chi.reshape(NAUXF, NAUXF), None)
    start = jnp.zeros((NAUXF, NAUXF), jnp.float32)
    total, _ = lax.scan(block_step, start, jnp.arange(NOB, dtype=jnp.int32))
    return total * scale
```

```python
import math

import jax
import jax.numpy as jnp
from jax import lax
from jax.sharding import PartitionSpec as P

PRECISION = lax.Precision.HIGH


def gather_orb(block, nob):
    if nob == 1:
        return block[None]
    me = lax.axis_index("orb")
    pieces = [block]
    for shift in range(1, nob):
        pairs = [(source, (source - shift) % nob) for source in range(nob)]
        pieces.append(lax.ppermute(block, "orb", pairs))
    stacked = jnp.stack(pieces)
    order = (jnp.arange(nob) - me) % nob
    return jnp.take(stacked, order, axis=0)


def local(three_center, occupied_green, virtual_green, block_list, nob, npieces):
    slots = three_center.shape[2]
    width = three_center.shape[3]
    columns = three_center.shape[4]
    rows_aux = columns // width
    norb = occupied_green.shape[1]
    own_list = block_list[0]
    flat_tensor = three_center.reshape(slots * width, columns)
    listed = jnp.zeros((8, norb), jnp.float32).at[0, :slots].set(own_list.astype(jnp.float32))
    small = lax.all_gather(jnp.concatenate([virtual_green, listed]), "orb", axis=0, tiled=False)
    virt_full = small[:, :width]
    lists = small[:, width, :slots].astype(jnp.int32)
    tensors = gather_orb(flat_tensor, nob)
    tensor_moved = lax.all_to_all(flat_tensor, ("aux", "sub"), split_axis=0, concat_axis=1, tiled=True)
    occ_sel = jnp.take(occupied_green.reshape(width, nob, width), lists.reshape(-1), axis=1)
    occ_sel = occ_sel.reshape(width, nob, slots * width)
    middle = jnp.einsum("lnm,nmc->lnc", occ_sel, tensors, precision=PRECISION)
    middle_four = middle.reshape(width, nob, rows_aux, width)
    virt_sel = jnp.take(virt_full.reshape(nob, width, nob, width), own_list, axis=2)
    products = jnp.einsum("lnpw,nwks->kspl", middle_four, virt_sel, precision=PRECISION)
    products = products.reshape(slots * width, columns)
    product_moved = lax.all_to_all(products, ("aux", "sub"), split_axis=0, concat_axis=1, tiled=True)
    piece_rows = product_moved.shape[0]
    nauxf = product_moved.shape[1] // width
    partial_chi = jnp.einsum(
        "rpl,rql->pq",
        product_moved.reshape(piece_rows, nauxf, width),
        tensor_moved.reshape(piece_rows, nauxf, width),
        precision=PRECISION,
    )
    partial_chi = partial_chi * (-2.0 / math.sqrt(norb * slots * width))
    pieces = npieces
    received = lax.all_to_all(
        partial_chi.reshape(pieces, nauxf // pieces, nauxf), ("aux", "orb", "sub"), split_axis=0, concat_axis=0, tiled=True
    )
    return received.sum(axis=0)


def solution(mesh):
    nob = mesh.shape["orb"]
    npieces = mesh.shape["aux"] * nob * mesh.shape["sub"]
    in_specs = (
        P("aux", "orb", None, None, "sub"),
        P(("tau", "orb"), None),
        P(("tau", "orb"), None),
        P("orb", None),
    )
    out_specs = P(("tau", "aux", "orb", "sub"), None)

    def run(three_center, occupied_green, virtual_green, block_list):
        return local(three_center, occupied_green, virtual_green, block_list, nob, npieces)

    return jax.shard_map(run, mesh=mesh, in_specs=in_specs, out_specs=out_specs, check_vma=False)
```

```python
import functools
import math

import jax
import jax.numpy as jnp
from jax import lax
from jax.experimental import pallas as pl
from jax.experimental.pallas import tpu as pltpu
from jax.sharding import PartitionSpec as P

VMEM = pl.BlockSpec(memory_space=pltpu.VMEM)
SMEM = pl.BlockSpec(memory_space=pltpu.SMEM)
F32 = jnp.float32
BF16 = jnp.bfloat16
LIST_ROWS = 8
PARAMS = pltpu.CompilerParams(vmem_limit_bytes=48 * 1024 * 1024)


def halves(x):
    high = x.astype(BF16)
    return high, (x - high.astype(F32)).astype(BF16)


def dot(a, b):
    return lax.dot_general(a, b, (((1,), (0,)), ((), ())), preferred_element_type=F32)


def dot_nt(a, b):
    return lax.dot_general(a, b, (((1,), (1,)), ((), ())), preferred_element_type=F32)


def dot_nt3(a, b):
    return dot_nt(a[0], b[0]) + dot_nt(a[0], b[1]) + dot_nt(a[1], b[0])


def prepare(place, tensor_ref, mine_ref, turned, *, share):
    turned[...] = tensor_ref[...].T.reshape(turned.shape)
    start = pl.multiple_of(place[1] * share, share)
    mine_ref[...] = turned[:, pl.ds(start, share), :]


def shifts_of(naux):
    plan = []
    for shift in range(1, naux // 2 + 1):
        if 2 * shift < naux:
            plan.append([(source, (source + shift) % naux) for source in range(naux)])
        else:
            plan.append([(z, z + shift) if z % 2 == 0 else (z + shift, z) for z in range(shift)])
    return plan


def contract(place, greens, *refs, slots, width, share, nob, naux, nt):
    tensors, refs = refs[:nob], refs[nob:]
    mine, refs = refs[:2], refs[2:]
    meets = naux // 2
    pieces_own, refs = refs[:meets], refs[meets:]
    pieces_other, refs = refs[:meets], refs[meets:]
    direct_ref, refs = refs[0], refs[1:]
    back_refs, refs = refs[:meets], refs[meets:]
    acc, spread, side_high, side_low, tensor_high, tensor_low = refs
    me_orb, me_tau, me_sub = place[0], place[1], place[2]
    listed = slots * width
    rows_aux = tensors[0].shape[1] // width
    pairs = rows_aux // 2
    groups = 2 * nt

    def select(block, owner):
        parts = []
        for slot in range(slots):
            entry = greens[0, owner, 2 * width : 2 * width + 1, slot : slot + 1]
            chosen = jnp.zeros((block.shape[0], width), F32)
            for j in range(nob):
                chosen = jnp.where(entry == float(j), block[:, j * width : (j + 1) * width], chosen)
            parts.append(chosen)
        return jnp.concatenate(parts, axis=1)

    for i in range(nob):
        owner = lax.rem(me_orb + i, nob)
        left = []
        for kind in range(2):
            for tau in range(nt):
                start = pl.multiple_of(kind * width + me_tau * share, share)
                left.append(select(greens[tau, me_orb, pl.ds(start, share), :], owner))
        left_high, left_low = halves(jnp.concatenate(left, axis=0))
        high, low = halves(tensors[i][...])
        middle = dot(
            jnp.concatenate([left_high, left_high, left_low], axis=1), jnp.concatenate([high, low, high], axis=0)
        )
        middle_high, middle_low = halves(middle)
        for group in range(groups):
            kind, tau = group // nt, group % nt
            right = select(greens[tau, owner, (1 - kind) * width : (2 - kind) * width, :], me_orb)
            zero = jnp.zeros_like(right)
            right_high, right_low = halves(
                jnp.concatenate(
                    [jnp.concatenate([right, zero], axis=1), jnp.concatenate([zero, right], axis=1)], axis=0
                )
            )

            def stacked(array):
                rows = array[group * share : (group + 1) * share]
                return jnp.concatenate(
                    [rows[:, 2 * width * at : 2 * width * (at + 1)] for at in range(pairs)], axis=0
                )

            rows_high, rows_low = stacked(middle_high), stacked(middle_low)
            result = dot(
                jnp.concatenate([rows_high, rows_high, rows_low], axis=1),
                jnp.concatenate([right_high, right_low, right_high], axis=0),
            )
            if i > 0:
                result = acc[group] + result
            if i < nob - 1:
                acc[group] = result
            else:
                for at in range(pairs):
                    for second in range(2):
                        row = (group * rows_aux + 2 * at + second) * share
                        spread[row : row + share, :] = result[
                            at * share : (at + 1) * share, second * listed : (second + 1) * listed
                        ]

    rows = groups * rows_aux
    for at in range(share):
        high, low = halves(spread[pl.ds(at, rows, stride=share), :])
        side_high[:, at * listed : (at + 1) * listed] = high
        side_low[:, at * listed : (at + 1) * listed] = low
    direct_rows = nt * rows_aux
    side_direct = side_high[:direct_rows], side_low[:direct_rows]
    side_back = side_high[direct_rows:], side_low[direct_rows:]

    blocks = [jnp.zeros((direct_rows, 2 * rows_aux), F32)] * naux
    for shift, sources in enumerate([mine] + list(zip(pieces_own, pieces_other))):
        for which, source in enumerate(sources):
            start = pl.multiple_of(jnp.where(me_sub == which, 0, rows_aux), rows_aux)
            for at in range(share):
                high, low = halves(source[pl.ds(at, rows_aux, stride=share), :])
                tensor_high[shift, pl.ds(start, rows_aux), at * listed : (at + 1) * listed] = high
                tensor_low[shift, pl.ds(start, rows_aux), at * listed : (at + 1) * listed] = low
        tensor = tensor_high[shift], tensor_low[shift]
        blocks[(naux - shift) % naux] = dot_nt3(side_direct, tensor)
        if shift == 0:
            continue
        back = dot_nt3(tensor, side_back)
        parts = []
        for tau in range(nt):
            part = back[:, tau * rows_aux : (tau + 1) * rows_aux]
            zero = jnp.zeros_like(part)
            parts.append(
                jnp.where(
                    me_sub == 0, jnp.concatenate([part, zero], axis=1), jnp.concatenate([zero, part], axis=1)
                )
            )
        back_refs[shift - 1][...] = jnp.concatenate(parts, axis=1)
    direct = jnp.concatenate(blocks, axis=1)
    for tau in range(nt):
        direct_ref[tau] = direct[tau * rows_aux : (tau + 1) * rows_aux]


def assemble(place, direct_ref, *refs):
    back_refs, out_ref = refs[:-1], refs[-1]
    nt, half, _ = direct_ref.shape
    block = back_refs[0].shape[1] // nt
    start = pl.multiple_of(place[2] * half, half)
    for tau in range(nt):
        parts = [ref[:, tau * block : (tau + 1) * block] for ref in back_refs]
        rest = jnp.zeros((block, direct_ref.shape[2] - block * (1 + len(parts))), F32)
        out_ref[tau] = jnp.concatenate([jnp.zeros_like(parts[0])] + parts + [rest], axis=1)
        out_ref[tau, pl.ds(start, half), :] += direct_ref[tau]


def local(three_center, occupied_green, virtual_green, block_list, sizes):
    nt, naux, nob, nsub = sizes
    slots = three_center.shape[2]
    width = three_center.shape[3]
    columns = three_center.shape[4]
    rows_aux = columns // width
    block_aux = rows_aux * nsub
    norb = occupied_green.shape[1]
    listed = slots * width
    share = width // nt
    nauxf = naux * block_aux
    me_orb, me_tau, me_sub, me_aux = (lax.axis_index(axis) for axis in ("orb", "tau", "sub", "aux"))
    place = jnp.stack([me_orb, me_tau, me_sub, me_aux]).astype(jnp.int32)
    tensor = three_center.reshape(listed, columns)

    tensors = [tensor]
    for shift in range(1, nob):
        pairs = [(source, (source - shift) % nob) for source in range(nob)]
        tensors.append(lax.ppermute(tensor, "orb", pairs))

    mine = pl.pallas_call(
        functools.partial(prepare, share=share),
        out_shape=jax.ShapeDtypeStruct((rows_aux, share, listed), F32),
        in_specs=[SMEM, VMEM],
        out_specs=VMEM,
        scratch_shapes=[pltpu.VMEM((rows_aux, width, listed), F32)],
        compiler_params=PARAMS,
        name="prepare",
    )(place, tensor)
    plan = shifts_of(naux)
    pieces = [lax.ppermute(mine, "aux", pairs) for pairs in plan]
    swap = [(source, (source + 1) % nsub) for source in range(nsub)]
    mine_other = lax.ppermute(mine, "sub", swap)

    small = jnp.concatenate(
        [
            occupied_green,
            virtual_green,
            jnp.pad(block_list.astype(F32), ((0, LIST_ROWS - 1), (0, norb - slots))),
        ]
    )
    greens = lax.all_gather(small, ("tau", "orb"), axis=0, tiled=False)
    greens = greens.reshape((nt, nob) + small.shape)

    pieces_other = [lax.ppermute(block, "sub", swap) for block in pieces]
    flat = lambda block: block.reshape(-1, listed)
    groups = 2 * nt
    direct, *backs = pl.pallas_call(
        functools.partial(contract, slots=slots, width=width, share=share, nob=nob, naux=naux, nt=nt),
        out_shape=[jax.ShapeDtypeStruct((nt, rows_aux, nauxf), F32)]
        + [jax.ShapeDtypeStruct((block_aux, nt * block_aux), F32)] * len(plan),
        in_specs=[SMEM] + [VMEM] * (1 + nob + 2 + 2 * len(plan)),
        out_specs=[VMEM] * (1 + len(plan)),
        scratch_shapes=[
            pltpu.VMEM((groups, rows_aux // 2 * share, 2 * listed), F32),
            pltpu.VMEM((groups * rows_aux * share, listed), F32),
            pltpu.VMEM((groups * rows_aux, share * listed), BF16),
            pltpu.VMEM((groups * rows_aux, share * listed), BF16),
            pltpu.VMEM((1 + len(plan), block_aux, share * listed), BF16),
            pltpu.VMEM((1 + len(plan), block_aux, share * listed), BF16),
        ],
        compiler_params=PARAMS,
        name="contract",
    )(place, greens, *tensors, flat(mine), flat(mine_other), *map(flat, pieces), *map(flat, pieces_other))

    returned = [
        lax.ppermute(back, "aux", [(target, source) for source, target in pairs]) for back, pairs in zip(backs, plan)
    ]
    partial_chi = pl.pallas_call(
        assemble,
        out_shape=jax.ShapeDtypeStruct((nt, block_aux, nauxf), F32),
        in_specs=[SMEM] + [VMEM] * (1 + len(plan)),
        out_specs=VMEM,
        compiler_params=PARAMS,
        name="assemble",
    )(place, direct, *returned)
    owners = nt * nob * nsub
    received = lax.all_to_all(
        partial_chi.reshape(owners, nt * block_aux // owners, nauxf),
        ("tau", "orb", "sub"),
        split_axis=0,
        concat_axis=0,
        tiled=True,
    )
    total = received.sum(axis=0) * (-2.0 / math.sqrt(norb * slots * width))
    return jnp.roll(total, me_aux * block_aux, axis=1)


def solution(mesh):
    sizes = tuple(mesh.shape[axis] for axis in ("tau", "aux", "orb", "sub"))
    in_specs = (
        P("aux", "orb", None, None, "sub"),
        P(("tau", "orb"), None),
        P(("tau", "orb"), None),
        P("orb", None),
    )
    out_specs = P(("tau", "aux", "orb", "sub"), None)
    return jax.shard_map(
        functools.partial(local, sizes=sizes), mesh=mesh, in_specs=in_specs, out_specs=out_specs, check_vma=False
    )
```

```python
import functools
import math

import jax
import jax.numpy as jnp
from jax import lax
from jax.experimental import pallas as pl
from jax.experimental.pallas import tpu as pltpu
from jax.sharding import PartitionSpec as P

VMEM = pl.BlockSpec(memory_space=pltpu.VMEM)
SMEM = pl.BlockSpec(memory_space=pltpu.SMEM)
F32 = jnp.float32
BF16 = jnp.bfloat16
LIST_ROWS = 8
PARAMS = pltpu.CompilerParams(vmem_limit_bytes=48 * 1024 * 1024)


def halves(x):
    high = x.astype(BF16)
    return high, (x - high.astype(F32)).astype(BF16)


def dot(a, b):
    return lax.dot_general(a, b, (((1,), (0,)), ((), ())), preferred_element_type=F32)


def dot_nt(a, b):
    return lax.dot_general(a, b, (((1,), (1,)), ((), ())), preferred_element_type=F32)


def dot_nt3(a, b):
    return dot_nt(a[0], b[0]) + dot_nt(a[0], b[1]) + dot_nt(a[1], b[0])


def ring(count, shift):
    return [((target + shift) % count, target) for target in range(count)]


def prepare(place, tensor_ref, token_ref, mine_ref, part_ref, common_ref, turned, *, share):
    part = part_ref.shape[0]
    common = common_ref.shape[0]
    start = pl.multiple_of(place[1] * (part + common), 8)
    part_ref[...] = tensor_ref[pl.ds(start, part), :]
    common_ref[...] = tensor_ref[part : part + common, :]
    turned[...] = tensor_ref[...].T.reshape(turned.shape)
    start = pl.multiple_of(place[1] * share, share)
    mine_ref[...] = turned[:, pl.ds(start, share), :]


def after(block, *tokens):
    return pl.pallas_call(
        lambda *refs: None,
        out_shape=jax.ShapeDtypeStruct(block.shape, block.dtype),
        in_specs=[pl.BlockSpec(memory_space=pl.ANY)] * (1 + len(tokens)),
        out_specs=pl.BlockSpec(memory_space=pl.ANY),
        input_output_aliases={0: 0},
        name="after",
    )(block, *tokens)


def shifts_of(naux):
    plan = []
    for shift in range(1, naux // 2 + 1):
        if 2 * shift < naux:
            plan.append([(source, (source + shift) % naux) for source in range(naux)])
        else:
            plan.append([(z, z + shift) if z % 2 == 0 else (z + shift, z) for z in range(shift)])
    return plan


def select(block, list_rows, slots, width):
    parts = []
    for slot in range(slots):
        entry = list_rows[:1, slot : slot + 1]
        chosen = jnp.zeros((block.shape[0], width), F32)
        for j in range(block.shape[1] // width):
            chosen = jnp.where(entry == float(j), block[:, j * width : (j + 1) * width], chosen)
        parts.append(chosen)
    return jnp.concatenate(parts, axis=1)


def mix(place, greens, i, tensor, slots, width, share):
    nt = greens.shape[0]
    pairs = tensor.shape[1] // (2 * width)
    near_list, far_list = greens[0, 0, 2 * width :, :], greens[0, i, 2 * width :, :]
    which = [lax.rem(tau + nt - place[1], nt) for tau in range(nt)]
    left = []
    for kind in range(2):
        for tau in range(nt):
            start = pl.multiple_of(kind * width + place[1] * share, share)
            left.append(select(greens[which[tau], 0, pl.ds(start, share), :], far_list, slots, width))
    left_high, left_low = halves(jnp.concatenate(left, axis=0))
    high, low = halves(tensor[...])
    middle = dot(
        jnp.concatenate([left_high, left_high, left_low], axis=1), jnp.concatenate([high, low, high], axis=0)
    )
    middle_high, middle_low = halves(middle)
    results = []
    for group in range(2 * nt):
        kind, tau = group // nt, group % nt
        right = select(greens[which[tau], i, (1 - kind) * width : (2 - kind) * width, :], near_list, slots, width)
        zero = jnp.zeros_like(right)
        right_high, right_low = halves(
            jnp.concatenate([jnp.concatenate([right, zero], axis=1), jnp.concatenate([zero, right], axis=1)], axis=0)
        )

        def stacked(array):
            rows = array[group * share : (group + 1) * share]
            return jnp.concatenate([rows[:, 2 * width * at : 2 * width * (at + 1)] for at in range(pairs)], axis=0)

        rows_high, rows_low = stacked(middle_high), stacked(middle_low)
        results.append(
            dot(
                jnp.concatenate([rows_high, rows_high, rows_low], axis=1),
                jnp.concatenate([right_high, right_low, right_high], axis=0),
            )
        )
    return results


def first(place, greens, tensor, acc, *, slots, width, share):
    for group, result in enumerate(mix(place, greens, 0, tensor, slots, width, share)):
        acc[group] = result


def second(place, greens, acc, *refs, slots, width, share):
    refs, (side_high, side_low, spread, tensor) = refs[:-4], refs[-4:]
    listed = slots * width
    groups, tall, _ = acc.shape
    pairs = tall // share
    terms = []
    for i in range(len(refs) // 3):
        direct, shared, over_tau = refs[3 * i : 3 * i + 3]
        part, common = direct.shape[0], shared.shape[0]
        for which, block in enumerate((direct, over_tau)):
            start = jnp.where(place[1] == which, 0, part + common)
            tensor[pl.ds(pl.multiple_of(start, 8), part), :] = block[...]
        tensor[part : part + common, :] = shared[...]
        terms.append(mix(place, greens, 1 + i, tensor, slots, width, share))
    for group in range(groups):
        result = acc[group]
        for term in terms:
            result = result + term[group]
        for at in range(pairs):
            for place_in in range(2):
                row = (group * 2 * pairs + 2 * at + place_in) * share
                spread[row : row + share, :] = result[
                    at * share : (at + 1) * share, place_in * listed : (place_in + 1) * listed
                ]
    rows = groups * 2 * pairs
    for at in range(share):
        high, low = halves(spread[pl.ds(at, rows, stride=share), :])
        side_high[:, at * listed : (at + 1) * listed] = high
        side_low[:, at * listed : (at + 1) * listed] = low


def meet(place, side_high, side_low, own, other, *refs, share, nt):
    outs, (tensor_high, tensor_low) = refs[:-2], refs[-2:]
    listed = own.shape[1]
    rows_aux = own.shape[0] // share
    for which, source in enumerate((own, other)):
        start = pl.multiple_of(jnp.where(place[2] == which, 0, rows_aux), rows_aux)
        for at in range(share):
            high, low = halves(source[pl.ds(at, rows_aux, stride=share), :])
            tensor_high[pl.ds(start, rows_aux), at * listed : (at + 1) * listed] = high
            tensor_low[pl.ds(start, rows_aux), at * listed : (at + 1) * listed] = low
    tensor = tensor_high[...], tensor_low[...]
    rows = nt * rows_aux
    if len(outs) == 2:
        back = dot_nt3(tensor, (side_high[rows:], side_low[rows:]))
        parts = []
        for tau in range(nt):
            part = back[:, tau * rows_aux : (tau + 1) * rows_aux]
            zero = jnp.zeros_like(part)
            parts.append(
                jnp.where(
                    place[2] == 0, jnp.concatenate([part, zero], axis=1), jnp.concatenate([zero, part], axis=1)
                )
            )
        outs[1][...] = jnp.concatenate(parts, axis=1)
    outs[0][...] = dot_nt3((side_high[:rows], side_low[:rows]), tensor)


def assemble(place, *refs, naux, nt):
    refs, out_ref = refs[:-1], refs[-1]
    meets = naux // 2
    directs, backs = refs[: 1 + meets], refs[1 + meets :]
    block = directs[0].shape[1]
    half = directs[0].shape[0] // nt
    start = pl.multiple_of(place[2] * half, half)
    for tau in range(nt):
        here = [jnp.zeros((half, block), F32)] * naux
        for shift, ref in enumerate(directs):
            here[(naux - shift) % naux] = ref[tau * half : (tau + 1) * half, :]
        there = [jnp.zeros((block, block), F32)] * naux
        for shift, ref in enumerate(backs, 1):
            there[shift] = ref[:, tau * block : (tau + 1) * block]
        out_ref[tau] = jnp.concatenate(there, axis=1)
        out_ref[tau, pl.ds(start, half), :] += jnp.concatenate(here, axis=1)


def local(three_center, occupied_green, virtual_green, block_list, sizes):
    nt, naux, nob, nsub = sizes
    slots = three_center.shape[2]
    width = three_center.shape[3]
    columns = three_center.shape[4]
    rows_aux = columns // width
    block_aux = rows_aux * nsub
    norb = occupied_green.shape[1]
    listed = slots * width
    share = width // nt
    nauxf = naux * block_aux
    me_orb, me_tau, me_sub, me_aux = (lax.axis_index(axis) for axis in ("orb", "tau", "sub", "aux"))
    place = jnp.stack([me_orb, me_tau, me_sub, me_aux]).astype(jnp.int32)
    tensor = three_center.reshape(listed, columns)

    small = jnp.concatenate(
        [
            occupied_green,
            virtual_green,
            jnp.pad(block_list.astype(F32), ((0, LIST_ROWS - 1), (0, norb - slots))),
        ]
    )
    row = jnp.stack([small] + [lax.ppermute(small, "orb", ring(nob, shift)) for shift in range(1, nob)])
    greens = jnp.stack([row] + [lax.ppermute(row, "tau", ring(nt, shift)) for shift in range(1, nt)])

    part = listed // 3 // 8 * 8
    common = listed - 2 * part
    mine, part_own, common_own = pl.pallas_call(
        functools.partial(prepare, share=share),
        out_shape=[
            jax.ShapeDtypeStruct(shape, F32)
            for shape in ((rows_aux, share, listed), (part, columns), (common, columns))
        ],
        in_specs=[SMEM, VMEM, pl.BlockSpec(memory_space=pl.ANY)],
        out_specs=[VMEM] * 3,
        scratch_shapes=[pltpu.VMEM((rows_aux, width, listed), F32)],
        compiler_params=PARAMS,
        name="prepare",
    )(place, tensor, row)
    tensors = []
    for shift in range(1, nob):
        direct = after(lax.ppermute(part_own, "orb", ring(nob, shift)), greens)
        over_tau = lax.ppermute(direct, "tau", ring(nt, 1))
        tensors += [direct, lax.ppermute(common_own, "orb", ring(nob, shift)), over_tau]
    plan = shifts_of(naux)
    pieces = [lax.ppermute(mine, "aux", pairs) for pairs in plan]
    swap = ring(nsub, 1)
    mine_other = lax.ppermute(mine, "sub", swap)
    def call(kernel, outs, scratch, flops, *arguments, **options):
        shapes = [jax.ShapeDtypeStruct(shape, kind) for shape, kind in outs]
        size = sum(4 * math.prod(x.shape) for x in arguments)
        return pl.pallas_call(
            functools.partial(kernel, **options),
            out_shape=shapes,
            in_specs=[SMEM] + [VMEM] * len(arguments),
            out_specs=[VMEM] * len(shapes),
            scratch_shapes=[pltpu.VMEM(shape, kind) for shape, kind in scratch],
            compiler_params=PARAMS,
            cost_estimate=pl.CostEstimate(flops=flops, bytes_accessed=size, transcendentals=0),
            name=kernel.__name__,
        )(place, *arguments)

    groups = 2 * nt
    work = 6 * groups * share * columns * listed * 3
    rows = groups * rows_aux
    depth = share * listed
    options = dict(slots=slots, width=width, share=share)
    (acc,) = call(
        first, [((groups, rows_aux // 2 * share, 2 * listed), F32)], [], work, greens, tensor, **options
    )
    side = call(
        second,
        [((rows, depth), BF16)] * 2,
        [((rows * share, listed), F32), ((listed, columns), F32)],
        work * (nob - 1),
        greens,
        acc,
        *tensors,
        **options,
    )
    tokens = [(tensors[-1], mine_other)] + [(side[0],)] * (len(plan) - 1)
    pieces = [after(block, *token) for block, token in zip(pieces, tokens)]
    pieces_other = [lax.ppermute(block, "sub", swap) for block in pieces]
    flat = lambda block: block.reshape(-1, listed)
    turned = [((block_aux, depth), BF16)] * 2
    shape_direct = ((nt * rows_aux, block_aux), F32)
    shape_back = ((block_aux, nt * block_aux), F32)
    work = 6 * rows * block_aux * depth
    (direct,) = call(
        meet, [shape_direct], turned, work, *side, flat(mine), flat(mine_other), share=share, nt=nt
    )
    directs, returned = [direct], []
    for own, other, pairs in zip(pieces, pieces_other, plan):
        direct, back = call(
            meet, [shape_direct, shape_back], turned, work, *side, flat(own), flat(other), share=share, nt=nt
        )
        directs.append(direct)
        returned.append(lax.ppermute(back, "aux", [(target, source) for source, target in pairs]))
    (partial_chi,) = call(
        assemble, [((nt, block_aux, nauxf), F32)], [], 0, *directs, *returned, naux=naux, nt=nt
    )
    owners = nt * nob * nsub
    received = lax.all_to_all(
        partial_chi.reshape(owners, nt * block_aux // owners, nauxf),
        ("tau", "orb", "sub"),
        split_axis=0,
        concat_axis=0,
        tiled=True,
    )
    total = received.sum(axis=0) * (-2.0 / math.sqrt(norb * slots * width))
    return jnp.roll(total, me_aux * block_aux, axis=1)


def solution(mesh):
    sizes = tuple(mesh.shape[axis] for axis in ("tau", "aux", "orb", "sub"))
    in_specs = (
        P("aux", "orb", None, None, "sub"),
        P(("tau", "orb"), None),
        P(("tau", "orb"), None),
        P("orb", None),
    )
    out_specs = P(("tau", "aux", "orb", "sub"), None)
    return jax.shard_map(
        functools.partial(local, sizes=sizes), mesh=mesh, in_specs=in_specs, out_specs=out_specs, check_vma=False
    )
```

```python
import functools
import math

import jax
import jax.numpy as jnp
from jax import lax
from jax.experimental import pallas as pl
from jax.experimental.pallas import tpu as pltpu
from jax.sharding import PartitionSpec as P

VMEM = pl.BlockSpec(memory_space=pltpu.VMEM)
SMEM = pl.BlockSpec(memory_space=pltpu.SMEM)
F32 = jnp.float32
BF16 = jnp.bfloat16
LIST_ROWS = 8
MIB = 1024 * 1024


def halves(x):
    high = x.astype(BF16)
    return high, (x - high.astype(F32)).astype(BF16)


def dot(a, b):
    return lax.dot_general(a, b, (((1,), (0,)), ((), ())), preferred_element_type=F32)


def dot_nt(a, b):
    return lax.dot_general(a, b, (((1,), (1,)), ((), ())), preferred_element_type=F32)


def ring(count, shift):
    return [((target + shift) % count, target) for target in range(count)]


def prepare(place, tensor, occupied, virtual, listed_ref, mine, small, turned, *, share):
    width, norb = occupied.shape
    turned[...] = tensor[...].T.reshape(turned.shape)
    start = pl.multiple_of(place[1] * share, share)
    mine[...] = turned[:, pl.ds(start, share), :]
    small[:width, :] = occupied[...]
    small[width : 2 * width, :] = virtual[...]
    entries = listed_ref[...].astype(F32)
    lanes = lax.broadcasted_iota(jnp.int32, (LIST_ROWS, norb), 1)
    rows = jnp.zeros((LIST_ROWS, norb), F32)
    for slot in range(entries.shape[1]):
        rows = jnp.where(lanes == slot, entries[:, slot : slot + 1], rows)
    small[2 * width :, :] = rows


def hold(block, *refs):
    refs[-1][...] = block[...]


def after(block, *tokens):
    return pl.pallas_call(
        hold,
        out_shape=jax.ShapeDtypeStruct(block.shape, block.dtype),
        in_specs=[VMEM] * (1 + len(tokens)),
        out_specs=VMEM,
        name="hold",
    )(block, *tokens)


def shifts_of(naux):
    plan = []
    for shift in range(1, naux // 2 + 1):
        if 2 * shift < naux:
            plan.append([(source, (source + shift) % naux) for source in range(naux)])
        else:
            plan.append([(z, z + shift) if z % 2 == 0 else (z + shift, z) for z in range(shift)])
    return plan


def select(block, list_rows, slots, width):
    parts = []
    for slot in range(slots):
        entry = list_rows[:1, slot : slot + 1]
        chosen = jnp.zeros((block.shape[0], width), F32)
        for j in range(block.shape[1] // width):
            chosen = jnp.where(entry == float(j), block[:, j * width : (j + 1) * width], chosen)
        parts.append(chosen)
    return jnp.concatenate(parts, axis=1)


def mix(place, near, far, tensor, slots, width, share):
    nt = near.shape[0]
    pairs = tensor.shape[1] // (2 * width)
    near_list, far_list = near[0, 2 * width :, :], far[0, 2 * width :, :]
    which = [lax.rem(tau + nt - place[1], nt) for tau in range(nt)]
    left = []
    for kind in range(2):
        for tau in range(nt):
            start = pl.multiple_of(kind * width + place[1] * share, share)
            left.append(select(near[which[tau], pl.ds(start, share), :], far_list, slots, width))
    left_high, left_low = halves(jnp.concatenate(left, axis=0))
    high, low = halves(tensor[...])
    middle = dot(
        jnp.concatenate([left_high, left_high, left_low], axis=1), jnp.concatenate([high, low, high], axis=0)
    )
    middle_high, middle_low = halves(middle)
    results = []
    for group in range(2 * nt):
        kind, tau = group // nt, group % nt
        right = select(far[which[tau], (1 - kind) * width : (2 - kind) * width, :], near_list, slots, width)
        zero = jnp.zeros_like(right)
        right_high, right_low = halves(
            jnp.concatenate([jnp.concatenate([right, zero], axis=1), jnp.concatenate([zero, right], axis=1)], axis=0)
        )

        def stacked(array):
            rows = array[group * share : (group + 1) * share]
            return jnp.concatenate([rows[:, 2 * width * at : 2 * width * (at + 1)] for at in range(pairs)], axis=0)

        rows_high, rows_low = stacked(middle_high), stacked(middle_low)
        results.append(
            dot(
                jnp.concatenate([rows_high, rows_high, rows_low], axis=1),
                jnp.concatenate([right_high, right_low, right_high], axis=0),
            )
        )
    return results


def first(place, near, tensor, acc, token, *, slots, width, share):
    token[...] = jnp.zeros_like(token)
    for group, result in enumerate(mix(place, near, near, tensor, slots, width, share)):
        acc[group] = result


def second(place, near, acc, *refs, slots, width, share):
    refs, (sides, token, spread) = refs[:-3], refs[-3:]
    tensors, fars = refs[: len(refs) // 2], refs[len(refs) // 2 :]
    token[...] = jnp.zeros_like(token)
    listed = slots * width
    groups, tall, _ = acc.shape
    pairs = tall // share
    total = [acc[group] for group in range(groups)]
    for tensor, far in zip(tensors, fars):
        term = mix(place, near, far, tensor, slots, width, share)
        total = [x + y for x, y in zip(total, term)]
    for group in range(groups):
        for at in range(pairs):
            for place_in in range(2):
                row = (group * 2 * pairs + 2 * at + place_in) * share
                spread[row : row + share, :] = total[group][
                    at * share : (at + 1) * share, place_in * listed : (place_in + 1) * listed
                ]
    rows = groups * 2 * pairs
    for at in range(share):
        high, low = halves(spread[pl.ds(at, rows, stride=share), :])
        sides[:rows, at * listed : (at + 1) * listed] = high
        sides[rows:, at * listed : (at + 1) * listed] = low


def meet(place, sides, own, other, *refs, share, nt, given):
    outs, tensor = refs[given:-1], refs[-1]
    listed = own.shape[1]
    rows_aux = own.shape[0] // share
    block = 2 * rows_aux
    for which, source in enumerate((own, other)):
        start = pl.multiple_of(jnp.where(place[2] == which, 0, rows_aux), rows_aux)
        for at in range(share):
            high, low = halves(source[pl.ds(at, rows_aux, stride=share), :])
            tensor[pl.ds(start, rows_aux), at * listed : (at + 1) * listed] = high
            tensor[pl.ds(block + start, rows_aux), at * listed : (at + 1) * listed] = low
    product = dot_nt(sides[...], tensor[...])
    product = product[:, :block] + product[:, block:]
    product = product[: 2 * nt * rows_aux] + product[2 * nt * rows_aux :]
    outs[0][...] = product[: nt * rows_aux]
    if len(outs) == 2:
        back = product[nt * rows_aux :].T
        parts = []
        for tau in range(nt):
            part = back[:, tau * rows_aux : (tau + 1) * rows_aux]
            zero = jnp.zeros_like(part)
            parts.append(
                jnp.where(
                    place[2] == 0, jnp.concatenate([part, zero], axis=1), jnp.concatenate([zero, part], axis=1)
                )
            )
        outs[1][...] = jnp.concatenate(parts, axis=1)


def assemble(place, *refs, naux, nt):
    refs, out_ref = refs[:-1], refs[-1]
    meets = naux // 2
    directs, backs = refs[: 1 + meets], refs[1 + meets :]
    block = directs[0].shape[1]
    half = directs[0].shape[0] // nt
    start = pl.multiple_of(place[2] * half, half)
    for tau in range(nt):
        here = [jnp.zeros((half, block), F32)] * naux
        for shift, ref in enumerate(directs):
            here[(naux - shift) % naux] = ref[tau * half : (tau + 1) * half, :]
        there = [jnp.zeros((block, block), F32)] * naux
        for shift, ref in enumerate(backs, 1):
            there[shift] = ref[:, tau * block : (tau + 1) * block]
        out_ref[tau] = jnp.concatenate(there, axis=1)
        out_ref[tau, pl.ds(start, half), :] += jnp.concatenate(here, axis=1)


def finish(place, received, out_ref, *, scale):
    total = received[0]
    for i in range(1, received.shape[0]):
        total = total + received[i]
    block = place[4]
    out_ref[...] = pltpu.roll(total * scale, place[3] * block, 1)


def local(three_center, occupied_green, virtual_green, block_list, sizes):
    nt, naux, nob, nsub = sizes
    slots = three_center.shape[2]
    width = three_center.shape[3]
    columns = three_center.shape[4]
    rows_aux = columns // width
    block_aux = rows_aux * nsub
    norb = occupied_green.shape[1]
    listed = slots * width
    share = width // nt
    nauxf = naux * block_aux
    me_orb, me_tau, me_sub, me_aux = (lax.axis_index(axis) for axis in ("orb", "tau", "sub", "aux"))
    place = jnp.stack([me_orb, me_tau, me_sub, me_aux, block_aux]).astype(jnp.int32)
    tensor = three_center.reshape(listed, columns)
    limit = 24 + 3 * max(nob - 2, 0)

    def call(kernel, outs, scratch, flops, *arguments, **options):
        shapes = [jax.ShapeDtypeStruct(shape, kind) for shape, kind in outs]
        size = sum(4 * math.prod(x.shape) for x in arguments)
        return pl.pallas_call(
            functools.partial(kernel, **options),
            out_shape=shapes,
            in_specs=[SMEM] + [VMEM] * len(arguments),
            out_specs=[VMEM] * len(shapes),
            scratch_shapes=[pltpu.VMEM(shape, kind) for shape, kind in scratch],
            compiler_params=pltpu.CompilerParams(vmem_limit_bytes=limit * MIB),
            cost_estimate=pl.CostEstimate(flops=flops, bytes_accessed=size, transcendentals=0),
            name=kernel.__name__,
        )(place, *arguments)

    tensors = [lax.ppermute(tensor, "orb", ring(nob, shift)) for shift in range(1, nob)]
    mine, small = call(
        prepare,
        [((rows_aux, share, listed), F32), ((2 * width + LIST_ROWS, norb), F32)],
        [((rows_aux, width, listed), F32)],
        0,
        tensor,
        occupied_green,
        virtual_green,
        block_list,
        share=share,
    )
    plan = shifts_of(naux)
    pieces = [lax.ppermute(mine, "aux", pairs) for pairs in plan]
    swap = ring(nsub, 1)
    mine_other = lax.ppermute(mine, "sub", swap)
    near = jnp.stack([small] + [lax.ppermute(small, "tau", ring(nt, shift)) for shift in range(1, nt)])
    fars = [lax.ppermute(near, "orb", ring(nob, shift)) for shift in range(1, nob)]

    groups = 2 * nt
    work = 6 * groups * share * columns * listed * 3
    rows = groups * rows_aux
    depth = share * listed
    options = dict(slots=slots, width=width, share=share)
    acc, token = call(
        first,
        [((groups, rows_aux // 2 * share, 2 * listed), F32), ((8, 128), F32)],
        [],
        work,
        near,
        tensor,
        **options,
    )
    sides, token_late = call(
        second,
        [((2 * rows, depth), BF16), ((8, 128), F32)],
        [((rows * share, listed), F32)],
        work * (nob - 1),
        near,
        acc,
        *tensors,
        *fars,
        **options,
    )
    tokens = [(token, mine_other) + tuple(fars[-1:])] + [(token_late,)] * (len(plan) - 1)
    pieces = [after(block, *token) for block, token in zip(pieces, tokens)]
    others = [lax.ppermute(block, "sub", swap) for block in pieces]
    flat = lambda block: block.reshape(-1, listed)
    turned = [((2 * block_aux, depth), BF16)]
    shape_direct = ((nt * rows_aux, block_aux), F32)
    shape_back = ((block_aux, nt * block_aux), F32)
    work = 16 * rows * block_aux * depth
    options = dict(share=share, nt=nt)
    (direct,) = call(meet, [shape_direct], turned, work, sides, flat(mine), flat(mine_other), given=0, **options)
    directs, returned = [direct], []
    for own, other, pairs in zip(pieces, others, plan):
        direct, back = call(meet, [shape_direct, shape_back], turned, work, sides, flat(own), flat(other), given=0, **options)
        directs.append(direct)
        returned.append(lax.ppermute(back, "aux", [(target, source) for source, target in pairs]))
    (partial_chi,) = call(assemble, [((nt, block_aux, nauxf), F32)], [], 0, *directs, *returned, naux=naux, nt=nt)
    owners = nt * nob * nsub
    received = lax.all_to_all(
        partial_chi.reshape(owners, nt * block_aux // owners, nauxf),
        ("tau", "orb", "sub"),
        split_axis=0,
        concat_axis=0,
        tiled=True,
    )
    (chi,) = call(
        finish,
        [((nt * block_aux // owners, nauxf), F32)],
        [],
        0,
        received,
        scale=-2.0 / math.sqrt(norb * slots * width),
    )
    return chi


def solution(mesh):
    sizes = tuple(mesh.shape[axis] for axis in ("tau", "aux", "orb", "sub"))
    in_specs = (
        P("aux", "orb", None, None, "sub"),
        P(("tau", "orb"), None),
        P(("tau", "orb"), None),
        P("orb", None),
    )
    out_specs = P(("tau", "aux", "orb", "sub"), None)
    return jax.shard_map(
        functools.partial(local, sizes=sizes), mesh=mesh, in_specs=in_specs, out_specs=out_specs, check_vma=False
    )
```

```python
import functools
import math

import jax
import jax.numpy as jnp
from jax import lax
from jax.experimental import pallas as pl
from jax.experimental.pallas import tpu as pltpu
from jax.sharding import PartitionSpec as P

VMEM = pl.BlockSpec(memory_space=pltpu.VMEM)
ANY = pl.BlockSpec(memory_space=pl.ANY)
HBM = pl.BlockSpec(memory_space=pltpu.HBM)
SMEM = pl.BlockSpec(memory_space=pltpu.SMEM)
F32 = jnp.float32
BF16 = jnp.bfloat16
LIST_ROWS = 8
MIB = 1024 * 1024


def halves(x):
    high = x.astype(BF16)
    return high, (x - high.astype(F32)).astype(BF16)


def dot(a, b):
    return lax.dot_general(a, b, (((1,), (0,)), ((), ())), preferred_element_type=F32)


def dot_nt(a, b):
    return lax.dot_general(a, b, (((1,), (1,)), ((), ())), preferred_element_type=F32)


def ring(count, shift):
    return [((target + shift) % count, target) for target in range(count)]


def prepare(place, tensor_ref, occupied, virtual, listed_ref, tensor, mine, small, entries, turned, sems, *, share):
    width, norb = occupied.shape
    chunks = sems.shape[0] - 3
    columns = tensor.shape[1] // chunks
    some = columns // width
    loads = [
        pltpu.make_async_copy(
            tensor_ref.at[:, pl.ds(i * columns, columns)], tensor.at[:, pl.ds(i * columns, columns)], sems.at[i]
        )
        for i in range(chunks)
    ]
    loads.append(pltpu.make_async_copy(occupied, small.at[pl.ds(0, width), :], sems.at[chunks]))
    loads.append(pltpu.make_async_copy(virtual, small.at[pl.ds(width, width), :], sems.at[chunks + 1]))
    loads.append(pltpu.make_async_copy(listed_ref, entries, sems.at[chunks + 2]))
    for load in loads:
        load.start()
    start = place[1] * share
    for i in range(chunks):
        loads[i].wait()
        turned[...] = tensor[:, i * columns : (i + 1) * columns].T
        for at in range(share):
            mine[at, i * some : (i + 1) * some, :] = turned[pl.ds(start + at, some, stride=width), :]
    for load in loads[chunks:]:
        load.wait()
    lanes = lax.broadcasted_iota(jnp.int32, (LIST_ROWS, norb), 1)
    rows = jnp.zeros((LIST_ROWS, norb), F32)
    for slot in range(entries.shape[1]):
        rows = jnp.where(lanes == slot, entries[:, slot : slot + 1].astype(F32), rows)
    small[2 * width :, :] = rows


def after(block, *tokens):
    return pl.pallas_call(
        lambda *refs: None,
        out_shape=jax.ShapeDtypeStruct(block.shape, block.dtype),
        in_specs=[ANY] * (1 + len(tokens)),
        out_specs=ANY,
        input_output_aliases={0: 0},
        compiler_params=pltpu.CompilerParams(vmem_limit_bytes=MIB),
        name="after",
    )(block, *tokens)


def shifts_of(naux):
    plan = []
    for shift in range(1, naux // 2 + 1):
        if 2 * shift < naux:
            plan.append([(source, (source + shift) % naux) for source in range(naux)])
        else:
            plan.append([(z, z + shift) if z % 2 == 0 else (z + shift, z) for z in range(shift)])
    return plan


def select(block, list_rows, slots, width):
    parts = []
    for slot in range(slots):
        entry = list_rows[:1, slot : slot + 1]
        chosen = jnp.zeros((block.shape[0], width), F32)
        for j in range(block.shape[1] // width):
            chosen = jnp.where(entry == float(j), block[:, j * width : (j + 1) * width], chosen)
        parts.append(chosen)
    return jnp.concatenate(parts, axis=1)


def mix(place, near, far, tensor, slots, width, share):
    nt = near.shape[0]
    pairs = tensor.shape[1] // (2 * width)
    near_list, far_list = near[0, 2 * width :, :], far[0, 2 * width :, :]
    which = [lax.rem(tau + nt - place[1], nt) for tau in range(nt)]
    left = []
    for kind in range(2):
        for tau in range(nt):
            start = pl.multiple_of(kind * width + place[1] * share, share)
            left.append(select(near[which[tau], pl.ds(start, share), :], far_list, slots, width))
    left_high, left_low = halves(jnp.concatenate(left, axis=0))
    high, low = halves(tensor[...])
    middle = dot(
        jnp.concatenate([left_high, left_high, left_low], axis=1), jnp.concatenate([high, low, high], axis=0)
    )
    middle_high, middle_low = halves(middle)
    results = []
    for group in range(2 * nt):
        kind, tau = group // nt, group % nt
        right = select(far[which[tau], (1 - kind) * width : (2 - kind) * width, :], near_list, slots, width)
        zero = jnp.zeros_like(right)
        right_high, right_low = halves(
            jnp.concatenate([jnp.concatenate([right, zero], axis=1), jnp.concatenate([zero, right], axis=1)], axis=0)
        )

        def stacked(array):
            rows = array[group * share : (group + 1) * share]
            return jnp.concatenate([rows[:, 2 * width * at : 2 * width * (at + 1)] for at in range(pairs)], axis=0)

        rows_high, rows_low = stacked(middle_high), stacked(middle_low)
        results.append(
            dot(
                jnp.concatenate([rows_high, rows_high, rows_low], axis=1),
                jnp.concatenate([right_high, right_low, right_high], axis=0),
            )
        )
    return results


def first(place, near, tensor, acc, token, *, slots, width, share):
    token[...] = jnp.zeros_like(token)
    for group, result in enumerate(mix(place, near, near, tensor, slots, width, share)):
        acc[group] = result


def second(place, near, acc, *refs, slots, width, share):
    refs, (sides, token, spread) = refs[:-3], refs[-3:]
    tensors, fars = refs[: len(refs) // 2], refs[len(refs) // 2 :]
    token[...] = jnp.zeros_like(token)
    listed = slots * width
    groups, tall, _ = acc.shape
    pairs = tall // share
    total = [acc[group] for group in range(groups)]
    for tensor, far in zip(tensors, fars):
        term = mix(place, near, far, tensor, slots, width, share)
        total = [x + y for x, y in zip(total, term)]
    for group in range(groups):
        for at in range(pairs):
            for place_in in range(2):
                row = (group * 2 * pairs + 2 * at + place_in) * share
                spread[row : row + share, :] = total[group][
                    at * share : (at + 1) * share, place_in * listed : (place_in + 1) * listed
                ]
    rows = groups * 2 * pairs
    for at in range(share):
        high, low = halves(spread[pl.ds(at, rows, stride=share), :])
        sides[:rows, at * listed : (at + 1) * listed] = high
        sides[rows:, at * listed : (at + 1) * listed] = low


def meet(place, sides, own, other, *refs, share, nt, given):
    outs, tensor = refs[given:-1], refs[-1]
    listed = own.shape[1]
    rows_aux = own.shape[0] // share
    block = 2 * rows_aux
    for which, source in enumerate((own, other)):
        start = pl.multiple_of(jnp.where(place[2] == which, 0, rows_aux), rows_aux)
        for at in range(share):
            high, low = halves(source[at * rows_aux : (at + 1) * rows_aux, :])
            tensor[pl.ds(start, rows_aux), at * listed : (at + 1) * listed] = high
            tensor[pl.ds(block + start, rows_aux), at * listed : (at + 1) * listed] = low
    product = dot_nt(sides[...], tensor[...])
    product = product[:, :block] + product[:, block:]
    product = product[: 2 * nt * rows_aux] + product[2 * nt * rows_aux :]
    outs[0][...] = product[: nt * rows_aux]
    if len(outs) == 2:
        back = product[nt * rows_aux :].T
        parts = []
        for tau in range(nt):
            part = back[:, tau * rows_aux : (tau + 1) * rows_aux]
            zero = jnp.zeros_like(part)
            parts.append(
                jnp.where(
                    place[2] == 0, jnp.concatenate([part, zero], axis=1), jnp.concatenate([zero, part], axis=1)
                )
            )
        outs[1][...] = jnp.concatenate(parts, axis=1)


def assemble(place, *refs, naux, nt):
    refs, out_ref = refs[:-1], refs[-1]
    meets = naux // 2
    directs, backs = refs[: 1 + meets], refs[1 + meets :]
    block = directs[0].shape[1]
    half = directs[0].shape[0] // nt
    start = pl.multiple_of(place[2] * half, half)
    for tau in range(nt):
        here = [jnp.zeros((half, block), F32)] * naux
        for shift, ref in enumerate(directs):
            here[(naux - shift) % naux] = ref[tau * half : (tau + 1) * half, :]
        there = [jnp.zeros((block, block), F32)] * naux
        for shift, ref in enumerate(backs, 1):
            there[shift] = ref[:, tau * block : (tau + 1) * block]
        out_ref[tau] = jnp.concatenate(there, axis=1)
        out_ref[tau, pl.ds(start, half), :] += jnp.concatenate(here, axis=1)


def local(three_center, occupied_green, virtual_green, block_list, sizes):
    nt, naux, nob, nsub = sizes
    slots = three_center.shape[2]
    width = three_center.shape[3]
    columns = three_center.shape[4]
    rows_aux = columns // width
    block_aux = rows_aux * nsub
    norb = occupied_green.shape[1]
    listed = slots * width
    share = width // nt
    nauxf = naux * block_aux
    me_orb, me_tau, me_sub, me_aux = (lax.axis_index(axis) for axis in ("orb", "tau", "sub", "aux"))
    place = jnp.stack([me_orb, me_tau, me_sub, me_aux]).astype(jnp.int32)
    tensor = three_center.reshape(listed, columns)
    limit = 24 + 3 * max(nob - 2, 0)

    def call(kernel, outs, scratch, flops, *arguments, **options):
        shapes = [jax.ShapeDtypeStruct(shape, kind) for shape, kind in outs]
        size = sum(4 * math.prod(x.shape) for x in arguments)
        return pl.pallas_call(
            functools.partial(kernel, **options),
            out_shape=shapes,
            in_specs=[SMEM] + [VMEM] * len(arguments),
            out_specs=[VMEM] * len(shapes),
            scratch_shapes=[pltpu.VMEM(shape, kind) for shape, kind in scratch],
            compiler_params=pltpu.CompilerParams(vmem_limit_bytes=limit * MIB),
            cost_estimate=pl.CostEstimate(flops=flops, bytes_accessed=size, transcendentals=0),
            name=kernel.__name__,
        )(place, *arguments)

    tensors = [lax.ppermute(tensor, "orb", ring(nob, shift)) for shift in range(1, nob)]
    chunks = 4
    held, mine, small = pl.pallas_call(
        functools.partial(prepare, share=share),
        out_shape=[
            jax.ShapeDtypeStruct(shape, F32)
            for shape in ((listed, columns), (share, rows_aux, listed), (2 * width + LIST_ROWS, norb))
        ],
        in_specs=[SMEM] + [HBM] * 4,
        out_specs=[VMEM] * 3,
        scratch_shapes=[
            pltpu.VMEM(block_list.shape, jnp.int32),
            pltpu.VMEM((columns // chunks, listed), F32),
            pltpu.SemaphoreType.DMA((chunks + 3,)),
        ],
        compiler_params=pltpu.CompilerParams(vmem_limit_bytes=limit * MIB),
        name="prepare",
    )(place, tensor, occupied_green, virtual_green, block_list)
    plan = shifts_of(naux)
    pieces = [lax.ppermute(mine, "aux", pairs) for pairs in plan]
    swap = ring(nsub, 1)
    mine_other = lax.ppermute(mine, "sub", swap)
    near = jnp.stack([small] + [lax.ppermute(small, "tau", ring(nt, shift)) for shift in range(1, nt)])
    fars = [lax.ppermute(near, "orb", ring(nob, shift)) for shift in range(1, nob)]

    groups = 2 * nt
    work = 6 * groups * share * columns * listed * 3
    rows = groups * rows_aux
    depth = share * listed
    options = dict(slots=slots, width=width, share=share)
    acc, token = call(
        first,
        [((groups, rows_aux // 2 * share, 2 * listed), F32), ((8, 128), F32)],
        [],
        work,
        near,
        held,
        **options,
    )
    sides, token_late = call(
        second,
        [((2 * rows, depth), BF16), ((8, 128), F32)],
        [((rows * share, listed), F32)],
        work * (nob - 1),
        near,
        acc,
        *tensors,
        *fars,
        **options,
    )
    tokens = [(token, mine_other) + tuple(fars[-1:])] + [(token_late,)] * (len(plan) - 1)
    pieces = [after(block, *token) for block, token in zip(pieces, tokens)]
    others = [lax.ppermute(block, "sub", swap) for block in pieces]
    flat = lambda block: block.reshape(-1, listed)
    turned = [((2 * block_aux, depth), BF16)]
    shape_direct = ((nt * rows_aux, block_aux), F32)
    shape_back = ((block_aux, nt * block_aux), F32)
    work = 16 * rows * block_aux * depth
    options = dict(share=share, nt=nt)
    (direct,) = call(meet, [shape_direct], turned, work, sides, flat(mine), flat(mine_other), given=0, **options)
    directs, returned = [direct], []
    for own, other, pairs in zip(pieces, others, plan):
        direct, back = call(meet, [shape_direct, shape_back], turned, work, sides, flat(own), flat(other), given=0, **options)
        directs.append(direct)
        returned.append(lax.ppermute(back, "aux", [(target, source) for source, target in pairs]))
    (partial_chi,) = call(assemble, [((nt, block_aux, nauxf), F32)], [], 0, *directs, *returned, naux=naux, nt=nt)
    owners = nt * nob * nsub
    received = lax.all_to_all(
        partial_chi.reshape(owners, nt * block_aux // owners, nauxf),
        ("tau", "orb", "sub"),
        split_axis=0,
        concat_axis=0,
        tiled=True,
    )
    total = received.sum(axis=0) * (-2.0 / math.sqrt(norb * slots * width))
    return jnp.roll(total, me_aux * block_aux, axis=1)


def solution(mesh):
    sizes = tuple(mesh.shape[axis] for axis in ("tau", "aux", "orb", "sub"))
    in_specs = (
        P("aux", "orb", None, None, "sub"),
        P(("tau", "orb"), None),
        P(("tau", "orb"), None),
        P("orb", None),
    )
    out_specs = P(("tau", "aux", "orb", "sub"), None)
    return jax.shard_map(
        functools.partial(local, sizes=sizes), mesh=mesh, in_specs=in_specs, out_specs=out_specs, check_vma=False
    )
```

```python
import functools
import math

import jax
import jax.numpy as jnp
from jax import lax
from jax.experimental import pallas as pl
from jax.experimental.pallas import tpu as pltpu
from jax.sharding import PartitionSpec as P

VMEM = pl.BlockSpec(memory_space=pltpu.VMEM)
ANY = pl.BlockSpec(memory_space=pl.ANY)
HBM = pl.BlockSpec(memory_space=pltpu.HBM)
SMEM = pl.BlockSpec(memory_space=pltpu.SMEM)
F32 = jnp.float32
BF16 = jnp.bfloat16
LIST_ROWS = 8
MIB = 1024 * 1024


def halves(x):
    high = x.astype(BF16)
    return high, (x - high.astype(F32)).astype(BF16)


def dot(a, b):
    return lax.dot_general(a, b, (((1,), (0,)), ((), ())), preferred_element_type=F32)


def dot_nt(a, b):
    return lax.dot_general(a, b, (((1,), (1,)), ((), ())), preferred_element_type=F32)


def ring(count, shift):
    return [((target + shift) % count, target) for target in range(count)]


def prepare(place, tensor, mine, turned, *, share):
    some = mine.shape[1]
    turned[...] = tensor[...].T
    start = place[1] * share
    for at in range(share):
        mine[at] = turned[pl.ds(start + at, some, stride=turned.shape[0] // some), :]


def after(block, *tokens):
    return pl.pallas_call(
        lambda *refs: None,
        out_shape=jax.ShapeDtypeStruct(block.shape, block.dtype),
        in_specs=[ANY] * (1 + len(tokens)),
        out_specs=ANY,
        input_output_aliases={0: 0},
        compiler_params=pltpu.CompilerParams(vmem_limit_bytes=MIB),
        name="after",
    )(block, *tokens)


def shifts_of(naux):
    plan = []
    for shift in range(1, naux // 2 + 1):
        if 2 * shift < naux:
            plan.append([(source, (source + shift) % naux) for source in range(naux)])
        else:
            plan.append([(z, z + shift) if z % 2 == 0 else (z + shift, z) for z in range(shift)])
    return plan


def select(block, list_rows, slots, width):
    parts = []
    for slot in range(slots):
        entry = list_rows[:1, slot : slot + 1]
        chosen = jnp.zeros((block.shape[0], width), F32)
        for j in range(block.shape[1] // width):
            chosen = jnp.where(entry == float(j), block[:, j * width : (j + 1) * width], chosen)
        parts.append(chosen)
    return jnp.concatenate(parts, axis=1)


def mix(place, near, far, tensor, slots, width, share):
    nt = near.shape[0]
    pairs = tensor.shape[1] // (2 * width)
    near_list, far_list = near[0, 2 * width :, :], far[0, 2 * width :, :]
    which = [lax.rem(tau + nt - place[1], nt) for tau in range(nt)]
    left = []
    for kind in range(2):
        for tau in range(nt):
            start = pl.multiple_of(kind * width + place[1] * share, share)
            left.append(select(near[which[tau], pl.ds(start, share), :], far_list, slots, width))
    left_high, left_low = halves(jnp.concatenate(left, axis=0))
    high, low = halves(tensor[...])
    middle = dot(
        jnp.concatenate([left_high, left_high, left_low], axis=1), jnp.concatenate([high, low, high], axis=0)
    )
    middle_high, middle_low = halves(middle)
    results = []
    for group in range(2 * nt):
        kind, tau = group // nt, group % nt
        right = select(far[which[tau], (1 - kind) * width : (2 - kind) * width, :], near_list, slots, width)
        zero = jnp.zeros_like(right)
        right_high, right_low = halves(
            jnp.concatenate([jnp.concatenate([right, zero], axis=1), jnp.concatenate([zero, right], axis=1)], axis=0)
        )

        def stacked(array):
            rows = array[group * share : (group + 1) * share]
            return jnp.concatenate([rows[:, 2 * width * at : 2 * width * (at + 1)] for at in range(pairs)], axis=0)

        rows_high, rows_low = stacked(middle_high), stacked(middle_low)
        results.append(
            dot(
                jnp.concatenate([rows_high, rows_high, rows_low], axis=1),
                jnp.concatenate([right_high, right_low, right_high], axis=0),
            )
        )
    return results


def first(place, near, tensor, acc, token, *, slots, width, share):
    token[...] = jnp.zeros_like(token)
    for group, result in enumerate(mix(place, near, near, tensor, slots, width, share)):
        acc[group] = result


def second(place, near, acc, *refs, slots, width, share):
    refs, (sides, token, spread) = refs[:-3], refs[-3:]
    tensors, fars = refs[: len(refs) // 2], refs[len(refs) // 2 :]
    token[...] = jnp.zeros_like(token)
    listed = slots * width
    groups, tall, _ = acc.shape
    pairs = tall // share
    total = [acc[group] for group in range(groups)]
    for tensor, far in zip(tensors, fars):
        term = mix(place, near, far, tensor, slots, width, share)
        total = [x + y for x, y in zip(total, term)]
    for group in range(groups):
        for at in range(pairs):
            for place_in in range(2):
                row = (group * 2 * pairs + 2 * at + place_in) * share
                spread[row : row + share, :] = total[group][
                    at * share : (at + 1) * share, place_in * listed : (place_in + 1) * listed
                ]
    rows = groups * 2 * pairs
    for at in range(share):
        high, low = halves(spread[pl.ds(at, rows, stride=share), :])
        sides[:rows, at * listed : (at + 1) * listed] = high
        sides[rows:, at * listed : (at + 1) * listed] = low


def meet(place, sides, own, other, *refs, share, nt):
    outs, tensor = refs[:-1], refs[-1]
    listed = own.shape[1]
    rows_aux = own.shape[0] // share
    block = 2 * rows_aux
    for which, source in enumerate((own, other)):
        start = pl.multiple_of(jnp.where(place[2] == which, 0, rows_aux), rows_aux)
        for at in range(share):
            high, low = halves(source[at * rows_aux : (at + 1) * rows_aux, :])
            tensor[pl.ds(start, rows_aux), at * listed : (at + 1) * listed] = high
            tensor[pl.ds(block + start, rows_aux), at * listed : (at + 1) * listed] = low
    product = dot_nt(sides[...], tensor[...])
    product = product[:, :block] + product[:, block:]
    product = product[: 2 * nt * rows_aux] + product[2 * nt * rows_aux :]
    outs[0][...] = product[: nt * rows_aux]
    if len(outs) == 2:
        back = product[nt * rows_aux :].T
        parts = []
        for tau in range(nt):
            part = back[:, tau * rows_aux : (tau + 1) * rows_aux]
            zero = jnp.zeros_like(part)
            parts.append(
                jnp.where(
                    place[2] == 0, jnp.concatenate([part, zero], axis=1), jnp.concatenate([zero, part], axis=1)
                )
            )
        outs[1][...] = jnp.concatenate(parts, axis=1)


def assemble(place, *refs, naux, nt):
    refs, out_ref = refs[:-1], refs[-1]
    count = naux // 2
    directs, backs = refs[:count], refs[count:]
    block = directs[0].shape[1]
    half = directs[0].shape[0] // nt
    start = pl.multiple_of(place[2] * half, half)
    for tau in range(nt):
        here = [jnp.zeros((half, block), F32)] * naux
        for shift, ref in enumerate(directs):
            here[(naux - shift) % naux] = ref[tau * half : (tau + 1) * half, :]
        there = [jnp.zeros((block, block), F32)] * naux
        for shift, ref in enumerate(backs, 1):
            there[shift] = ref[:, tau * block : (tau + 1) * block]
        out_ref[tau] = jnp.concatenate(there, axis=1)
        out_ref[tau, pl.ds(start, half), :] += jnp.concatenate(here, axis=1)


def complete(place, early, direct, back, out_ref):
    nt, block, wide = early.shape
    half = direct.shape[0] // nt
    naux = wide // block
    last = naux // 2
    start = pl.multiple_of(place[2] * half, half)
    for tau in range(nt):
        out_ref[tau] = early[tau]
        out_ref[tau, :, last * block : (last + 1) * block] += back[:, tau * block : (tau + 1) * block]
        at = (naux - last) * block
        out_ref[tau, pl.ds(start, half), at : at + block] += direct[tau * half : (tau + 1) * half, :]


def local(three_center, occupied_green, virtual_green, block_list, sizes):
    nt, naux, nob, nsub = sizes
    slots = three_center.shape[2]
    width = three_center.shape[3]
    columns = three_center.shape[4]
    rows_aux = columns // width
    block_aux = rows_aux * nsub
    norb = occupied_green.shape[1]
    listed = slots * width
    share = width // nt
    nauxf = naux * block_aux
    me_orb, me_tau, me_sub, me_aux = (lax.axis_index(axis) for axis in ("orb", "tau", "sub", "aux"))
    place = jnp.stack([me_orb, me_tau, me_sub, me_aux]).astype(jnp.int32)
    tensor = three_center.reshape(listed, columns)
    limit = 24 + 3 * max(nob - 2, 0)

    def call(kernel, outs, scratch, flops, *arguments, **options):
        shapes = [jax.ShapeDtypeStruct(shape, kind) for shape, kind in outs]
        size = sum(4 * math.prod(x.shape) for x in arguments)
        return pl.pallas_call(
            functools.partial(kernel, **options),
            out_shape=shapes,
            in_specs=[SMEM] + [VMEM] * len(arguments),
            out_specs=[VMEM] * len(shapes),
            scratch_shapes=[pltpu.VMEM(shape, kind) for shape, kind in scratch],
            compiler_params=pltpu.CompilerParams(vmem_limit_bytes=limit * MIB),
            cost_estimate=pl.CostEstimate(flops=flops, bytes_accessed=size, transcendentals=0),
            name=kernel.__name__,
        )(place, *arguments)

    tensors = [lax.ppermute(tensor, "orb", ring(nob, shift)) for shift in range(1, nob)]
    (mine,) = call(
        prepare, [((share, rows_aux, listed), F32)], [((columns, listed), F32)], 0, tensor, share=share
    )
    plan = shifts_of(naux)
    pieces = [lax.ppermute(mine, "aux", pairs) for pairs in plan]
    swap = ring(nsub, 1)
    mine_other = lax.ppermute(mine, "sub", swap)
    small = jnp.concatenate(
        [
            occupied_green,
            virtual_green,
            jnp.pad(block_list.astype(F32), ((0, LIST_ROWS - 1), (0, norb - slots))),
        ]
    )
    near = jnp.stack([small] + [lax.ppermute(small, "tau", ring(nt, shift)) for shift in range(1, nt)])
    fars = []
    for shift in range(1, nob):
        pairs = [(a * nsub + c, b * nsub + (c + 1) % nsub) for a, b in ring(nob, shift) for c in range(nsub)]
        fars.append(lax.ppermute(near, ("orb", "sub"), pairs))

    groups = 2 * nt
    work = 6 * groups * share * columns * listed * 3
    rows = groups * rows_aux
    depth = share * listed
    options = dict(slots=slots, width=width, share=share)
    acc, token = call(
        first,
        [((groups, rows_aux // 2 * share, 2 * listed), F32), ((8, 128), F32)],
        [],
        work,
        near,
        tensor,
        **options,
    )
    sides, token_late = call(
        second,
        [((2 * rows, depth), BF16), ((8, 128), F32)],
        [((rows * share, listed), F32)],
        work * (nob - 1),
        near,
        acc,
        *tensors,
        *fars,
        **options,
    )
    tokens = [(token, mine_other) + tuple(fars[-1:])] + [(token_late,)] * (len(plan) - 1)
    pieces = [after(block, *token) for block, token in zip(pieces, tokens)]
    others = [lax.ppermute(block, "sub", swap) for block in pieces]
    flat = lambda block: block.reshape(-1, listed)
    turned = [((2 * block_aux, depth), BF16)]
    shape_direct = ((nt * rows_aux, block_aux), F32)
    shape_back = ((block_aux, nt * block_aux), F32)
    work = 16 * rows * block_aux * depth
    options = dict(share=share, nt=nt)
    (direct,) = call(meet, [shape_direct], turned, work, sides, flat(mine), flat(mine_other), **options)
    directs, returned = [direct], []
    for own, other, pairs in zip(pieces, others, plan):
        direct, back = call(meet, [shape_direct, shape_back], turned, work, sides, flat(own), flat(other), **options)
        directs.append(direct)
        returned.append(lax.ppermute(back, "aux", [(target, source) for source, target in pairs]))
    shape = ((nt, block_aux, nauxf), F32)
    (early,) = call(assemble, [shape], [], 0, *directs[:-1], *returned[:-1], naux=naux, nt=nt)
    (partial_chi,) = call(complete, [shape], [], 0, early, directs[-1], returned[-1])
    owners = nt * nob * nsub
    received = lax.all_to_all(
        partial_chi.reshape(owners, nt * block_aux // owners, nauxf),
        ("tau", "orb", "sub"),
        split_axis=0,
        concat_axis=0,
        tiled=True,
    )
    total = received.sum(axis=0) * (-2.0 / math.sqrt(norb * slots * width))
    return jnp.roll(total, me_aux * block_aux, axis=1)


def solution(mesh):
    sizes = tuple(mesh.shape[axis] for axis in ("tau", "aux", "orb", "sub"))
    in_specs = (
        P("aux", "orb", None, None, "sub"),
        P(("tau", "orb"), None),
        P(("tau", "orb"), None),
        P("orb", None),
    )
    out_specs = P(("tau", "aux", "orb", "sub"), None)
    return jax.shard_map(
        functools.partial(local, sizes=sizes), mesh=mesh, in_specs=in_specs, out_specs=out_specs, check_vma=False
    )
```

```python
import functools
import math

import jax
import jax.numpy as jnp
from jax import lax
from jax.experimental import pallas as pl
from jax.experimental.pallas import tpu as pltpu
from jax.sharding import PartitionSpec as P

VMEM = pl.BlockSpec(memory_space=pltpu.VMEM)
ANY = pl.BlockSpec(memory_space=pl.ANY)
HBM = pl.BlockSpec(memory_space=pltpu.HBM)
SMEM = pl.BlockSpec(memory_space=pltpu.SMEM)
F32 = jnp.float32
BF16 = jnp.bfloat16
LIST_ROWS = 8
MIB = 1024 * 1024


def halves(x):
    high = x.astype(BF16)
    return high, (x - high.astype(F32)).astype(BF16)


def dot(a, b):
    return lax.dot_general(a, b, (((1,), (0,)), ((), ())), preferred_element_type=F32)


def dot_nt(a, b):
    return lax.dot_general(a, b, (((1,), (1,)), ((), ())), preferred_element_type=F32)


def ring(count, shift):
    return [((target + shift) % count, target) for target in range(count)]


def prepare(place, tensor, mine, turned, *, share):
    some = mine.shape[1]
    turned[...] = tensor[...].T
    start = place[1] * share
    for at in range(share):
        mine[at] = turned[pl.ds(start + at, some, stride=turned.shape[0] // some), :]


def after(block, *tokens):
    return pl.pallas_call(
        lambda *refs: None,
        out_shape=jax.ShapeDtypeStruct(block.shape, block.dtype),
        in_specs=[ANY] * (1 + len(tokens)),
        out_specs=ANY,
        input_output_aliases={0: 0},
        compiler_params=pltpu.CompilerParams(vmem_limit_bytes=MIB),
        name="after",
    )(block, *tokens)


def shifts_of(naux):
    plan = []
    for shift in range(1, naux // 2 + 1):
        if 2 * shift < naux:
            plan.append([(source, (source + shift) % naux) for source in range(naux)])
        else:
            plan.append([(z, z + shift) if z % 2 == 0 else (z + shift, z) for z in range(shift)])
    return plan


def select(block, list_rows, slots, width):
    parts = []
    for slot in range(slots):
        entry = list_rows[:1, slot : slot + 1]
        chosen = jnp.zeros((block.shape[0], width), F32)
        for j in range(block.shape[1] // width):
            chosen = jnp.where(entry == float(j), block[:, j * width : (j + 1) * width], chosen)
        parts.append(chosen)
    return jnp.concatenate(parts, axis=1)


def mix(place, near, far, tensor, slots, width, share):
    nt = near.shape[0]
    pairs = tensor.shape[1] // (2 * width)
    near_list, far_list = near[0, 2 * width :, :], far[0, 2 * width :, :]
    which = [lax.rem(tau + nt - place[1], nt) for tau in range(nt)]
    left = []
    for kind in range(2):
        for tau in range(nt):
            start = pl.multiple_of(kind * width + place[1] * share, share)
            left.append(select(near[which[tau], pl.ds(start, share), :], far_list, slots, width))
    left_high, left_low = halves(jnp.concatenate(left, axis=0))
    high, low = halves(tensor[...])
    middle = dot(
        jnp.concatenate([left_high, left_high, left_low], axis=1), jnp.concatenate([high, low, high], axis=0)
    )
    middle_high, middle_low = halves(middle)
    results = []
    for group in range(2 * nt):
        kind, tau = group // nt, group % nt
        right = select(far[which[tau], (1 - kind) * width : (2 - kind) * width, :], near_list, slots, width)
        zero = jnp.zeros_like(right)
        right_high, right_low = halves(
            jnp.concatenate([jnp.concatenate([right, zero], axis=1), jnp.concatenate([zero, right], axis=1)], axis=0)
        )

        def stacked(array):
            rows = array[group * share : (group + 1) * share]
            return jnp.concatenate([rows[:, 2 * width * at : 2 * width * (at + 1)] for at in range(pairs)], axis=0)

        rows_high, rows_low = stacked(middle_high), stacked(middle_low)
        results.append(
            dot(
                jnp.concatenate([rows_high, rows_high, rows_low], axis=1),
                jnp.concatenate([right_high, right_low, right_high], axis=0),
            )
        )
    return results


def first(place, near, tensor, acc, token, *, slots, width, share):
    token[...] = jnp.zeros_like(token)
    for group, result in enumerate(mix(place, near, near, tensor, slots, width, share)):
        acc[group] = result


def second(place, near, acc, *refs, slots, width, share):
    refs, (sides, token, spread) = refs[:-3], refs[-3:]
    tensors, fars = refs[: len(refs) // 2], refs[len(refs) // 2 :]
    token[...] = jnp.zeros_like(token)
    listed = slots * width
    groups, tall, _ = acc.shape
    pairs = tall // share
    total = [acc[group] for group in range(groups)]
    for tensor, far in zip(tensors, fars):
        term = mix(place, near, far, tensor, slots, width, share)
        total = [x + y for x, y in zip(total, term)]
    for group in range(groups):
        for at in range(pairs):
            for place_in in range(2):
                row = (group * 2 * pairs + 2 * at + place_in) * share
                spread[row : row + share, :] = total[group][
                    at * share : (at + 1) * share, place_in * listed : (place_in + 1) * listed
                ]
    rows = groups * 2 * pairs
    for at in range(share):
        high, low = halves(spread[pl.ds(at, rows, stride=share), :])
        sides[:rows, at * listed : (at + 1) * listed] = high
        sides[rows:, at * listed : (at + 1) * listed] = low


def meet(place, sides, own, other, *refs, share, nt):
    outs, tensor = refs[:-1], refs[-1]
    listed = own.shape[1]
    rows_aux = own.shape[0] // share
    block = 2 * rows_aux
    for which, source in enumerate((own, other)):
        start = pl.multiple_of(jnp.where(place[2] == which, 0, rows_aux), rows_aux)
        for at in range(share):
            high, low = halves(source[at * rows_aux : (at + 1) * rows_aux, :])
            tensor[pl.ds(start, rows_aux), at * listed : (at + 1) * listed] = high
            tensor[pl.ds(block + start, rows_aux), at * listed : (at + 1) * listed] = low
    product = dot_nt(sides[...], tensor[...])
    product = product[:, :block] + product[:, block:]
    product = product[: 2 * nt * rows_aux] + product[2 * nt * rows_aux :]
    outs[0][...] = product[: nt * rows_aux]
    if len(outs) == 2:
        back = product[nt * rows_aux :].T
        parts = []
        for tau in range(nt):
            part = back[:, tau * rows_aux : (tau + 1) * rows_aux]
            zero = jnp.zeros_like(part)
            parts.append(
                jnp.where(
                    place[2] == 0, jnp.concatenate([part, zero], axis=1), jnp.concatenate([zero, part], axis=1)
                )
            )
        outs[1][...] = jnp.concatenate(parts, axis=1)


def assemble(place, *refs, naux, nt):
    refs, out_ref = refs[:-1], refs[-1]
    count = naux // 2
    directs, backs = refs[:count], refs[count:]
    block = directs[0].shape[1]
    half = directs[0].shape[0] // nt
    start = pl.multiple_of(place[2] * half, half)
    for tau in range(nt):
        here = [jnp.zeros((half, block), F32)] * naux
        for shift, ref in enumerate(directs):
            here[(naux - shift) % naux] = ref[tau * half : (tau + 1) * half, :]
        there = [jnp.zeros((block, block), F32)] * naux
        for shift, ref in enumerate(backs, 1):
            there[shift] = ref[:, tau * block : (tau + 1) * block]
        out_ref[tau] = jnp.concatenate(there, axis=1)
        out_ref[tau, pl.ds(start, half), :] += jnp.concatenate(here, axis=1)


def complete(place, early, direct, back, out_ref):
    nt, block, wide = early.shape
    half = direct.shape[0] // nt
    naux = wide // block
    last = naux // 2
    start = pl.multiple_of(place[2] * half, half)
    for tau in range(nt):
        out_ref[tau] = early[tau]
        out_ref[tau, :, last * block : (last + 1) * block] += back[:, tau * block : (tau + 1) * block]
        at = (naux - last) * block
        out_ref[tau, pl.ds(start, half), at : at + block] += direct[tau * half : (tau + 1) * half, :]


def local(three_center, occupied_green, virtual_green, block_list, sizes):
    nt, naux, nob, nsub = sizes
    slots = three_center.shape[2]
    width = three_center.shape[3]
    columns = three_center.shape[4]
    rows_aux = columns // width
    block_aux = rows_aux * nsub
    norb = occupied_green.shape[1]
    listed = slots * width
    share = width // nt
    nauxf = naux * block_aux
    me_orb, me_tau, me_sub, me_aux = (lax.axis_index(axis) for axis in ("orb", "tau", "sub", "aux"))
    place = jnp.stack([me_orb, me_tau, me_sub, me_aux]).astype(jnp.int32)
    tensor = three_center.reshape(listed, columns)
    limit = 24 + 3 * max(nob - 2, 0)

    def call(kernel, outs, scratch, flops, *arguments, **options):
        shapes = [jax.ShapeDtypeStruct(shape, kind) for shape, kind in outs]
        size = sum(4 * math.prod(x.shape) for x in arguments)
        return pl.pallas_call(
            functools.partial(kernel, **options),
            out_shape=shapes,
            in_specs=[SMEM] + [VMEM] * len(arguments),
            out_specs=[VMEM] * len(shapes),
            scratch_shapes=[pltpu.VMEM(shape, kind) for shape, kind in scratch],
            compiler_params=pltpu.CompilerParams(vmem_limit_bytes=limit * MIB),
            cost_estimate=pl.CostEstimate(flops=flops, bytes_accessed=size, transcendentals=0),
            name=kernel.__name__,
        )(place, *arguments)

    tensors = [lax.ppermute(tensor, "orb", ring(nob, shift)) for shift in range(1, nob)]
    (mine,) = call(
        prepare, [((share, rows_aux, listed), F32)], [((columns, listed), F32)], 0, tensor, share=share
    )
    plan = shifts_of(naux)
    pieces = [lax.ppermute(mine, "aux", pairs) for pairs in plan]
    swap = ring(nsub, 1)
    mine_other = lax.ppermute(mine, "sub", swap)
    small = jnp.concatenate(
        [
            occupied_green,
            virtual_green,
            jnp.pad(block_list.astype(F32), ((0, LIST_ROWS - 1), (0, norb - slots))),
        ]
    )
    near = jnp.stack([small] + [lax.ppermute(small, "tau", ring(nt, shift)) for shift in range(1, nt)])
    fars = []
    for shift in range(1, nob):
        pairs = [(a * nsub + c, b * nsub + (c + 1) % nsub) for a, b in ring(nob, shift) for c in range(nsub)]
        fars.append(lax.ppermute(near, ("orb", "sub"), pairs))

    groups = 2 * nt
    work = 6 * groups * share * columns * listed * 3
    rows = groups * rows_aux
    depth = share * listed
    options = dict(slots=slots, width=width, share=share)
    acc, token = call(
        first,
        [((groups, rows_aux // 2 * share, 2 * listed), F32), ((8, 128), F32)],
        [],
        work,
        near,
        tensor,
        **options,
    )
    sides, token_late = call(
        second,
        [((2 * rows, depth), BF16), ((8, 128), F32)],
        [((rows * share, listed), F32)],
        work * (nob - 1),
        near,
        acc,
        *tensors,
        *fars,
        **options,
    )
    tokens = [(token, mine_other) + tuple(fars[-1:])] + [(token_late,)] * (len(plan) - 1)
    pieces = [after(block, *token) for block, token in zip(pieces, tokens)]
    others = [lax.ppermute(block, "sub", swap) for block in pieces]
    flat = lambda block: block.reshape(-1, listed)
    turned = [((2 * block_aux, depth), BF16)]
    shape_direct = ((nt * rows_aux, block_aux), F32)
    shape_back = ((block_aux, nt * block_aux), F32)
    work = 16 * rows * block_aux * depth
    options = dict(share=share, nt=nt)
    (direct,) = call(meet, [shape_direct], turned, work, sides, flat(mine), flat(mine_other), **options)
    directs, returned = [direct], []
    for own, other in zip(pieces, others):
        direct, back = call(meet, [shape_direct, shape_back], turned, work, sides, flat(own), flat(other), **options)
        directs.append(direct)
        returned.append(lax.ppermute(back, "aux", ring(naux, len(directs) - 1)))
    shape = ((nt, block_aux, nauxf), F32)
    (early,) = call(assemble, [shape], [], 0, *directs[:-1], *returned[:-1], naux=naux, nt=nt)
    (partial_chi,) = call(complete, [shape], [], 0, early, directs[-1], returned[-1])
    owners = nt * nob * nsub
    received = lax.all_to_all(
        partial_chi.reshape(owners, nt * block_aux // owners, nauxf),
        ("tau", "orb", "sub"),
        split_axis=0,
        concat_axis=0,
        tiled=True,
    )
    total = received.sum(axis=0) * (-2.0 / math.sqrt(norb * slots * width))
    return jnp.roll(total, me_aux * block_aux, axis=1)


def solution(mesh):
    sizes = tuple(mesh.shape[axis] for axis in ("tau", "aux", "orb", "sub"))
    in_specs = (
        P("aux", "orb", None, None, "sub"),
        P(("tau", "orb"), None),
        P(("tau", "orb"), None),
        P("orb", None),
    )
    out_specs = P(("tau", "aux", "orb", "sub"), None)
    return jax.shard_map(
        functools.partial(local, sizes=sizes), mesh=mesh, in_specs=in_specs, out_specs=out_specs, check_vma=False
    )
```

```python
import functools
import math

import jax
import jax.numpy as jnp
from jax import lax
from jax.experimental import pallas as pl
from jax.experimental.pallas import tpu as pltpu
from jax.sharding import PartitionSpec as P

VMEM = pl.BlockSpec(memory_space=pltpu.VMEM)
ANY = pl.BlockSpec(memory_space=pl.ANY)
HBM = pl.BlockSpec(memory_space=pltpu.HBM)
SMEM = pl.BlockSpec(memory_space=pltpu.SMEM)
F32 = jnp.float32
BF16 = jnp.bfloat16
LIST_ROWS = 8
MIB = 1024 * 1024


def halves(x):
    high = x.astype(BF16)
    return high, (x - high.astype(F32)).astype(BF16)


def dot(a, b):
    return lax.dot_general(a, b, (((1,), (0,)), ((), ())), preferred_element_type=F32)


def dot_nt(a, b):
    return lax.dot_general(a, b, (((1,), (1,)), ((), ())), preferred_element_type=F32)


def ring(count, shift):
    return [((target + shift) % count, target) for target in range(count)]


def prepare(place, tensor, mine, turned, *, share):
    some = mine.shape[1]
    turned[...] = tensor[...].T
    start = place[1] * share
    for at in range(share):
        mine[at] = turned[pl.ds(start + at, some, stride=turned.shape[0] // some), :]


def after(block, *tokens):
    return pl.pallas_call(
        lambda *refs: None,
        out_shape=jax.ShapeDtypeStruct(block.shape, block.dtype),
        in_specs=[ANY] * (1 + len(tokens)),
        out_specs=ANY,
        input_output_aliases={0: 0},
        compiler_params=pltpu.CompilerParams(vmem_limit_bytes=MIB),
        name="after",
    )(block, *tokens)


def shifts_of(naux):
    plan = []
    for shift in range(1, naux // 2 + 1):
        if 2 * shift < naux:
            plan.append([(source, (source + shift) % naux) for source in range(naux)])
        else:
            plan.append([(z, z + shift) if z % 2 == 0 else (z + shift, z) for z in range(shift)])
    return plan


def select(block, list_rows, slots, width):
    parts = []
    for slot in range(slots):
        entry = list_rows[:1, slot : slot + 1]
        chosen = jnp.zeros((block.shape[0], width), F32)
        for j in range(block.shape[1] // width):
            chosen = jnp.where(entry == float(j), block[:, j * width : (j + 1) * width], chosen)
        parts.append(chosen)
    return jnp.concatenate(parts, axis=1)


def mix(place, near, far, tensor, rows, slots, width, share):
    nt = near.shape[0]
    pairs = tensor.shape[1] // (2 * width)
    near_list, far_list = near[0, 2 * width :, :], far[0, 2 * width :, :]
    which = [lax.rem(tau + nt - place[1], nt) for tau in range(nt)]
    left = []
    for kind in range(2):
        for tau in range(nt):
            start = pl.multiple_of(kind * width + place[1] * share, share)
            left.append(select(near[which[tau], pl.ds(start, share), :], far_list, slots, width))
    left_high, left_low = halves(jnp.concatenate(left, axis=0))
    high, low = halves(tensor[...])
    middle = dot(
        jnp.concatenate([left_high, left_high, left_low], axis=1), jnp.concatenate([high, low, high], axis=0)
    )
    for group in range(2 * nt):
        for at in range(pairs):
            rows[(group * pairs + at) * share : (group * pairs + at + 1) * share, :] = middle[
                group * share : (group + 1) * share, 2 * width * at : 2 * width * (at + 1)
            ]
    results = []
    for group in range(2 * nt):
        kind, tau = group // nt, group % nt
        right = select(far[which[tau], (1 - kind) * width : (2 - kind) * width, :], near_list, slots, width)
        zero = jnp.zeros_like(right)
        right_high, right_low = halves(
            jnp.concatenate([jnp.concatenate([right, zero], axis=1), jnp.concatenate([zero, right], axis=1)], axis=0)
        )

        rows_high, rows_low = halves(
            jnp.concatenate(
                [rows[pl.ds(group * pairs * share + at, pairs, stride=share), :] for at in range(share)], axis=0
            )
        )
        results.append(
            dot(
                jnp.concatenate([rows_high, rows_high, rows_low], axis=1),
                jnp.concatenate([right_high, right_low, right_high], axis=0),
            )
        )
    return results


def first(place, near, tensor, acc, token, rows, *, slots, width, share):
    token[...] = jnp.zeros_like(token)
    for group, result in enumerate(mix(place, near, near, tensor, rows, slots, width, share)):
        acc[group] = result


def second(place, near, acc, *refs, slots, width, share):
    refs, (sides, token, rows) = refs[:-3], refs[-3:]
    tensors, fars = refs[: len(refs) // 2], refs[len(refs) // 2 :]
    token[...] = jnp.zeros_like(token)
    listed = slots * width
    groups, tall, _ = acc.shape
    pairs = tall // share
    total = [acc[group] for group in range(groups)]
    for tensor, far in zip(tensors, fars):
        term = mix(place, near, far, tensor, rows, slots, width, share)
        total = [x + y for x, y in zip(total, term)]
    for group in range(groups):
        high, low = halves(total[group])
        for odd in range(2):
            row = (2 * group + odd) * pairs
            for at in range(share):
                for part, array in enumerate((high, low)):
                    sides[
                        part * 2 * groups * pairs + row : part * 2 * groups * pairs + row + pairs,
                        at * listed : (at + 1) * listed,
                    ] = array[at * pairs : (at + 1) * pairs, odd * listed : (odd + 1) * listed]


def meet(place, sides, own, other, *refs, share, nt):
    outs, (tensor, ordered) = refs[:-2], refs[-2:]
    listed = own.shape[1]
    rows_aux = own.shape[0] // share
    block = 2 * rows_aux
    for which, source in enumerate((own, other)):
        start = pl.multiple_of(jnp.where(place[2] == which, 0, rows_aux), rows_aux)
        for at in range(share):
            high, low = halves(source[at * rows_aux : (at + 1) * rows_aux, :])
            tensor[pl.ds(start, rows_aux), at * listed : (at + 1) * listed] = high
            tensor[pl.ds(block + start, rows_aux), at * listed : (at + 1) * listed] = low
    product = dot_nt(tensor[...], sides[...])
    product = product[:block] + product[block:]
    product = (product[:, : 2 * nt * rows_aux] + product[:, 2 * nt * rows_aux :]).T
    pairs = rows_aux // 2
    for group in range(2 * nt):
        for odd in range(2):
            at = (2 * group + odd) * pairs
            ordered[pl.ds(group * rows_aux + odd, pairs, stride=2), :] = product[at : at + pairs]
    outs[0][...] = ordered[: nt * rows_aux, :]
    if len(outs) == 2:
        back = ordered[nt * rows_aux :, :].T
        parts = []
        for tau in range(nt):
            part = back[:, tau * rows_aux : (tau + 1) * rows_aux]
            zero = jnp.zeros_like(part)
            parts.append(
                jnp.where(
                    place[2] == 0, jnp.concatenate([part, zero], axis=1), jnp.concatenate([zero, part], axis=1)
                )
            )
        outs[1][...] = jnp.concatenate(parts, axis=1)


def assemble(place, *refs, naux, nt):
    refs, out_ref = refs[:-1], refs[-1]
    count = naux // 2
    directs, backs = refs[:count], refs[count:]
    block = directs[0].shape[1]
    half = directs[0].shape[0] // nt
    start = pl.multiple_of(place[2] * half, half)
    for tau in range(nt):
        here = [jnp.zeros((half, block), F32)] * naux
        for shift, ref in enumerate(directs):
            here[(naux - shift) % naux] = ref[tau * half : (tau + 1) * half, :]
        there = [jnp.zeros((block, block), F32)] * naux
        for shift, ref in enumerate(backs, 1):
            there[shift] = ref[:, tau * block : (tau + 1) * block]
        out_ref[tau] = jnp.concatenate(there, axis=1)
        out_ref[tau, pl.ds(start, half), :] += jnp.concatenate(here, axis=1)


def complete(place, early, direct, back, out_ref):
    nt, block, wide = early.shape
    half = direct.shape[0] // nt
    naux = wide // block
    last = naux // 2
    for tau in range(nt):
        here = direct[tau * half : (tau + 1) * half, :]
        zero = jnp.zeros_like(here)
        here = jnp.where(
            place[2] == 0, jnp.concatenate([here, zero], axis=0), jnp.concatenate([zero, here], axis=0)
        )
        parts = [jnp.zeros((block, block), F32)] * naux
        parts[last] = back[:, tau * block : (tau + 1) * block]
        parts[(naux - last) % naux] = parts[(naux - last) % naux] + here
        total = early[tau] + jnp.concatenate(parts, axis=1)
        out_ref[tau] = pltpu.roll(total, place[3] * block, 1)


def local(three_center, occupied_green, virtual_green, block_list, sizes):
    nt, naux, nob, nsub = sizes
    slots = three_center.shape[2]
    width = three_center.shape[3]
    columns = three_center.shape[4]
    rows_aux = columns // width
    block_aux = rows_aux * nsub
    norb = occupied_green.shape[1]
    listed = slots * width
    share = width // nt
    nauxf = naux * block_aux
    me_orb, me_tau, me_sub, me_aux = (lax.axis_index(axis) for axis in ("orb", "tau", "sub", "aux"))
    place = jnp.stack([me_orb, me_tau, me_sub, me_aux]).astype(jnp.int32)
    tensor = three_center.reshape(listed, columns)
    limit = 24 + 3 * max(nob - 2, 0)

    def call(kernel, outs, scratch, flops, *arguments, **options):
        shapes = [jax.ShapeDtypeStruct(shape, kind) for shape, kind in outs]
        size = sum(4 * math.prod(x.shape) for x in arguments)
        return pl.pallas_call(
            functools.partial(kernel, **options),
            out_shape=shapes,
            in_specs=[SMEM] + [VMEM] * len(arguments),
            out_specs=[VMEM] * len(shapes),
            scratch_shapes=[pltpu.VMEM(shape, kind) for shape, kind in scratch],
            compiler_params=pltpu.CompilerParams(vmem_limit_bytes=limit * MIB),
            cost_estimate=pl.CostEstimate(flops=flops, bytes_accessed=size, transcendentals=0),
            name=kernel.__name__,
        )(place, *arguments)

    tensors = [lax.ppermute(tensor, "orb", ring(nob, shift)) for shift in range(1, nob)]
    (mine,) = call(
        prepare, [((share, rows_aux, listed), F32)], [((columns, listed), F32)], 0, tensor, share=share
    )
    plan = shifts_of(naux)
    pieces = [lax.ppermute(mine, "aux", pairs) for pairs in plan]
    swap = ring(nsub, 1)
    mine_other = lax.ppermute(mine, "sub", swap)
    small = jnp.concatenate(
        [
            occupied_green,
            virtual_green,
            jnp.pad(block_list.astype(F32), ((0, LIST_ROWS - 1), (0, norb - slots))),
        ]
    )
    near = jnp.stack([small] + [lax.ppermute(small, "tau", ring(nt, shift)) for shift in range(1, nt)])
    fars = []
    for shift in range(1, nob):
        pairs = [(a * nsub + c, b * nsub + (c + 1) % nsub) for a, b in ring(nob, shift) for c in range(nsub)]
        fars.append(lax.ppermute(near, ("orb", "sub"), pairs))

    groups = 2 * nt
    work = 6 * groups * share * columns * listed * 3
    rows = groups * rows_aux
    depth = share * listed
    options = dict(slots=slots, width=width, share=share)
    acc, token = call(
        first,
        [((groups, rows_aux // 2 * share, 2 * listed), F32), ((8, 128), F32)],
        [((groups * rows_aux // 2 * share, 2 * width), F32)],
        work,
        near,
        tensor,
        **options,
    )
    sides, token_late = call(
        second,
        [((2 * rows, depth), BF16), ((8, 128), F32)],
        [((groups * rows_aux // 2 * share, 2 * width), F32)],
        work * (nob - 1),
        near,
        acc,
        *tensors,
        *fars,
        **options,
    )
    tokens = [(token, mine_other) + tuple(fars[-1:])] + [(token_late,)] * (len(plan) - 1)
    pieces = [after(block, *token) for block, token in zip(pieces, tokens)]
    others = [lax.ppermute(block, "sub", swap) for block in pieces]
    flat = lambda block: block.reshape(-1, listed)
    turned = [((2 * block_aux, depth), BF16), ((rows, block_aux), F32)]
    shape_direct = ((nt * rows_aux, block_aux), F32)
    shape_back = ((block_aux, nt * block_aux), F32)
    work = 16 * rows * block_aux * depth
    options = dict(share=share, nt=nt)
    (direct,) = call(meet, [shape_direct], turned, work, sides, flat(mine), flat(mine_other), **options)
    directs, returned = [direct], []
    for own, other in zip(pieces, others):
        direct, back = call(meet, [shape_direct, shape_back], turned, work, sides, flat(own), flat(other), **options)
        directs.append(direct)
        returned.append(lax.ppermute(back, "aux", ring(naux, len(directs) - 1)))
    shape = ((nt, block_aux, nauxf), F32)
    (early,) = call(assemble, [shape], [], 0, *directs[:-1], *returned[:-1], naux=naux, nt=nt)
    (partial_chi,) = call(complete, [shape], [], 0, early, directs[-1], returned[-1])
    owners = nt * nob * nsub
    received = lax.all_to_all(
        partial_chi.reshape(owners, nt * block_aux // owners, nauxf),
        ("tau", "orb", "sub"),
        split_axis=0,
        concat_axis=0,
        tiled=True,
    )
    return received.sum(axis=0) * (-2.0 / math.sqrt(norb * slots * width))


def solution(mesh):
    sizes = tuple(mesh.shape[axis] for axis in ("tau", "aux", "orb", "sub"))
    in_specs = (
        P("aux", "orb", None, None, "sub"),
        P(("tau", "orb"), None),
        P(("tau", "orb"), None),
        P("orb", None),
    )
    out_specs = P(("tau", "aux", "orb", "sub"), None)
    return jax.shard_map(
        functools.partial(local, sizes=sizes), mesh=mesh, in_specs=in_specs, out_specs=out_specs, check_vma=False
    )
```

```python
import functools
import math

import jax
import jax.numpy as jnp
from jax import lax
from jax.experimental import pallas as pl
from jax.experimental.pallas import tpu as pltpu
from jax.sharding import PartitionSpec as P

VMEM = pl.BlockSpec(memory_space=pltpu.VMEM)
ANY = pl.BlockSpec(memory_space=pl.ANY)
HBM = pl.BlockSpec(memory_space=pltpu.HBM)
SMEM = pl.BlockSpec(memory_space=pltpu.SMEM)
F32 = jnp.float32
BF16 = jnp.bfloat16
LIST_ROWS = 8
MIB = 1024 * 1024


def halves(x):
    high = x.astype(BF16)
    return high, (x - high.astype(F32)).astype(BF16)


def dot(a, b):
    return lax.dot_general(a, b, (((1,), (0,)), ((), ())), preferred_element_type=F32)


def dot_nt(a, b):
    return lax.dot_general(a, b, (((1,), (1,)), ((), ())), preferred_element_type=F32)


def ring(count, shift):
    return [((target + shift) % count, target) for target in range(count)]


def prepare(place, tensor, mine, turned, *, share):
    some = mine.shape[1]
    turned[...] = tensor[...].T
    start = place[1] * share
    for at in range(share):
        mine[at] = turned[pl.ds(start + at, some, stride=turned.shape[0] // some), :]


def after(block, *tokens):
    return pl.pallas_call(
        lambda *refs: None,
        out_shape=jax.ShapeDtypeStruct(block.shape, block.dtype),
        in_specs=[ANY] * (1 + len(tokens)),
        out_specs=ANY,
        input_output_aliases={0: 0},
        compiler_params=pltpu.CompilerParams(vmem_limit_bytes=MIB),
        name="after",
    )(block, *tokens)


def shifts_of(naux):
    plan = []
    for shift in range(1, naux // 2 + 1):
        if 2 * shift < naux:
            plan.append([(source, (source + shift) % naux) for source in range(naux)])
        else:
            plan.append([(z, z + shift) if z % 2 == 0 else (z + shift, z) for z in range(shift)])
    return plan


def select(block, list_rows, slots, width):
    parts = []
    for slot in range(slots):
        entry = list_rows[:1, slot : slot + 1]
        chosen = jnp.zeros((block.shape[0], width), F32)
        for j in range(block.shape[1] // width):
            chosen = jnp.where(entry == float(j), block[:, j * width : (j + 1) * width], chosen)
        parts.append(chosen)
    return jnp.concatenate(parts, axis=1)


def mix(place, near, far, tensor, rows, slots, width, share):
    nt = near.shape[0]
    pairs = tensor.shape[1] // (2 * width)
    near_list, far_list = near[0, 2 * width :, :], far[0, 2 * width :, :]
    which = [lax.rem(tau + nt - place[1], nt) for tau in range(nt)]
    left = []
    for kind in range(2):
        for tau in range(nt):
            start = pl.multiple_of(kind * width + place[1] * share, share)
            left.append(select(near[which[tau], pl.ds(start, share), :], far_list, slots, width))
    left_high, left_low = halves(jnp.concatenate(left, axis=0))
    high, low = halves(tensor[...])
    middle = dot(
        jnp.concatenate([left_high, left_high, left_low], axis=1), jnp.concatenate([high, low, high], axis=0)
    )
    for group in range(2 * nt):
        for at in range(pairs):
            rows[(group * pairs + at) * share : (group * pairs + at + 1) * share, :] = middle[
                group * share : (group + 1) * share, 2 * width * at : 2 * width * (at + 1)
            ]
    results = []
    for group in range(2 * nt):
        kind, tau = group // nt, group % nt
        right = select(far[which[tau], (1 - kind) * width : (2 - kind) * width, :], near_list, slots, width)
        zero = jnp.zeros_like(right)
        right_high, right_low = halves(
            jnp.concatenate([jnp.concatenate([right, zero], axis=1), jnp.concatenate([zero, right], axis=1)], axis=0)
        )

        rows_high, rows_low = halves(
            jnp.concatenate(
                [rows[pl.ds(group * pairs * share + at, pairs, stride=share), :] for at in range(share)], axis=0
            )
        )
        results.append(
            dot(
                jnp.concatenate([rows_high, rows_high, rows_low], axis=1),
                jnp.concatenate([right_high, right_low, right_high], axis=0),
            )
        )
    return results


def first(place, near, tensor, acc, token, rows, *, slots, width, share):
    token[...] = jnp.zeros_like(token)
    for group, result in enumerate(mix(place, near, near, tensor, rows, slots, width, share)):
        acc[group] = result


def second(place, near, acc, *refs, slots, width, share):
    refs, (sides, token, rows) = refs[:-3], refs[-3:]
    tensors, fars = refs[: len(refs) // 2], refs[len(refs) // 2 :]
    token[...] = jnp.zeros_like(token)
    listed = slots * width
    groups, tall, _ = acc.shape
    pairs = tall // share
    total = [acc[group] for group in range(groups)]
    for tensor, far in zip(tensors, fars):
        term = mix(place, near, far, tensor, rows, slots, width, share)
        total = [x + y for x, y in zip(total, term)]
    for group in range(groups):
        high, low = halves(total[group])
        for odd in range(2):
            row = (2 * group + odd) * pairs
            for at in range(share):
                for part, array in enumerate((high, low)):
                    sides[
                        part * 2 * groups * pairs + row : part * 2 * groups * pairs + row + pairs,
                        at * listed : (at + 1) * listed,
                    ] = array[at * pairs : (at + 1) * pairs, odd * listed : (odd + 1) * listed]


def meet(place, sides, *refs, share, nt):
    refs, (tensor, ordered) = refs[:-2], refs[-2:]
    count = (len(refs) + 1) // 4
    pieces, directs, backs = refs[: 2 * count], refs[2 * count : 3 * count], refs[3 * count :]
    listed = pieces[0].shape[1]
    rows_aux = pieces[0].shape[0] // share
    block = 2 * rows_aux
    for i in range(count):
        for which, source in enumerate(pieces[2 * i : 2 * i + 2]):
            start = pl.multiple_of(jnp.where(place[2] == which, 0, rows_aux), rows_aux)
            for at in range(share):
                high, low = halves(source[at * rows_aux : (at + 1) * rows_aux, :])
                tensor[pl.ds(2 * i * block + start, rows_aux), at * listed : (at + 1) * listed] = high
                tensor[pl.ds((2 * i + 1) * block + start, rows_aux), at * listed : (at + 1) * listed] = low
    products = dot_nt(tensor[...], sides[...])
    pairs = rows_aux // 2
    for i in range(count):
        product = products[2 * i * block : (2 * i + 1) * block] + products[(2 * i + 1) * block : 2 * (i + 1) * block]
        product = (product[:, : 2 * nt * rows_aux] + product[:, 2 * nt * rows_aux :]).T
        for group in range(2 * nt):
            for odd in range(2):
                at = (2 * group + odd) * pairs
                ordered[i, pl.ds(group * rows_aux + odd, pairs, stride=2), :] = product[at : at + pairs]
        directs[i][...] = ordered[i, : nt * rows_aux, :]
        if i == 0:
            continue
        back = ordered[i, nt * rows_aux :, :].T
        parts = []
        for tau in range(nt):
            part = back[:, tau * rows_aux : (tau + 1) * rows_aux]
            zero = jnp.zeros_like(part)
            parts.append(
                jnp.where(
                    place[2] == 0, jnp.concatenate([part, zero], axis=1), jnp.concatenate([zero, part], axis=1)
                )
            )
        backs[i - 1][...] = jnp.concatenate(parts, axis=1)


def assemble(place, *refs, naux, nt):
    directs, out_ref = refs[:-1], refs[-1]
    block = directs[0].shape[1]
    half = directs[0].shape[0] // nt
    for tau in range(nt):
        here = [jnp.zeros((half, block), F32)] * naux
        for shift, ref in enumerate(directs):
            here[(naux - shift) % naux] = ref[tau * half : (tau + 1) * half, :]
        here = jnp.concatenate(here, axis=1)
        zero = jnp.zeros_like(here)
        out_ref[tau] = jnp.where(
            place[2] == 0, jnp.concatenate([here, zero], axis=0), jnp.concatenate([zero, here], axis=0)
        )


def complete(place, early, *refs):
    backs, out_ref = refs[:-1], refs[-1]
    nt, block, wide = early.shape
    naux = wide // block
    for tau in range(nt):
        parts = [jnp.zeros((block, block), F32)] * naux
        for shift, ref in enumerate(backs, 1):
            parts[shift] = ref[:, tau * block : (tau + 1) * block]
        total = early[tau] + jnp.concatenate(parts, axis=1)
        out_ref[tau] = pltpu.roll(total, place[3] * block, 1)


def local(three_center, occupied_green, virtual_green, block_list, sizes):
    nt, naux, nob, nsub = sizes
    slots = three_center.shape[2]
    width = three_center.shape[3]
    columns = three_center.shape[4]
    rows_aux = columns // width
    block_aux = rows_aux * nsub
    norb = occupied_green.shape[1]
    listed = slots * width
    share = width // nt
    nauxf = naux * block_aux
    me_orb, me_tau, me_sub, me_aux = (lax.axis_index(axis) for axis in ("orb", "tau", "sub", "aux"))
    place = jnp.stack([me_orb, me_tau, me_sub, me_aux]).astype(jnp.int32)
    tensor = three_center.reshape(listed, columns)
    limit = 24 + 3 * max(nob - 2, 0)

    def call(kernel, outs, scratch, flops, *arguments, **options):
        shapes = [jax.ShapeDtypeStruct(shape, kind) for shape, kind in outs]
        size = sum(4 * math.prod(x.shape) for x in arguments)
        return pl.pallas_call(
            functools.partial(kernel, **options),
            out_shape=shapes,
            in_specs=[SMEM] + [VMEM] * len(arguments),
            out_specs=[VMEM] * len(shapes),
            scratch_shapes=[pltpu.VMEM(shape, kind) for shape, kind in scratch],
            compiler_params=pltpu.CompilerParams(vmem_limit_bytes=limit * MIB),
            cost_estimate=pl.CostEstimate(flops=flops, bytes_accessed=size, transcendentals=0),
            name=kernel.__name__,
        )(place, *arguments)

    tensors = [lax.ppermute(tensor, "orb", ring(nob, shift)) for shift in range(1, nob)]
    (mine,) = call(
        prepare, [((share, rows_aux, listed), F32)], [((columns, listed), F32)], 0, tensor, share=share
    )
    plan = shifts_of(naux)
    pieces = [lax.ppermute(mine, "aux", pairs) for pairs in plan]
    swap = ring(nsub, 1)
    mine_other = lax.ppermute(mine, "sub", swap)
    small = jnp.concatenate(
        [
            occupied_green,
            virtual_green,
            jnp.pad(block_list.astype(F32), ((0, LIST_ROWS - 1), (0, norb - slots))),
        ]
    )
    near = jnp.stack([small] + [lax.ppermute(small, "tau", ring(nt, shift)) for shift in range(1, nt)])
    fars = []
    for shift in range(1, nob):
        pairs = [(a * nsub + c, b * nsub + (c + 1) % nsub) for a, b in ring(nob, shift) for c in range(nsub)]
        fars.append(lax.ppermute(near, ("orb", "sub"), pairs))

    groups = 2 * nt
    work = 6 * groups * share * columns * listed * 3
    rows = groups * rows_aux
    depth = share * listed
    options = dict(slots=slots, width=width, share=share)
    acc, token = call(
        first,
        [((groups, rows_aux // 2 * share, 2 * listed), F32), ((8, 128), F32)],
        [((groups * rows_aux // 2 * share, 2 * width), F32)],
        work,
        near,
        tensor,
        **options,
    )
    sides, token_late = call(
        second,
        [((2 * rows, depth), BF16), ((8, 128), F32)],
        [((groups * rows_aux // 2 * share, 2 * width), F32)],
        work * (nob - 1),
        near,
        acc,
        *tensors,
        *fars,
        **options,
    )
    pieces = [after(block, token_late, mine_other) for block in pieces]
    others = [lax.ppermute(block, "sub", swap) for block in pieces]
    flat = lambda block: block.reshape(-1, listed)
    count = 1 + len(plan)
    work = 16 * rows * block_aux * depth * count
    blocks = [flat(x) for pair in zip([mine] + pieces, [mine_other] + others) for x in pair]
    results = call(
        meet,
        [((nt * rows_aux, block_aux), F32)] * count + [((block_aux, nt * block_aux), F32)] * (count - 1),
        [((2 * count * block_aux, depth), BF16), ((count, rows, block_aux), F32)],
        work,
        sides,
        *blocks,
        share=share,
        nt=nt,
    )
    returned = [lax.ppermute(back, "aux", ring(naux, i)) for i, back in enumerate(results[count:], 1)]
    shape = ((nt, block_aux, nauxf), F32)
    (early,) = call(assemble, [shape], [], 0, *results[:count], naux=naux, nt=nt)
    (partial_chi,) = call(complete, [shape], [], 0, early, *returned)
    owners = nt * nob * nsub
    received = lax.all_to_all(
        partial_chi.reshape(owners, nt * block_aux // owners, nauxf),
        ("tau", "orb", "sub"),
        split_axis=0,
        concat_axis=0,
        tiled=True,
    )
    return received.sum(axis=0) * (-2.0 / math.sqrt(norb * slots * width))


def solution(mesh):
    sizes = tuple(mesh.shape[axis] for axis in ("tau", "aux", "orb", "sub"))
    in_specs = (
        P("aux", "orb", None, None, "sub"),
        P(("tau", "orb"), None),
        P(("tau", "orb"), None),
        P("orb", None),
    )
    out_specs = P(("tau", "aux", "orb", "sub"), None)
    return jax.shard_map(
        functools.partial(local, sizes=sizes), mesh=mesh, in_specs=in_specs, out_specs=out_specs, check_vma=False
    )
```

```python
import functools
import math

import jax
import jax.numpy as jnp
from jax import lax
from jax.experimental import pallas as pl
from jax.experimental.pallas import tpu as pltpu
from jax.sharding import PartitionSpec as P

VMEM = pl.BlockSpec(memory_space=pltpu.VMEM)
ANY = pl.BlockSpec(memory_space=pl.ANY)
HBM = pl.BlockSpec(memory_space=pltpu.HBM)
SMEM = pl.BlockSpec(memory_space=pltpu.SMEM)
F32 = jnp.float32
BF16 = jnp.bfloat16
LIST_ROWS = 8
MIB = 1024 * 1024


def halves(x):
    high = x.astype(BF16)
    return high, (x - high.astype(F32)).astype(BF16)


def dot(a, b):
    return lax.dot_general(a, b, (((1,), (0,)), ((), ())), preferred_element_type=F32)


def dot_nt(a, b):
    return lax.dot_general(a, b, (((1,), (1,)), ((), ())), preferred_element_type=F32)


def ring(count, shift):
    return [((target + shift) % count, target) for target in range(count)]


def prepare(place, tensor, mine, turned, *, share):
    some = mine.shape[1]
    turned[...] = tensor[...].T
    start = place[1] * share
    for at in range(share):
        mine[at] = turned[pl.ds(start + at, some, stride=turned.shape[0] // some), :]


def after(block, *tokens):
    return pl.pallas_call(
        lambda *refs: None,
        out_shape=jax.ShapeDtypeStruct(block.shape, block.dtype),
        in_specs=[ANY] * (1 + len(tokens)),
        out_specs=ANY,
        input_output_aliases={0: 0},
        compiler_params=pltpu.CompilerParams(vmem_limit_bytes=MIB),
        name="after",
    )(block, *tokens)


def shifts_of(naux):
    plan = []
    for shift in range(1, naux // 2 + 1):
        if 2 * shift < naux:
            plan.append([(source, (source + shift) % naux) for source in range(naux)])
        else:
            plan.append([(z, z + shift) if z % 2 == 0 else (z + shift, z) for z in range(shift)])
    return plan


def select(block, list_rows, slots, width):
    parts = []
    for slot in range(slots):
        entry = list_rows[:1, slot : slot + 1]
        chosen = jnp.zeros((block.shape[0], width), F32)
        for j in range(block.shape[1] // width):
            chosen = jnp.where(entry == float(j), block[:, j * width : (j + 1) * width], chosen)
        parts.append(chosen)
    return jnp.concatenate(parts, axis=1)


def mix(place, near, far, tensor, rows, slots, width, share):
    nt = near.shape[0]
    pairs = tensor.shape[1] // (2 * width)
    near_list, far_list = near[0, 2 * width :, :], far[0, 2 * width :, :]
    which = [lax.rem(tau + nt - place[1], nt) for tau in range(nt)]
    left = []
    for kind in range(2):
        for tau in range(nt):
            start = pl.multiple_of(kind * width + place[1] * share, share)
            left.append(select(near[which[tau], pl.ds(start, share), :], far_list, slots, width))
    left_high, left_low = halves(jnp.concatenate(left, axis=0))
    high, low = halves(tensor[...])
    middle = dot(
        jnp.concatenate([left_high, left_high, left_low], axis=1), jnp.concatenate([high, low, high], axis=0)
    )
    for group in range(2 * nt):
        for at in range(pairs):
            rows[(group * pairs + at) * share : (group * pairs + at + 1) * share, :] = middle[
                group * share : (group + 1) * share, 2 * width * at : 2 * width * (at + 1)
            ]
    results = []
    for group in range(2 * nt):
        kind, tau = group // nt, group % nt
        right = select(far[which[tau], (1 - kind) * width : (2 - kind) * width, :], near_list, slots, width)
        zero = jnp.zeros_like(right)
        right_high, right_low = halves(
            jnp.concatenate([jnp.concatenate([right, zero], axis=1), jnp.concatenate([zero, right], axis=1)], axis=0)
        )

        rows_high, rows_low = halves(
            jnp.concatenate(
                [rows[pl.ds(group * pairs * share + at, pairs, stride=share), :] for at in range(share)], axis=0
            )
        )
        results.append(
            dot(
                jnp.concatenate([rows_high, rows_high, rows_low], axis=1),
                jnp.concatenate([right_high, right_low, right_high], axis=0),
            )
        )
    return results


def first(place, near, tensor, acc, token, rows, *, slots, width, share):
    token[...] = jnp.zeros_like(token)
    for group, result in enumerate(mix(place, near, near, tensor, rows, slots, width, share)):
        acc[group] = result


def second(place, near, acc, *refs, slots, width, share):
    refs, (sides, token, rows) = refs[:-3], refs[-3:]
    tensors, fars = refs[: len(refs) // 2], refs[len(refs) // 2 :]
    token[...] = jnp.zeros_like(token)
    listed = slots * width
    groups, tall, _ = acc.shape
    pairs = tall // share
    total = [acc[group] for group in range(groups)]
    for tensor, far in zip(tensors, fars):
        term = mix(place, near, far, tensor, rows, slots, width, share)
        total = [x + y for x, y in zip(total, term)]
    for group in range(groups):
        high, low = halves(total[group])
        for odd in range(2):
            row = (2 * group + odd) * pairs
            for at in range(share):
                for part, array in enumerate((high, low)):
                    sides[
                        part * 2 * groups * pairs + row : part * 2 * groups * pairs + row + pairs,
                        at * listed : (at + 1) * listed,
                    ] = array[at * pairs : (at + 1) * pairs, odd * listed : (odd + 1) * listed]


def meet(place, sides, *refs, share, nt, naux):
    pieces, (out_ref, tensor, ordered) = refs[:-3], refs[-3:]
    count = len(pieces) // 2
    listed = pieces[0].shape[1]
    half = pieces[0].shape[0] // share
    block = 2 * half
    for i in range(count):
        for which, source in enumerate(pieces[2 * i : 2 * i + 2]):
            start = pl.multiple_of(jnp.where(place[2] == which, 0, half), half)
            for at in range(share):
                high, low = halves(source[at * half : (at + 1) * half, :])
                tensor[pl.ds(2 * i * block + start, half), at * listed : (at + 1) * listed] = high
                tensor[pl.ds((2 * i + 1) * block + start, half), at * listed : (at + 1) * listed] = low
    products = dot_nt(tensor[...], sides[...])
    pairs = half // 2
    for i in range(count):
        product = products[2 * i * block : (2 * i + 1) * block] + products[(2 * i + 1) * block : 2 * (i + 1) * block]
        product = (product[:, : 2 * nt * half] + product[:, 2 * nt * half :]).T
        for group in range(2 * nt):
            for odd in range(2):
                at = (2 * group + odd) * pairs
                ordered[i, pl.ds(group * half + odd, pairs, stride=2), :] = product[at : at + pairs]

    def at_sub(x, axis):
        zero = jnp.zeros_like(x)
        return jnp.where(
            place[2] == 0, jnp.concatenate([x, zero], axis=axis), jnp.concatenate([zero, x], axis=axis)
        )

    wide = naux * block
    for tau in range(nt):
        here = [jnp.zeros((half, block), F32)] * naux
        for shift in range(count):
            here[(naux - shift) % naux] = ordered[shift, tau * half : (tau + 1) * half, :]
        here = pltpu.roll(jnp.concatenate(here, axis=1), place[3] * block, 1)
        out_ref[tau, :, :wide] = at_sub(here, 0)
        rest = [
            at_sub(ordered[shift, (nt + tau) * half : (nt + tau + 1) * half, :].T, 1) for shift in range(1, count)
        ]
        padding = out_ref.shape[2] - wide - block * len(rest)
        if padding:
            rest.append(jnp.zeros((block, padding), F32))
        out_ref[tau, :, wide:] = jnp.concatenate(rest, axis=1)


def add(place, received, *outs, block):
    total = received[0]
    for i in range(1, received.shape[0]):
        total = total + received[i]
    rows, wide = outs[0].shape
    outs[0][...] = total[:, :wide]
    for shift, out in enumerate(outs[1:]):
        back = total[:, wide + shift * block : wide + (shift + 1) * block]
        back = jnp.concatenate([back, jnp.zeros((rows, wide - block), F32)], axis=1)
        out[...] = pltpu.roll(back, place[3] * block, 1)


def local(three_center, occupied_green, virtual_green, block_list, sizes):
    nt, naux, nob, nsub = sizes
    slots = three_center.shape[2]
    width = three_center.shape[3]
    columns = three_center.shape[4]
    rows_aux = columns // width
    block_aux = rows_aux * nsub
    norb = occupied_green.shape[1]
    listed = slots * width
    share = width // nt
    nauxf = naux * block_aux
    me_orb, me_tau, me_sub, me_aux = (lax.axis_index(axis) for axis in ("orb", "tau", "sub", "aux"))
    place = jnp.stack([me_orb, me_tau, me_sub, me_aux]).astype(jnp.int32)
    tensor = three_center.reshape(listed, columns)
    limit = 24 + 3 * max(nob - 2, 0)

    def call(kernel, outs, scratch, flops, *arguments, **options):
        shapes = [jax.ShapeDtypeStruct(shape, kind) for shape, kind in outs]
        size = sum(4 * math.prod(x.shape) for x in arguments)
        return pl.pallas_call(
            functools.partial(kernel, **options),
            out_shape=shapes,
            in_specs=[SMEM] + [VMEM] * len(arguments),
            out_specs=[VMEM] * len(shapes),
            scratch_shapes=[pltpu.VMEM(shape, kind) for shape, kind in scratch],
            compiler_params=pltpu.CompilerParams(vmem_limit_bytes=limit * MIB),
            cost_estimate=pl.CostEstimate(flops=flops, bytes_accessed=size, transcendentals=0),
            name=kernel.__name__,
        )(place, *arguments)

    tensors = [lax.ppermute(tensor, "orb", ring(nob, shift)) for shift in range(1, nob)]
    (mine,) = call(
        prepare, [((share, rows_aux, listed), F32)], [((columns, listed), F32)], 0, tensor, share=share
    )
    plan = shifts_of(naux)
    pieces = [lax.ppermute(mine, "aux", pairs) for pairs in plan]
    swap = ring(nsub, 1)
    mine_other = lax.ppermute(mine, "sub", swap)
    small = jnp.concatenate(
        [
            occupied_green,
            virtual_green,
            jnp.pad(block_list.astype(F32), ((0, LIST_ROWS - 1), (0, norb - slots))),
        ]
    )
    near = jnp.stack([small] + [lax.ppermute(small, "tau", ring(nt, shift)) for shift in range(1, nt)])
    fars = []
    for shift in range(1, nob):
        pairs = [(a * nsub + c, b * nsub + (c + 1) % nsub) for a, b in ring(nob, shift) for c in range(nsub)]
        fars.append(lax.ppermute(near, ("orb", "sub"), pairs))

    groups = 2 * nt
    work = 6 * groups * share * columns * listed * 3
    rows = groups * rows_aux
    depth = share * listed
    options = dict(slots=slots, width=width, share=share)
    acc, token = call(
        first,
        [((groups, rows_aux // 2 * share, 2 * listed), F32), ((8, 128), F32)],
        [((groups * rows_aux // 2 * share, 2 * width), F32)],
        work,
        near,
        tensor,
        **options,
    )
    sides, token_late = call(
        second,
        [((2 * rows, depth), BF16), ((8, 128), F32)],
        [((groups * rows_aux // 2 * share, 2 * width), F32)],
        work * (nob - 1),
        near,
        acc,
        *tensors,
        *fars,
        **options,
    )
    held = []
    for block in pieces:
        held.append(after(block, token_late, mine_other, *held[-1:]))
    pieces = held
    others = [lax.ppermute(block, "sub", swap) for block in pieces]
    flat = lambda block: block.reshape(-1, listed)
    count = 1 + len(plan)
    work = 16 * rows * block_aux * depth * count
    blocks = [flat(x) for pair in zip([mine] + pieces, [mine_other] + others) for x in pair]
    wide = nauxf + -(-len(plan) * block_aux // 128) * 128
    (partial_chi,) = call(
        meet,
        [((nt, block_aux, wide), F32)],
        [((2 * count * block_aux, depth), BF16), ((count, rows, block_aux), F32)],
        work,
        sides,
        *blocks,
        share=share,
        nt=nt,
        naux=naux,
    )
    owners = nt * nob * nsub
    own_rows = nt * block_aux // owners
    received = lax.all_to_all(
        partial_chi.reshape(owners, own_rows, wide),
        ("tau", "orb", "sub"),
        split_axis=0,
        concat_axis=0,
        tiled=True,
    )
    chi, *backs = call(add, [((own_rows, nauxf), F32)] * count, [], 0, received, block=block_aux)
    for shift, back in enumerate(backs, 1):
        chi = chi + lax.ppermute(back, "aux", ring(naux, shift))
    return chi * (-2.0 / math.sqrt(norb * slots * width))


def solution(mesh):
    sizes = tuple(mesh.shape[axis] for axis in ("tau", "aux", "orb", "sub"))
    in_specs = (
        P("aux", "orb", None, None, "sub"),
        P(("tau", "orb"), None),
        P(("tau", "orb"), None),
        P("orb", None),
    )
    out_specs = P(("tau", "aux", "orb", "sub"), None)
    return jax.shard_map(
        functools.partial(local, sizes=sizes), mesh=mesh, in_specs=in_specs, out_specs=out_specs, check_vma=False
    )
```

```python
import functools
import math

import jax
import jax.numpy as jnp
from jax import lax
from jax.experimental import pallas as pl
from jax.experimental.pallas import tpu as pltpu
from jax.sharding import PartitionSpec as P

VMEM = pl.BlockSpec(memory_space=pltpu.VMEM)
ANY = pl.BlockSpec(memory_space=pl.ANY)
HBM = pl.BlockSpec(memory_space=pltpu.HBM)
SMEM = pl.BlockSpec(memory_space=pltpu.SMEM)
F32 = jnp.float32
BF16 = jnp.bfloat16
LIST_ROWS = 8
MIB = 1024 * 1024


def halves(x):
    high = x.astype(BF16)
    return high, (x - high.astype(F32)).astype(BF16)


def dot(a, b):
    return lax.dot_general(a, b, (((1,), (0,)), ((), ())), preferred_element_type=F32)


def dot_nt(a, b):
    return lax.dot_general(a, b, (((1,), (1,)), ((), ())), preferred_element_type=F32)


def ring(count, shift):
    return [((target + shift) % count, target) for target in range(count)]


def prepare(place, tensor, mine, turned, *, share):
    some = mine.shape[1]
    turned[...] = tensor[...].T
    start = place[1] * share
    for at in range(share):
        mine[at] = turned[pl.ds(start + at, some, stride=turned.shape[0] // some), :]


def after(block, *tokens):
    return pl.pallas_call(
        lambda *refs: None,
        out_shape=jax.ShapeDtypeStruct(block.shape, block.dtype),
        in_specs=[ANY] * (1 + len(tokens)),
        out_specs=ANY,
        input_output_aliases={0: 0},
        compiler_params=pltpu.CompilerParams(vmem_limit_bytes=MIB),
        name="after",
    )(block, *tokens)


def shifts_of(naux):
    plan = []
    for shift in range(1, naux // 2 + 1):
        if 2 * shift < naux:
            plan.append([(source, (source + shift) % naux) for source in range(naux)])
        else:
            plan.append([(z, z + shift) if z % 2 == 0 else (z + shift, z) for z in range(shift)])
    return plan


def select(block, list_rows, slots, width):
    parts = []
    for slot in range(slots):
        entry = list_rows[:1, slot : slot + 1]
        chosen = jnp.zeros((block.shape[0], width), F32)
        for j in range(block.shape[1] // width):
            chosen = jnp.where(entry == float(j), block[:, j * width : (j + 1) * width], chosen)
        parts.append(chosen)
    return jnp.concatenate(parts, axis=1)


def mix(place, near, far, tensor, rows, slots, width, share):
    nt = near.shape[0]
    pairs = tensor.shape[1] // (2 * width)
    near_list, far_list = near[0, 2 * width :, :], far[0, 2 * width :, :]
    which = [lax.rem(tau + nt - place[1], nt) for tau in range(nt)]
    left = []
    for kind in range(2):
        for tau in range(nt):
            start = pl.multiple_of(kind * width + place[1] * share, share)
            left.append(select(near[which[tau], pl.ds(start, share), :], far_list, slots, width))
    left_high, left_low = halves(jnp.concatenate(left, axis=0))
    high, low = halves(tensor[...])
    middle = dot(
        jnp.concatenate([left_high, left_high, left_low], axis=1), jnp.concatenate([high, low, high], axis=0)
    )
    for group in range(2 * nt):
        for at in range(pairs):
            rows[(group * pairs + at) * share : (group * pairs + at + 1) * share, :] = middle[
                group * share : (group + 1) * share, 2 * width * at : 2 * width * (at + 1)
            ]
    results = []
    for group in range(2 * nt):
        kind, tau = group // nt, group % nt
        right = select(far[which[tau], (1 - kind) * width : (2 - kind) * width, :], near_list, slots, width)
        zero = jnp.zeros_like(right)
        right_high, right_low = halves(
            jnp.concatenate([jnp.concatenate([right, zero], axis=1), jnp.concatenate([zero, right], axis=1)], axis=0)
        )

        rows_high, rows_low = halves(
            jnp.concatenate(
                [rows[pl.ds(group * pairs * share + at, pairs, stride=share), :] for at in range(share)], axis=0
            )
        )
        results.append(
            dot(
                jnp.concatenate([rows_high, rows_high, rows_low], axis=1),
                jnp.concatenate([right_high, right_low, right_high], axis=0),
            )
        )
    return results


def first(place, near, tensor, acc, token, rows, *, slots, width, share):
    token[...] = jnp.zeros_like(token)
    for group, result in enumerate(mix(place, near, near, tensor, rows, slots, width, share)):
        acc[group] = result


def second(place, near, acc, *refs, slots, width, share):
    refs, (side_direct, side_back, token, rows) = refs[:-4], refs[-4:]
    tensors, fars = refs[: len(refs) // 2], refs[len(refs) // 2 :]
    token[...] = jnp.zeros_like(token)
    listed = slots * width
    groups, tall, _ = acc.shape
    pairs = tall // share
    total = [acc[group] for group in range(groups)]
    for tensor, far in zip(tensors, fars):
        term = mix(place, near, far, tensor, rows, slots, width, share)
        total = [x + y for x, y in zip(total, term)]
    for group in range(groups):
        side = (side_direct, side_back)[group * 2 // groups]
        height = groups * pairs
        high, low = halves(total[group])
        for odd in range(2):
            row = (2 * (group % (groups // 2)) + odd) * pairs
            for at in range(share):
                for part, array in enumerate((high, low)):
                    side[part * height + row : part * height + row + pairs, at * listed : (at + 1) * listed] = array[
                        at * pairs : (at + 1) * pairs, odd * listed : (odd + 1) * listed
                    ]


def unfold(products, i, ordered):
    rows, block = ordered.shape[-2:]
    product = products[2 * i * block : (2 * i + 1) * block] + products[(2 * i + 1) * block : 2 * (i + 1) * block]
    product = (product[:, :rows] + product[:, rows:]).T
    pairs = block // 4
    for group in range(rows // (2 * pairs)):
        for odd in range(2):
            at = (2 * group + odd) * pairs
            ordered[i, pl.ds(2 * group * pairs + odd, pairs, stride=2), :] = product[at : at + pairs]


def at_sub(place, x, axis):
    zero = jnp.zeros_like(x)
    return jnp.where(place[2] == 0, jnp.concatenate([x, zero], axis=axis), jnp.concatenate([zero, x], axis=axis))


def meet_back(place, side, *refs, share, nt):
    count = (len(refs) - 1) // 3
    pieces, (tensor, *backs, ordered) = refs[: 2 * count], refs[2 * count :]
    listed = pieces[0].shape[1]
    half = pieces[0].shape[0] // share
    block = 2 * half
    for i in range(count):
        for which, source in enumerate(pieces[2 * i : 2 * i + 2]):
            start = pl.multiple_of(jnp.where(place[2] == which, 0, half), half)
            for at in range(share):
                high, low = halves(source[at * half : (at + 1) * half, :])
                tensor[pl.ds(2 * i * block + start, half), at * listed : (at + 1) * listed] = high
                tensor[pl.ds((2 * i + 1) * block + start, half), at * listed : (at + 1) * listed] = low
    products = dot_nt(tensor[2 * block :, :], side[...])
    for i, back_ref in enumerate(backs):
        unfold(products, i, ordered)
        back = ordered[i].T
        back_ref[...] = jnp.concatenate([back[:half], back[half:]], axis=1)


def meet_direct(place, side, tensor, out_ref, ordered, *, nt, naux):
    count = ordered.shape[0]
    block = ordered.shape[2]
    half = block // 2
    products = dot_nt(tensor[...], side[...])
    for i in range(count):
        unfold(products, i, ordered)
    for tau in range(nt):
        here = [jnp.zeros((half, block), F32)] * naux
        for shift in range(count):
            here[(naux - shift) % naux] = ordered[shift, tau * half : (tau + 1) * half, :]
        out_ref[tau] = at_sub(place, jnp.concatenate(here, axis=1), 0)


def complete(place, early, *refs):
    backs, out_ref = refs[:-1], refs[-1]
    nt, block, wide = early.shape
    naux = wide // block
    half = block // 2
    for tau in range(nt):
        parts = [jnp.zeros((block, block), F32)] * naux
        for shift, ref in enumerate(backs, 1):
            upper = ref[:, tau * half : (tau + 1) * half]
            lower = ref[:, (nt + tau) * half : (nt + tau + 1) * half]
            parts[shift] = at_sub(place, jnp.concatenate([upper, lower], axis=0), 1)
        total = early[tau] + jnp.concatenate(parts, axis=1)
        out_ref[tau] = pltpu.roll(total, place[3] * block, 1)


def local(three_center, occupied_green, virtual_green, block_list, sizes):
    nt, naux, nob, nsub = sizes
    slots = three_center.shape[2]
    width = three_center.shape[3]
    columns = three_center.shape[4]
    rows_aux = columns // width
    block_aux = rows_aux * nsub
    norb = occupied_green.shape[1]
    listed = slots * width
    share = width // nt
    nauxf = naux * block_aux
    me_orb, me_tau, me_sub, me_aux = (lax.axis_index(axis) for axis in ("orb", "tau", "sub", "aux"))
    place = jnp.stack([me_orb, me_tau, me_sub, me_aux]).astype(jnp.int32)
    tensor = three_center.reshape(listed, columns)
    limit = 24 + 3 * max(nob - 2, 0)

    def call(kernel, outs, scratch, flops, *arguments, **options):
        shapes = [jax.ShapeDtypeStruct(shape, kind) for shape, kind in outs]
        size = sum(4 * math.prod(x.shape) for x in arguments)
        return pl.pallas_call(
            functools.partial(kernel, **options),
            out_shape=shapes,
            in_specs=[SMEM] + [VMEM] * len(arguments),
            out_specs=[VMEM] * len(shapes),
            scratch_shapes=[pltpu.VMEM(shape, kind) for shape, kind in scratch],
            compiler_params=pltpu.CompilerParams(vmem_limit_bytes=limit * MIB),
            cost_estimate=pl.CostEstimate(flops=flops, bytes_accessed=size, transcendentals=0),
            name=kernel.__name__,
        )(place, *arguments)

    tensors = [lax.ppermute(tensor, "orb", ring(nob, shift)) for shift in range(1, nob)]
    (mine,) = call(
        prepare, [((share, rows_aux, listed), F32)], [((columns, listed), F32)], 0, tensor, share=share
    )
    plan = shifts_of(naux)
    pieces = [lax.ppermute(mine, "aux", pairs) for pairs in plan]
    swap = ring(nsub, 1)
    mine_other = lax.ppermute(mine, "sub", swap)
    small = jnp.concatenate(
        [
            occupied_green,
            virtual_green,
            jnp.pad(block_list.astype(F32), ((0, LIST_ROWS - 1), (0, norb - slots))),
        ]
    )
    near = jnp.stack([small] + [lax.ppermute(small, "tau", ring(nt, shift)) for shift in range(1, nt)])
    fars = []
    for shift in range(1, nob):
        pairs = [(a * nsub + c, b * nsub + (c + 1) % nsub) for a, b in ring(nob, shift) for c in range(nsub)]
        fars.append(lax.ppermute(near, ("orb", "sub"), pairs))

    groups = 2 * nt
    work = 6 * groups * share * columns * listed * 3
    rows = groups * rows_aux
    depth = share * listed
    options = dict(slots=slots, width=width, share=share)
    acc, token = call(
        first,
        [((groups, rows_aux // 2 * share, 2 * listed), F32), ((8, 128), F32)],
        [((groups * rows_aux // 2 * share, 2 * width), F32)],
        work,
        near,
        tensor,
        **options,
    )
    side_direct, side_back, token_late = call(
        second,
        [((rows, depth), BF16)] * 2 + [((8, 128), F32)],
        [((groups * rows_aux // 2 * share, 2 * width), F32)],
        work * (nob - 1),
        near,
        acc,
        *tensors,
        *fars,
        **options,
    )
    held = []
    for block in pieces:
        held.append(after(block, token_late, mine_other, *held[-1:]))
    pieces = held
    others = [lax.ppermute(block, "sub", swap) for block in pieces]
    flat = lambda block: block.reshape(-1, listed)
    count = 1 + len(plan)
    blocks = [flat(x) for pair in zip([mine] + pieces, [mine_other] + others) for x in pair]
    work = 8 * rows * block_aux * depth * count
    tensor, *backs = call(
        meet_back,
        [((2 * count * block_aux, depth), BF16)] + [((rows_aux, 2 * nt * rows_aux), F32)] * (count - 1),
        [((count - 1, nt * rows_aux, block_aux), F32)],
        work,
        side_back,
        *blocks,
        share=share,
        nt=nt,
    )
    returned = [lax.ppermute(back, "aux", ring(naux, i)) for i, back in enumerate(backs, 1)]
    shape = ((nt, block_aux, nauxf), F32)
    (early,) = call(
        meet_direct,
        [shape],
        [((count, nt * rows_aux, block_aux), F32)],
        work,
        side_direct,
        tensor,
        nt=nt,
        naux=naux,
    )
    (partial_chi,) = call(complete, [shape], [], 0, early, *returned)
    owners = nt * nob * nsub
    received = lax.all_to_all(
        partial_chi.reshape(owners, nt * block_aux // owners, nauxf),
        ("tau", "orb", "sub"),
        split_axis=0,
        concat_axis=0,
        tiled=True,
    )
    return received.sum(axis=0) * (-2.0 / math.sqrt(norb * slots * width))


def solution(mesh):
    sizes = tuple(mesh.shape[axis] for axis in ("tau", "aux", "orb", "sub"))
    in_specs = (
        P("aux", "orb", None, None, "sub"),
        P(("tau", "orb"), None),
        P(("tau", "orb"), None),
        P("orb", None),
    )
    out_specs = P(("tau", "aux", "orb", "sub"), None)
    return jax.shard_map(
        functools.partial(local, sizes=sizes), mesh=mesh, in_specs=in_specs, out_specs=out_specs, check_vma=False
    )
```

```python
import functools
import math

import jax
import jax.numpy as jnp
from jax import lax
from jax.experimental import pallas as pl
from jax.experimental.pallas import tpu as pltpu
from jax.sharding import PartitionSpec as P

VMEM = pl.BlockSpec(memory_space=pltpu.VMEM)
ANY = pl.BlockSpec(memory_space=pl.ANY)
HBM = pl.BlockSpec(memory_space=pltpu.HBM)
F32 = jnp.float32
BF16 = jnp.bfloat16
LIST_ROWS = 8
MIB = 1024 * 1024


def halves(x):
    high = x.astype(BF16)
    return high, (x - high.astype(F32)).astype(BF16)


def dot(a, b):
    return lax.dot_general(a, b, (((1,), (0,)), ((), ())), preferred_element_type=F32)


def dot_nt(a, b):
    return lax.dot_general(a, b, (((1,), (1,)), ((), ())), preferred_element_type=F32)


def ring(count, shift):
    return [((target + shift) % count, target) for target in range(count)]


def prepare(place, tensor, mine, turned, *, share):
    some = mine.shape[1]
    turned[...] = tensor[...].T
    start = place[1] * share
    for at in range(share):
        mine[at] = turned[pl.ds(start + at, some, stride=turned.shape[0] // some), :]


def after(block, *tokens):
    return pl.pallas_call(
        lambda *refs: None,
        out_shape=jax.ShapeDtypeStruct(block.shape, block.dtype),
        in_specs=[ANY] * (1 + len(tokens)),
        out_specs=ANY,
        input_output_aliases={0: 0},
        compiler_params=pltpu.CompilerParams(vmem_limit_bytes=MIB),
        name="after",
    )(block, *tokens)


def shifts_of(naux):
    plan = []
    for shift in range(1, naux // 2 + 1):
        if 2 * shift < naux:
            plan.append([(source, (source + shift) % naux) for source in range(naux)])
        else:
            plan.append([(z, z + shift) if z % 2 == 0 else (z + shift, z) for z in range(shift)])
    return plan


def select(block, list_rows, slots, width):
    parts = []
    for slot in range(slots):
        entry = list_rows[:1, slot : slot + 1]
        chosen = jnp.zeros((block.shape[0], width), F32)
        for j in range(block.shape[1] // width):
            chosen = jnp.where(entry == float(j), block[:, j * width : (j + 1) * width], chosen)
        parts.append(chosen)
    return jnp.concatenate(parts, axis=1)


def mix(place, near, far, tensor, rows, slots, width, share):
    nt = near.shape[0]
    pairs = tensor.shape[1] // (2 * width)
    near_list, far_list = near[0, 2 * width :, :], far[0, 2 * width :, :]
    which = [lax.rem(tau + nt - place[1], nt) for tau in range(nt)]
    left = []
    for kind in range(2):
        for tau in range(nt):
            start = pl.multiple_of(kind * width + place[1] * share, share)
            left.append(select(near[which[tau], pl.ds(start, share), :], far_list, slots, width))
    left_high, left_low = halves(jnp.concatenate(left, axis=0))
    high, low = halves(tensor[...])
    middle = dot(
        jnp.concatenate([left_high, left_high, left_low], axis=1), jnp.concatenate([high, low, high], axis=0)
    )
    for group in range(2 * nt):
        for at in range(pairs):
            rows[(group * pairs + at) * share : (group * pairs + at + 1) * share, :] = middle[
                group * share : (group + 1) * share, 2 * width * at : 2 * width * (at + 1)
            ]
    results = []
    for group in range(2 * nt):
        kind, tau = group // nt, group % nt
        right = select(far[which[tau], (1 - kind) * width : (2 - kind) * width, :], near_list, slots, width)
        zero = jnp.zeros_like(right)
        right_high, right_low = halves(
            jnp.concatenate([jnp.concatenate([right, zero], axis=1), jnp.concatenate([zero, right], axis=1)], axis=0)
        )

        rows_high, rows_low = halves(
            jnp.concatenate(
                [rows[pl.ds(group * pairs * share + at, pairs, stride=share), :] for at in range(share)], axis=0
            )
        )
        results.append(
            dot(
                jnp.concatenate([rows_high, rows_high, rows_low], axis=1),
                jnp.concatenate([right_high, right_low, right_high], axis=0),
            )
        )
    return results


def first(place, near, tensor, acc, token, rows, *, slots, width, share):
    token[...] = jnp.zeros_like(token)
    for group, result in enumerate(mix(place, near, near, tensor, rows, slots, width, share)):
        acc[group] = result


def second(place, near, acc, *refs, slots, width, share):
    refs, (sides, token, rows) = refs[:-3], refs[-3:]
    tensors, fars = refs[: len(refs) // 2], refs[len(refs) // 2 :]
    token[...] = jnp.zeros_like(token)
    listed = slots * width
    groups, tall, _ = acc.shape
    pairs = tall // share
    total = [acc[group] for group in range(groups)]
    for tensor, far in zip(tensors, fars):
        term = mix(place, near, far, tensor, rows, slots, width, share)
        total = [x + y for x, y in zip(total, term)]
    for group in range(groups):
        height = groups * pairs
        high, low = halves(total[group])
        for odd in range(2):
            row = (2 * (group % (groups // 2)) + odd) * pairs + 2 * height * (group * 2 // groups)
            for at in range(share):
                for part, array in enumerate((high, low)):
                    sides[
                        part * height + row : part * height + row + pairs, at * listed : (at + 1) * listed
                    ] = array[at * pairs : (at + 1) * pairs, odd * listed : (odd + 1) * listed]


def relay(pieces, tensor):
    share, half, listed = pieces[0].shape
    for i, source in enumerate(pieces):
        for at in range(share):
            high, low = halves(source[at])
            tensor[2 * i * half : (2 * i + 1) * half, at * listed : (at + 1) * listed] = high
            tensor[(2 * i + 1) * half : 2 * (i + 1) * half, at * listed : (at + 1) * listed] = low


def products(tensor, side, half):
    all_parts = dot_nt(tensor, side)
    width = side.shape[0] // 2
    rows = []
    for i in range(tensor.shape[0] // (2 * half)):
        block = all_parts[2 * i * half : (2 * i + 1) * half] + all_parts[(2 * i + 1) * half : 2 * (i + 1) * half]
        rows.append(block[:, :width] + block[:, width:])
    return jnp.concatenate(rows, axis=0)


def unfold(block, ordered, i):
    turned = block.T
    pairs = block.shape[0] // 4
    for group in range(turned.shape[0] // (2 * pairs)):
        for odd in range(2):
            at = (2 * group + odd) * pairs
            ordered[i, pl.ds(2 * group * pairs + odd, pairs, stride=2), :] = turned[at : at + pairs]


def at_sub(place, x, axis):
    zero = jnp.zeros_like(x)
    return by_sub(place, x, zero, axis)


def by_sub(place, own, other, axis):
    return jnp.where(
        place[2] == 0, jnp.concatenate([own, other], axis=axis), jnp.concatenate([other, own], axis=axis)
    )


def meet_own(place, sides, *refs):
    pieces, (direct, back, tensor) = refs[:-3], refs[-3:]
    half = pieces[0].shape[1]
    rows = sides.shape[0] // 2
    relay(pieces, tensor)
    direct[...] = products(tensor[...], sides[:rows, :], half)
    back[...] = products(tensor[4 * half :, :], sides[rows:, :], half)


def meet_back(place, sides, own, *refs):
    count = own.shape[0] // refs[0].shape[1]
    pieces, (tensor, *backs, ordered) = refs[:count], refs[count:]
    half = pieces[0].shape[1]
    relay(pieces, tensor)
    other = products(tensor[...], sides[sides.shape[0] // 2 :, :], half)
    for i, back_ref in enumerate(backs):
        rows = slice(i * half, (i + 1) * half)
        unfold(by_sub(place, own[rows, :], other[rows], 0), ordered, i)
        back = ordered[i].T
        back_ref[...] = jnp.concatenate([back[:half], back[half:]], axis=1)


def meet_direct(place, sides, own, tensor, out_ref, ordered, *, nt, naux):
    count = ordered.shape[0]
    block = ordered.shape[2]
    half = block // 2
    other = products(tensor[...], sides[: sides.shape[0] // 2, :], half)
    unfold(by_sub(place, own[:half, :], own[half:block, :], 0), ordered, 0)
    for i in range(1, count):
        rows = slice((i - 1) * half, i * half)
        unfold(by_sub(place, own[block + rows.start : block + rows.stop, :], other[rows], 0), ordered, i)
    for tau in range(nt):
        here = [jnp.zeros((half, block), F32)] * naux
        for shift in range(count):
            here[(naux - shift) % naux] = ordered[shift, tau * half : (tau + 1) * half, :]
        out_ref[tau] = at_sub(place, jnp.concatenate(here, axis=1), 0)


def complete(place, early, *refs):
    backs, out_ref = refs[:-1], refs[-1]
    nt, block, wide = early.shape
    naux = wide // block
    half = block // 2
    for tau in range(nt):
        parts = [jnp.zeros((block, block), F32)] * naux
        for shift, ref in enumerate(backs, 1):
            upper = ref[:, tau * half : (tau + 1) * half]
            lower = ref[:, (nt + tau) * half : (nt + tau + 1) * half]
            parts[shift] = at_sub(place, jnp.concatenate([upper, lower], axis=0), 1)
        total = early[tau] + jnp.concatenate(parts, axis=1)
        out_ref[tau] = pltpu.roll(total, place[3] * block, 1)


def local(three_center, occupied_green, virtual_green, block_list, sizes):
    nt, naux, nob, nsub = sizes
    slots = three_center.shape[2]
    width = three_center.shape[3]
    columns = three_center.shape[4]
    rows_aux = columns // width
    block_aux = rows_aux * nsub
    norb = occupied_green.shape[1]
    listed = slots * width
    share = width // nt
    nauxf = naux * block_aux
    tensor = three_center.reshape(listed, columns)
    limit = 24 + 3 * max(nob - 2, 0)

    def call(kernel, outs, scratch, flops, *arguments, **options):
        shapes = [jax.ShapeDtypeStruct(shape, kind) for shape, kind in outs]
        size = sum(4 * math.prod(x.shape) for x in arguments)

        def here(*refs):
            kernel([lax.axis_index(axis) for axis in ("orb", "tau", "sub", "aux")], *refs, **options)

        return pl.pallas_call(
            here,
            out_shape=shapes,
            in_specs=[VMEM] * len(arguments),
            out_specs=[VMEM] * len(shapes),
            scratch_shapes=[pltpu.VMEM(shape, kind) for shape, kind in scratch],
            compiler_params=pltpu.CompilerParams(vmem_limit_bytes=limit * MIB),
            cost_estimate=pl.CostEstimate(flops=flops, bytes_accessed=size, transcendentals=0),
            name=kernel.__name__,
        )(*arguments)

    tensors = [lax.ppermute(tensor, "orb", ring(nob, shift)) for shift in range(1, nob)]
    (mine,) = call(
        prepare, [((share, rows_aux, listed), F32)], [((columns, listed), F32)], 0, tensor, share=share
    )
    plan = shifts_of(naux)
    pieces = [lax.ppermute(mine, "aux", pairs) for pairs in plan]
    swap = ring(nsub, 1)
    mine_other = lax.ppermute(mine, "sub", swap)
    small = jnp.concatenate(
        [
            occupied_green,
            virtual_green,
            jnp.pad(block_list.astype(F32), ((0, LIST_ROWS - 1), (0, norb - slots))),
        ]
    )
    near = jnp.stack([small] + [lax.ppermute(small, "tau", ring(nt, shift)) for shift in range(1, nt)])
    fars = []
    for shift in range(1, nob):
        pairs = [(a * nsub + c, b * nsub + (c + 1) % nsub) for a, b in ring(nob, shift) for c in range(nsub)]
        fars.append(lax.ppermute(near, ("orb", "sub"), pairs))

    groups = 2 * nt
    work = 6 * groups * share * columns * listed * 3
    rows = groups * rows_aux
    depth = share * listed
    options = dict(slots=slots, width=width, share=share)
    acc, token = call(
        first,
        [((groups, rows_aux // 2 * share, 2 * listed), F32), ((8, 128), F32)],
        [((groups * rows_aux // 2 * share, 2 * width), F32)],
        work,
        near,
        tensor,
        **options,
    )
    sides, token_late = call(
        second,
        [((2 * rows, depth), BF16), ((8, 128), F32)],
        [((groups * rows_aux // 2 * share, 2 * width), F32)],
        work * (nob - 1),
        near,
        acc,
        *tensors,
        *fars,
        **options,
    )
    held = []
    for block in pieces:
        held.append(after(block, token_late, mine_other, *held[-1:]))
    pieces = held
    others = [lax.ppermute(block, "sub", swap) for block in pieces]
    count = 1 + len(plan)
    height = (count + 1) * rows_aux
    work = 8 * rows * depth * rows_aux
    wide = nt * rows_aux
    direct, back = call(
        meet_own,
        [((height, wide), F32), ((height - block_aux, wide), F32)],
        [((2 * height, depth), BF16)],
        work * count * 2,
        sides,
        mine,
        mine_other,
        *pieces,
    )
    others, *backs = call(
        meet_back,
        [((2 * len(plan) * rows_aux, depth), BF16)] + [((rows_aux, 2 * wide), F32)] * len(plan),
        [((len(plan), wide, block_aux), F32)],
        work * len(plan),
        sides,
        back,
        *others,
    )
    returned = [lax.ppermute(back, "aux", ring(naux, i)) for i, back in enumerate(backs, 1)]
    shape = ((nt, block_aux, nauxf), F32)
    (direct,) = call(
        meet_direct, [shape], [((count, wide, block_aux), F32)], work * len(plan), sides, direct, others, nt=nt, naux=naux
    )
    (partial_chi,) = call(complete, [shape], [], 0, direct, *returned)
    owners = nt * nob * nsub
    received = lax.all_to_all(
        partial_chi.reshape(owners, nt * block_aux // owners, nauxf),
        ("tau", "orb", "sub"),
        split_axis=0,
        concat_axis=0,
        tiled=True,
    )
    return received.sum(axis=0) * (-2.0 / math.sqrt(norb * slots * width))


def solution(mesh):
    sizes = tuple(mesh.shape[axis] for axis in ("tau", "aux", "orb", "sub"))
    in_specs = (
        P("aux", "orb", None, None, "sub"),
        P(("tau", "orb"), None),
        P(("tau", "orb"), None),
        P("orb", None),
    )
    out_specs = P(("tau", "aux", "orb", "sub"), None)
    return jax.shard_map(
        functools.partial(local, sizes=sizes), mesh=mesh, in_specs=in_specs, out_specs=out_specs, check_vma=False
    )
```

```python
import functools
import math

import jax
import jax.numpy as jnp
from jax import lax
from jax.experimental import pallas as pl
from jax.experimental.pallas import tpu as pltpu
from jax.sharding import PartitionSpec as P

VMEM = pl.BlockSpec(memory_space=pltpu.VMEM)
ANY = pl.BlockSpec(memory_space=pl.ANY)
HBM = pl.BlockSpec(memory_space=pltpu.HBM)
F32 = jnp.float32
BF16 = jnp.bfloat16
LIST_ROWS = 8
MIB = 1024 * 1024


def halves(x):
    high = x.astype(BF16)
    return high, (x - high.astype(F32)).astype(BF16)


def dot(a, b):
    return lax.dot_general(a, b, (((1,), (0,)), ((), ())), preferred_element_type=F32)


def dot_nt(a, b):
    return lax.dot_general(a, b, (((1,), (1,)), ((), ())), preferred_element_type=F32)


def ring(count, shift):
    return [((target + shift) % count, target) for target in range(count)]


def prepare(place, tensor, mine, again, turned, *, share):
    some = mine.shape[1]
    turned[...] = tensor[...].T
    start = place[1] * share
    for at in range(share):
        rows = turned[pl.ds(start + at, some, stride=turned.shape[0] // some), :]
        mine[at] = rows
        again[at] = rows


def after(block, *tokens):
    return pl.pallas_call(
        lambda *refs: None,
        out_shape=jax.ShapeDtypeStruct(block.shape, block.dtype),
        in_specs=[ANY] * (1 + len(tokens)),
        out_specs=ANY,
        input_output_aliases={0: 0},
        compiler_params=pltpu.CompilerParams(vmem_limit_bytes=MIB),
        name="after",
    )(block, *tokens)


def shifts_of(naux):
    plan = []
    for shift in range(1, naux // 2 + 1):
        if 2 * shift < naux:
            plan.append([(source, (source + shift) % naux) for source in range(naux)])
        else:
            plan.append([(z, z + shift) if z % 2 == 0 else (z + shift, z) for z in range(shift)])
    return plan


def select(block, list_rows, slots, width):
    parts = []
    for slot in range(slots):
        entry = list_rows[:1, slot : slot + 1]
        chosen = jnp.zeros((block.shape[0], width), F32)
        for j in range(block.shape[1] // width):
            chosen = jnp.where(entry == float(j), block[:, j * width : (j + 1) * width], chosen)
        parts.append(chosen)
    return jnp.concatenate(parts, axis=1)


def mix(place, near, far, tensor, rows, slots, width, share):
    nt = near.shape[0]
    pairs = tensor.shape[1] // (2 * width)
    near_list, far_list = near[0, 2 * width :, :], far[0, 2 * width :, :]
    which = [lax.rem(tau + nt - place[1], nt) for tau in range(nt)]
    left = []
    for kind in range(2):
        for tau in range(nt):
            start = pl.multiple_of(kind * width + place[1] * share, share)
            left.append(select(near[which[tau], pl.ds(start, share), :], far_list, slots, width))
    left_high, left_low = halves(jnp.concatenate(left, axis=0))
    high, low = halves(tensor[...])
    middle = dot(
        jnp.concatenate([left_high, left_high, left_low], axis=1), jnp.concatenate([high, low, high], axis=0)
    )
    for group in range(2 * nt):
        for at in range(pairs):
            rows[(group * pairs + at) * share : (group * pairs + at + 1) * share, :] = middle[
                group * share : (group + 1) * share, 2 * width * at : 2 * width * (at + 1)
            ]
    results = []
    for group in range(2 * nt):
        kind, tau = group // nt, group % nt
        right = select(far[which[tau], (1 - kind) * width : (2 - kind) * width, :], near_list, slots, width)
        zero = jnp.zeros_like(right)
        right_high, right_low = halves(
            jnp.concatenate([jnp.concatenate([right, zero], axis=1), jnp.concatenate([zero, right], axis=1)], axis=0)
        )

        rows_high, rows_low = halves(
            jnp.concatenate(
                [rows[pl.ds(group * pairs * share + at, pairs, stride=share), :] for at in range(share)], axis=0
            )
        )
        results.append(
            dot(
                jnp.concatenate([rows_high, rows_high, rows_low], axis=1),
                jnp.concatenate([right_high, right_low, right_high], axis=0),
            )
        )
    return results


def first(place, near, tensor, acc, token, rows, *, slots, width, share):
    token[...] = jnp.zeros_like(token)
    for group, result in enumerate(mix(place, near, near, tensor, rows, slots, width, share)):
        acc[group] = result


def second(place, near, acc, *refs, slots, width, share, others):
    refs, (sides, token, rows) = refs[: 2 * others], refs[-3:]
    tensors, fars = refs[: len(refs) // 2], refs[len(refs) // 2 :]
    token[...] = jnp.zeros_like(token)
    listed = slots * width
    groups, tall, _ = acc.shape
    pairs = tall // share
    total = [acc[group] for group in range(groups)]
    for tensor, far in zip(tensors, fars):
        term = mix(place, near, far, tensor, rows, slots, width, share)
        total = [x + y for x, y in zip(total, term)]
    for group in range(groups):
        height = groups * pairs
        high, low = halves(total[group])
        for odd in range(2):
            row = (2 * (group % (groups // 2)) + odd) * pairs + 2 * height * (group * 2 // groups)
            for at in range(share):
                for part, array in enumerate((high, low)):
                    sides[
                        part * height + row : part * height + row + pairs, at * listed : (at + 1) * listed
                    ] = array[at * pairs : (at + 1) * pairs, odd * listed : (odd + 1) * listed]


def relay(pieces, tensor):
    share, half, listed = pieces[0].shape
    for i, source in enumerate(pieces):
        for at in range(share):
            high, low = halves(source[at])
            tensor[2 * i * half : (2 * i + 1) * half, at * listed : (at + 1) * listed] = high
            tensor[(2 * i + 1) * half : 2 * (i + 1) * half, at * listed : (at + 1) * listed] = low


def products(tensor, side, half):
    all_parts = dot_nt(tensor, side)
    width = side.shape[0] // 2
    rows = []
    for i in range(tensor.shape[0] // (2 * half)):
        block = all_parts[2 * i * half : (2 * i + 1) * half] + all_parts[(2 * i + 1) * half : 2 * (i + 1) * half]
        rows.append(block[:, :width] + block[:, width:])
    return jnp.concatenate(rows, axis=0)


def unfold(block, ordered, i):
    turned = block.T
    pairs = block.shape[0] // 4
    for group in range(turned.shape[0] // (2 * pairs)):
        for odd in range(2):
            at = (2 * group + odd) * pairs
            ordered[i, pl.ds(2 * group * pairs + odd, pairs, stride=2), :] = turned[at : at + pairs]


def at_sub(place, x, axis):
    zero = jnp.zeros_like(x)
    return by_sub(place, x, zero, axis)


def by_sub(place, own, other, axis):
    return jnp.where(
        place[2] == 0, jnp.concatenate([own, other], axis=axis), jnp.concatenate([other, own], axis=axis)
    )


def fold(place, own, other, ordered):
    unfold(by_sub(place, own, other, 0), ordered, 0)
    back = ordered[0].T
    half = own.shape[0]
    return jnp.concatenate([back[:half], back[half:]], axis=1)


def meet_own(place, sides, *refs):
    count = (len(refs) - 4) // 3
    pieces, (direct, back, *backs, tensor, ordered) = refs[: 2 * count + 1], refs[2 * count + 1 :]
    half = pieces[0].shape[1]
    rows = sides.shape[0] // 2
    relay(pieces, tensor)
    direct[...] = products(tensor[...], sides[:rows, :], half)
    rest = products(tensor[4 * half :, :], sides[rows:, :], half)
    for i, back_ref in enumerate(backs):
        back_ref[...] = fold(
            place, rest[2 * i * half : (2 * i + 1) * half], rest[(2 * i + 1) * half : 2 * (i + 1) * half], ordered
        )
    back[...] = rest[-half:]


def meet_back(place, sides, own, piece, tensor, back_ref, ordered):
    half = piece.shape[1]
    relay([piece], tensor)
    other = products(tensor[...], sides[sides.shape[0] // 2 :, :], half)
    back_ref[...] = fold(place, own[...], other, ordered)


def meet_direct(place, sides, own, tensor, out_ref, ordered, *, nt, naux):
    count = ordered.shape[0]
    block = ordered.shape[2]
    half = block // 2
    other = products(tensor[...], sides[: sides.shape[0] // 2, :], half)
    for i in range(count):
        first_half = own[i * block : i * block + half, :]
        second_half = own[i * block + half : (i + 1) * block, :] if i < count - 1 else other
        unfold(by_sub(place, first_half, second_half, 0), ordered, i)
    for tau in range(nt):
        here = [jnp.zeros((half, block), F32)] * naux
        for shift in range(count):
            here[(naux - shift) % naux] = ordered[shift, tau * half : (tau + 1) * half, :]
        out_ref[tau] = at_sub(place, jnp.concatenate(here, axis=1), 0)


def complete(place, early, *refs):
    backs, out_ref = refs[:-1], refs[-1]
    nt, block, wide = early.shape
    naux = wide // block
    half = block // 2
    for tau in range(nt):
        parts = [jnp.zeros((block, block), F32)] * naux
        for shift, ref in enumerate(backs, 1):
            upper = ref[:, tau * half : (tau + 1) * half]
            lower = ref[:, (nt + tau) * half : (nt + tau + 1) * half]
            parts[shift] = at_sub(place, jnp.concatenate([upper, lower], axis=0), 1)
        total = early[tau] + jnp.concatenate(parts, axis=1)
        out_ref[tau] = pltpu.roll(total, place[3] * block, 1)


def local(three_center, occupied_green, virtual_green, block_list, sizes):
    nt, naux, nob, nsub = sizes
    slots = three_center.shape[2]
    width = three_center.shape[3]
    columns = three_center.shape[4]
    rows_aux = columns // width
    block_aux = rows_aux * nsub
    norb = occupied_green.shape[1]
    listed = slots * width
    share = width // nt
    nauxf = naux * block_aux
    tensor = three_center.reshape(listed, columns)
    limit = 24 + 3 * max(nob - 2, 0)

    def call(kernel, outs, scratch, flops, *arguments, **options):
        shapes = [jax.ShapeDtypeStruct(shape, kind) for shape, kind in outs]
        size = sum(4 * math.prod(x.shape) for x in arguments)

        def here(*refs):
            kernel([lax.axis_index(axis) for axis in ("orb", "tau", "sub", "aux")], *refs, **options)

        return pl.pallas_call(
            here,
            out_shape=shapes,
            in_specs=[VMEM] * len(arguments),
            out_specs=[VMEM] * len(shapes),
            scratch_shapes=[pltpu.VMEM(shape, kind) for shape, kind in scratch],
            compiler_params=pltpu.CompilerParams(vmem_limit_bytes=limit * MIB),
            cost_estimate=pl.CostEstimate(flops=flops, bytes_accessed=size, transcendentals=0),
            name=kernel.__name__,
        )(*arguments)

    tensors = [lax.ppermute(tensor, "orb", ring(nob, shift)) for shift in range(1, nob)]
    mine, again = call(
        prepare, [((share, rows_aux, listed), F32)] * 2, [((columns, listed), F32)], 0, tensor, share=share
    )
    plan = shifts_of(naux)
    swap = ring(nsub, 1)
    mine_other = lax.ppermute(mine, "sub", swap)
    small = jnp.concatenate(
        [
            occupied_green,
            virtual_green,
            jnp.pad(block_list.astype(F32), ((0, LIST_ROWS - 1), (0, norb - slots))),
        ]
    )
    near = jnp.stack([small] + [lax.ppermute(small, "tau", ring(nt, shift)) for shift in range(1, nt)])
    fars = []
    for shift in range(1, nob):
        pairs = [(a * nsub + c, b * nsub + (c + 1) % nsub) for a, b in ring(nob, shift) for c in range(nsub)]
        fars.append(lax.ppermute(near, ("orb", "sub"), pairs))

    groups = 2 * nt
    work = 6 * groups * share * columns * listed * 3
    rows = groups * rows_aux
    depth = share * listed
    options = dict(slots=slots, width=width, share=share)
    acc, token = call(
        first,
        [((groups, rows_aux // 2 * share, 2 * listed), F32), ((8, 128), F32)],
        [((groups * rows_aux // 2 * share, 2 * width), F32)],
        work,
        near,
        tensor,
        **options,
    )
    again = after(again, mine_other)
    pieces = [after(lax.ppermute(mine, "aux", pairs), token, *fars[-1:]) for pairs in plan[:-1]]
    pieces.append(lax.ppermute(again, "aux", plan[-1]))
    early = [mine_other, again]
    for block in pieces[:-1]:
        early += [block, lax.ppermute(block, "sub", swap)]
    sides, token_late = call(
        second,
        [((2 * rows, depth), BF16), ((8, 128), F32)],
        [((groups * rows_aux // 2 * share, 2 * width), F32)],
        work * (nob - 1),
        near,
        acc,
        *tensors,
        *fars,
        *early[::2],
        others=nob - 1,
        **options,
    )
    last = after(pieces[-1], token_late)
    last_other = lax.ppermute(last, "sub", swap)
    count = 1 + len(plan)
    work = 8 * rows * depth * rows_aux
    wide = nt * rows_aux
    shape = ((rows_aux, 2 * wide), F32)
    scratch = lambda count: ((count, wide, block_aux), F32)
    direct, back, *backs = call(
        meet_own,
        [(((2 * count - 1) * rows_aux, wide), F32), ((rows_aux, wide), F32)] + [shape] * (len(plan) - 1),
        [((2 * (2 * count - 1) * rows_aux, depth), BF16), scratch(1)],
        work * (2 * count - 1) * 2,
        sides,
        mine,
        *early[:1],
        *early[2:],
        last,
    )
    tensor, *last_back = call(
        meet_back,
        [((2 * rows_aux, depth), BF16), shape],
        [scratch(1)],
        work,
        sides,
        back,
        last_other,
    )
    backs += last_back
    returned = [lax.ppermute(back, "aux", ring(naux, i)) for i, back in enumerate(backs, 1)]
    shape = ((nt, block_aux, nauxf), F32)
    (direct,) = call(
        meet_direct, [shape], [scratch(count)], work, sides, direct, tensor, nt=nt, naux=naux
    )
    (partial_chi,) = call(complete, [shape], [], 0, direct, *returned)
    owners = nt * nob * nsub
    received = lax.all_to_all(
        partial_chi.reshape(owners, nt * block_aux // owners, nauxf),
        ("tau", "orb", "sub"),
        split_axis=0,
        concat_axis=0,
        tiled=True,
    )
    return received.sum(axis=0) * (-2.0 / math.sqrt(norb * slots * width))


def solution(mesh):
    sizes = tuple(mesh.shape[axis] for axis in ("tau", "aux", "orb", "sub"))
    in_specs = (
        P("aux", "orb", None, None, "sub"),
        P(("tau", "orb"), None),
        P(("tau", "orb"), None),
        P("orb", None),
    )
    out_specs = P(("tau", "aux", "orb", "sub"), None)
    return jax.shard_map(
        functools.partial(local, sizes=sizes), mesh=mesh, in_specs=in_specs, out_specs=out_specs, check_vma=False
    )
```

```python
import functools
import math

import jax
import jax.numpy as jnp
from jax import lax
from jax.experimental import pallas as pl
from jax.experimental.pallas import tpu as pltpu
from jax.sharding import PartitionSpec as P

VMEM = pl.BlockSpec(memory_space=pltpu.VMEM)
ANY = pl.BlockSpec(memory_space=pl.ANY)
HBM = pl.BlockSpec(memory_space=pltpu.HBM)
F32 = jnp.float32
BF16 = jnp.bfloat16
LIST_ROWS = 8
MIB = 1024 * 1024


def halves(x):
    high = x.astype(BF16)
    return high, (x - high.astype(F32)).astype(BF16)


def dot(a, b):
    return lax.dot_general(a, b, (((1,), (0,)), ((), ())), preferred_element_type=F32)


def dot_nt(a, b):
    return lax.dot_general(a, b, (((1,), (1,)), ((), ())), preferred_element_type=F32)


def ring(count, shift):
    return [((target + shift) % count, target) for target in range(count)]


def prepare(place, tensor, mine, again, turned, *, share):
    some = mine.shape[1]
    turned[...] = tensor[...].T
    start = place[1] * share
    for at in range(share):
        rows = turned[pl.ds(start + at, some, stride=turned.shape[0] // some), :]
        mine[at] = rows
        again[at] = rows


def halve(place, block, token, *outs):
    some = outs[0].shape[0]
    for i, out in enumerate(outs):
        out[...] = block[i * some : (i + 1) * some]


def after(block, *tokens):
    return pl.pallas_call(
        lambda *refs: None,
        out_shape=jax.ShapeDtypeStruct(block.shape, block.dtype),
        in_specs=[ANY] * (1 + len(tokens)),
        out_specs=ANY,
        input_output_aliases={0: 0},
        compiler_params=pltpu.CompilerParams(vmem_limit_bytes=MIB),
        name="after",
    )(block, *tokens)


def shifts_of(naux):
    plan = []
    for shift in range(1, naux // 2 + 1):
        if 2 * shift < naux:
            plan.append([(source, (source + shift) % naux) for source in range(naux)])
        else:
            plan.append([(z, z + shift) if z % 2 == 0 else (z + shift, z) for z in range(shift)])
    return plan


def select(block, list_rows, slots, width):
    parts = []
    for slot in range(slots):
        entry = list_rows[:1, slot : slot + 1]
        chosen = jnp.zeros((block.shape[0], width), F32)
        for j in range(block.shape[1] // width):
            chosen = jnp.where(entry == float(j), block[:, j * width : (j + 1) * width], chosen)
        parts.append(chosen)
    return jnp.concatenate(parts, axis=1)


def mix(place, near, far, tensor, rows, slots, width, share):
    nt = near.shape[0]
    pairs = tensor.shape[1] // (2 * width)
    near_list, far_list = near[0, 2 * width :, :], far[0, 2 * width :, :]
    which = [lax.rem(tau + nt - place[1], nt) for tau in range(nt)]
    left = []
    for kind in range(2):
        for tau in range(nt):
            start = pl.multiple_of(kind * width + place[1] * share, share)
            left.append(select(near[which[tau], pl.ds(start, share), :], far_list, slots, width))
    left_high, left_low = halves(jnp.concatenate(left, axis=0))
    high, low = halves(tensor[...])
    middle = dot(
        jnp.concatenate([left_high, left_high, left_low], axis=1), jnp.concatenate([high, low, high], axis=0)
    )
    for group in range(2 * nt):
        for at in range(pairs):
            rows[(group * pairs + at) * share : (group * pairs + at + 1) * share, :] = middle[
                group * share : (group + 1) * share, 2 * width * at : 2 * width * (at + 1)
            ]
    results = []
    for group in range(2 * nt):
        kind, tau = group // nt, group % nt
        right = select(far[which[tau], (1 - kind) * width : (2 - kind) * width, :], near_list, slots, width)
        zero = jnp.zeros_like(right)
        right_high, right_low = halves(
            jnp.concatenate([jnp.concatenate([right, zero], axis=1), jnp.concatenate([zero, right], axis=1)], axis=0)
        )

        rows_high, rows_low = halves(
            jnp.concatenate(
                [rows[pl.ds(group * pairs * share + at, pairs, stride=share), :] for at in range(share)], axis=0
            )
        )
        results.append(
            dot(
                jnp.concatenate([rows_high, rows_high, rows_low], axis=1),
                jnp.concatenate([right_high, right_low, right_high], axis=0),
            )
        )
    return results


def first(place, near, tensor, acc, token, rows, *, slots, width, share):
    token[...] = jnp.zeros_like(token)
    for group, result in enumerate(mix(place, near, near, tensor, rows, slots, width, share)):
        acc[group] = result


def second(place, near, acc, *refs, slots, width, share, others):
    refs, (sides, token, rows) = refs[: 2 * others], refs[-3:]
    tensors, fars = refs[: len(refs) // 2], refs[len(refs) // 2 :]
    token[...] = jnp.zeros_like(token)
    listed = slots * width
    groups, tall, _ = acc.shape
    pairs = tall // share
    total = [acc[group] for group in range(groups)]
    for tensor, far in zip(tensors, fars):
        term = mix(place, near, far, tensor, rows, slots, width, share)
        total = [x + y for x, y in zip(total, term)]
    for group in range(groups):
        height = groups * pairs
        high, low = halves(total[group])
        for odd in range(2):
            row = (2 * (group % (groups // 2)) + odd) * pairs + 2 * height * (group * 2 // groups)
            for at in range(share):
                for part, array in enumerate((high, low)):
                    sides[
                        part * height + row : part * height + row + pairs, at * listed : (at + 1) * listed
                    ] = array[at * pairs : (at + 1) * pairs, odd * listed : (odd + 1) * listed]


def relay(pieces, tensor):
    for i, parts in enumerate(pieces):
        at = 0
        for part in parts:
            per, half, listed = part.shape
            for inner in range(per):
                high, low = halves(part[inner])
                tensor[2 * i * half : (2 * i + 1) * half, at * listed : (at + 1) * listed] = high
                tensor[(2 * i + 1) * half : 2 * (i + 1) * half, at * listed : (at + 1) * listed] = low
                at += 1


def products(tensor, side, half):
    all_parts = dot_nt(tensor, side)
    width = side.shape[0] // 2
    rows = []
    for i in range(tensor.shape[0] // (2 * half)):
        block = all_parts[2 * i * half : (2 * i + 1) * half] + all_parts[(2 * i + 1) * half : 2 * (i + 1) * half]
        rows.append(block[:, :width] + block[:, width:])
    return jnp.concatenate(rows, axis=0)


def unfold(block, ordered, i):
    turned = block.T
    pairs = block.shape[0] // 4
    for group in range(turned.shape[0] // (2 * pairs)):
        for odd in range(2):
            at = (2 * group + odd) * pairs
            ordered[i, pl.ds(2 * group * pairs + odd, pairs, stride=2), :] = turned[at : at + pairs]


def at_sub(place, x, axis):
    zero = jnp.zeros_like(x)
    return by_sub(place, x, zero, axis)


def by_sub(place, own, other, axis):
    return jnp.where(
        place[2] == 0, jnp.concatenate([own, other], axis=axis), jnp.concatenate([other, own], axis=axis)
    )


def fold(place, own, other, ordered):
    unfold(by_sub(place, own, other, 0), ordered, 0)
    back = ordered[0].T
    half = own.shape[0]
    return jnp.concatenate([back[:half], back[half:]], axis=1)


def meet_own(place, sides, *refs, count):
    refs, (direct, back, *backs, tensor, ordered) = refs[: 4 * count - 1], refs[4 * count - 1 :]
    pieces = [refs[:1], refs[1:2]] + [refs[i : i + 2] for i in range(2, 4 * count - 2, 2)] + [refs[-1:]]
    half = refs[0].shape[1]
    rows = sides.shape[0] // 2
    relay(pieces, tensor)
    direct[...] = products(tensor[...], sides[:rows, :], half)
    rest = products(tensor[4 * half :, :], sides[rows:, :], half)
    for i, back_ref in enumerate(backs):
        back_ref[...] = fold(
            place, rest[2 * i * half : (2 * i + 1) * half], rest[(2 * i + 1) * half : 2 * (i + 1) * half], ordered
        )
    back[...] = rest[-half:]


def meet_back(place, sides, own, piece, tensor, back_ref, ordered):
    half = piece.shape[1]
    relay([[piece]], tensor)
    other = products(tensor[...], sides[sides.shape[0] // 2 :, :], half)
    back_ref[...] = fold(place, own[...], other, ordered)


def meet_direct(place, sides, own, tensor, out_ref, ordered, *, nt, naux):
    count = ordered.shape[0]
    block = ordered.shape[2]
    half = block // 2
    other = products(tensor[...], sides[: sides.shape[0] // 2, :], half)
    for i in range(count):
        first_half = own[i * block : i * block + half, :]
        second_half = own[i * block + half : (i + 1) * block, :] if i < count - 1 else other
        unfold(by_sub(place, first_half, second_half, 0), ordered, i)
    for tau in range(nt):
        here = [jnp.zeros((half, block), F32)] * naux
        for shift in range(count):
            here[(naux - shift) % naux] = ordered[shift, tau * half : (tau + 1) * half, :]
        out_ref[tau] = at_sub(place, jnp.concatenate(here, axis=1), 0)


def complete(place, early, *refs):
    backs, out_ref = refs[:-1], refs[-1]
    nt, block, wide = early.shape
    naux = wide // block
    half = block // 2
    for tau in range(nt):
        parts = [jnp.zeros((block, block), F32)] * naux
        for shift, ref in enumerate(backs, 1):
            upper = ref[:, tau * half : (tau + 1) * half]
            lower = ref[:, (nt + tau) * half : (nt + tau + 1) * half]
            parts[shift] = at_sub(place, jnp.concatenate([upper, lower], axis=0), 1)
        total = early[tau] + jnp.concatenate(parts, axis=1)
        out_ref[tau] = pltpu.roll(total, place[3] * block, 1)


def local(three_center, occupied_green, virtual_green, block_list, sizes):
    nt, naux, nob, nsub = sizes
    slots = three_center.shape[2]
    width = three_center.shape[3]
    columns = three_center.shape[4]
    rows_aux = columns // width
    block_aux = rows_aux * nsub
    norb = occupied_green.shape[1]
    listed = slots * width
    share = width // nt
    nauxf = naux * block_aux
    tensor = three_center.reshape(listed, columns)
    limit = 24 + 3 * max(nob - 2, 0)

    def call(kernel, outs, scratch, flops, *arguments, **options):
        shapes = [jax.ShapeDtypeStruct(shape, kind) for shape, kind in outs]
        size = sum(4 * math.prod(x.shape) for x in arguments)

        def here(*refs):
            kernel([lax.axis_index(axis) for axis in ("orb", "tau", "sub", "aux")], *refs, **options)

        return pl.pallas_call(
            here,
            out_shape=shapes,
            in_specs=[VMEM] * len(arguments),
            out_specs=[VMEM] * len(shapes),
            scratch_shapes=[pltpu.VMEM(shape, kind) for shape, kind in scratch],
            compiler_params=pltpu.CompilerParams(vmem_limit_bytes=limit * MIB),
            cost_estimate=pl.CostEstimate(flops=flops, bytes_accessed=size, transcendentals=0),
            name=kernel.__name__,
        )(*arguments)

    tensors = [lax.ppermute(tensor, "orb", ring(nob, shift)) for shift in range(1, nob)]
    mine, again = call(
        prepare, [((share, rows_aux, listed), F32)] * 2, [((columns, listed), F32)], 0, tensor, share=share
    )
    plan = shifts_of(naux)
    swap = ring(nsub, 1)
    mine_other = lax.ppermute(mine, "sub", swap)
    small = jnp.concatenate(
        [
            occupied_green,
            virtual_green,
            jnp.pad(block_list.astype(F32), ((0, LIST_ROWS - 1), (0, norb - slots))),
        ]
    )
    near = jnp.stack([small] + [lax.ppermute(small, "tau", ring(nt, shift)) for shift in range(1, nt)])
    groups = 2 * nt
    work = 6 * groups * share * columns * listed * 3
    rows = groups * rows_aux
    depth = share * listed
    options = dict(slots=slots, width=width, share=share)
    acc, token = call(
        first,
        [((groups, rows_aux // 2 * share, 2 * listed), F32), ((8, 128), F32)],
        [((groups * rows_aux // 2 * share, 2 * width), F32)],
        work,
        near,
        tensor,
        **options,
    )
    again = after(again, token)
    early = [mine_other]
    for pairs in plan[:-1]:
        parts = call(
            halve, [((share // 2, rows_aux, listed), F32)] * 2, [], 0, lax.ppermute(mine, "aux", pairs), token
        )
        early += [*parts, *(lax.ppermute(part, "sub", swap) for part in parts)]
    last = lax.ppermute(again, "aux", plan[-1])
    fars = []
    late_near = after(near, *early)
    for shift in range(1, nob):
        pairs = [(a * nsub + c, b * nsub + (c + 1) % nsub) for a, b in ring(nob, shift) for c in range(nsub)]
        fars.append(lax.ppermute(late_near, ("orb", "sub"), pairs))
    sides, token_late = call(
        second,
        [((2 * rows, depth), BF16), ((8, 128), F32)],
        [((groups * rows_aux // 2 * share, 2 * width), F32)],
        work * (nob - 1),
        near,
        acc,
        *tensors,
        *fars,
        *early,
        others=nob - 1,
        **options,
    )
    last = after(last, token_late)
    last_other = lax.ppermute(last, "sub", swap)
    count = 1 + len(plan)
    work = 8 * rows * depth * rows_aux
    wide = nt * rows_aux
    shape = ((rows_aux, 2 * wide), F32)
    scratch = lambda count: ((count, wide, block_aux), F32)
    direct, back, *backs = call(
        meet_own,
        [(((2 * count - 1) * rows_aux, wide), F32), ((rows_aux, wide), F32)] + [shape] * (len(plan) - 1),
        [((2 * (2 * count - 1) * rows_aux, depth), BF16), scratch(1)],
        work * (2 * count - 1) * 2,
        sides,
        mine,
        *early,
        last,
        count=len(plan),
    )
    tensor, *last_back = call(
        meet_back,
        [((2 * rows_aux, depth), BF16), shape],
        [scratch(1)],
        work,
        sides,
        back,
        last_other,
    )
    backs += last_back
    returned = [lax.ppermute(back, "aux", ring(naux, i)) for i, back in enumerate(backs, 1)]
    shape = ((nt, block_aux, nauxf), F32)
    (direct,) = call(
        meet_direct, [shape], [scratch(count)], work, sides, direct, tensor, nt=nt, naux=naux
    )
    (partial_chi,) = call(complete, [shape], [], 0, direct, *returned)
    owners = nt * nob * nsub
    received = lax.all_to_all(
        partial_chi.reshape(owners, nt * block_aux // owners, nauxf),
        ("tau", "orb", "sub"),
        split_axis=0,
        concat_axis=0,
        tiled=True,
    )
    return received.sum(axis=0) * (-2.0 / math.sqrt(norb * slots * width))


def solution(mesh):
    sizes = tuple(mesh.shape[axis] for axis in ("tau", "aux", "orb", "sub"))
    in_specs = (
        P("aux", "orb", None, None, "sub"),
        P(("tau", "orb"), None),
        P(("tau", "orb"), None),
        P("orb", None),
    )
    out_specs = P(("tau", "aux", "orb", "sub"), None)
    return jax.shard_map(
        functools.partial(local, sizes=sizes), mesh=mesh, in_specs=in_specs, out_specs=out_specs, check_vma=False
    )
```

```python
import functools
import math

import jax
import jax.numpy as jnp
from jax import lax
from jax.experimental import pallas as pl
from jax.experimental.pallas import tpu as pltpu
from jax.sharding import PartitionSpec as P

VMEM = pl.BlockSpec(memory_space=pltpu.VMEM)
ANY = pl.BlockSpec(memory_space=pl.ANY)
HBM = pl.BlockSpec(memory_space=pltpu.HBM)
F32 = jnp.float32
BF16 = jnp.bfloat16
LIST_ROWS = 8
MIB = 1024 * 1024


def halves(x):
    high = x.astype(BF16)
    return high, (x - high.astype(F32)).astype(BF16)


def dot(a, b):
    return lax.dot_general(a, b, (((1,), (0,)), ((), ())), preferred_element_type=F32)


def dot_nt(a, b):
    return lax.dot_general(a, b, (((1,), (1,)), ((), ())), preferred_element_type=F32)


def ring(count, shift):
    return [((target + shift) % count, target) for target in range(count)]


def prepare(place, tensor, mine, again, turned, *, share):
    some = mine.shape[1]
    turned[...] = tensor[...].T
    start = place[1] * share
    for at in range(share):
        rows = turned[pl.ds(start + at, some, stride=turned.shape[0] // some), :]
        mine[at] = rows
        again[at] = rows


def halve(place, block, token, *outs):
    some = outs[0].shape[0]
    for i, out in enumerate(outs):
        out[...] = block[i * some : (i + 1) * some]


def after(block, *tokens):
    return pl.pallas_call(
        lambda *refs: None,
        out_shape=jax.ShapeDtypeStruct(block.shape, block.dtype),
        in_specs=[ANY] * (1 + len(tokens)),
        out_specs=ANY,
        input_output_aliases={0: 0},
        compiler_params=pltpu.CompilerParams(vmem_limit_bytes=MIB),
        name="after",
    )(block, *tokens)


def shifts_of(naux):
    plan = []
    for shift in range(1, naux // 2 + 1):
        if 2 * shift < naux:
            plan.append([(source, (source + shift) % naux) for source in range(naux)])
        else:
            plan.append([(z, z + shift) if z % 2 == 0 else (z + shift, z) for z in range(shift)])
    return plan


def select(block, list_rows, slots, width):
    parts = []
    for slot in range(slots):
        entry = list_rows[:1, slot : slot + 1]
        chosen = jnp.zeros((block.shape[0], width), F32)
        for j in range(block.shape[1] // width):
            chosen = jnp.where(entry == float(j), block[:, j * width : (j + 1) * width], chosen)
        parts.append(chosen)
    return jnp.concatenate(parts, axis=1)


def mix(place, near, far, tensor, rows, slots, width, share):
    nt = near.shape[0]
    pairs = tensor.shape[1] // (2 * width)
    near_list, far_list = near[0, 2 * width :, :], far[0, 2 * width :, :]
    which = [lax.rem(tau + nt - place[1], nt) for tau in range(nt)]
    left = []
    for kind in range(2):
        for tau in range(nt):
            start = pl.multiple_of(kind * width + place[1] * share, share)
            left.append(select(near[which[tau], pl.ds(start, share), :], far_list, slots, width))
    left_high, left_low = halves(jnp.concatenate(left, axis=0))
    high, low = halves(tensor[...])
    middle = dot(
        jnp.concatenate([left_high, left_high, left_low], axis=1), jnp.concatenate([high, low, high], axis=0)
    )
    for group in range(2 * nt):
        for at in range(pairs):
            rows[(group * pairs + at) * share : (group * pairs + at + 1) * share, :] = middle[
                group * share : (group + 1) * share, 2 * width * at : 2 * width * (at + 1)
            ]
    results = []
    for group in range(2 * nt):
        kind, tau = group // nt, group % nt
        right = select(far[which[tau], (1 - kind) * width : (2 - kind) * width, :], near_list, slots, width)
        zero = jnp.zeros_like(right)
        right_high, right_low = halves(
            jnp.concatenate([jnp.concatenate([right, zero], axis=1), jnp.concatenate([zero, right], axis=1)], axis=0)
        )

        rows_high, rows_low = halves(
            jnp.concatenate(
                [rows[pl.ds(group * pairs * share + at, pairs, stride=share), :] for at in range(share)], axis=0
            )
        )
        results.append(
            dot(
                jnp.concatenate([rows_high, rows_high, rows_low], axis=1),
                jnp.concatenate([right_high, right_low, right_high], axis=0),
            )
        )
    return results


def first(place, near, tensor, acc, token, rows, *, slots, width, share):
    token[...] = jnp.zeros_like(token)
    for group, result in enumerate(mix(place, near, near, tensor, rows, slots, width, share)):
        acc[group] = result


def second(place, near, acc, *refs, slots, width, share, others):
    refs, (sides, token, rows) = refs[: 2 * others], refs[-3:]
    tensors, fars = refs[: len(refs) // 2], refs[len(refs) // 2 :]
    token[...] = jnp.zeros_like(token)
    listed = slots * width
    groups, tall, _ = acc.shape
    pairs = tall // share
    total = [acc[group] for group in range(groups)]
    for tensor, far in zip(tensors, fars):
        term = mix(place, near, far, tensor, rows, slots, width, share)
        total = [x + y for x, y in zip(total, term)]
    for group in range(groups):
        height = groups * pairs
        high, low = halves(total[group])
        for odd in range(2):
            row = (2 * (group % (groups // 2)) + odd) * pairs + 2 * height * (group * 2 // groups)
            for at in range(share):
                for part, array in enumerate((high, low)):
                    sides[
                        part * height + row : part * height + row + pairs, at * listed : (at + 1) * listed
                    ] = array[at * pairs : (at + 1) * pairs, odd * listed : (odd + 1) * listed]


def relay(pieces, tensor):
    for i, parts in enumerate(pieces):
        at = 0
        for part in parts:
            per, half, listed = part.shape
            for inner in range(per):
                high, low = halves(part[inner])
                tensor[2 * i * half : (2 * i + 1) * half, at * listed : (at + 1) * listed] = high
                tensor[(2 * i + 1) * half : 2 * (i + 1) * half, at * listed : (at + 1) * listed] = low
                at += 1


def products(tensor, side, half):
    all_parts = dot_nt(tensor, side)
    width = side.shape[0] // 2
    rows = []
    for i in range(tensor.shape[0] // (2 * half)):
        block = all_parts[2 * i * half : (2 * i + 1) * half] + all_parts[(2 * i + 1) * half : 2 * (i + 1) * half]
        rows.append(block[:, :width] + block[:, width:])
    return jnp.concatenate(rows, axis=0)


def unfold(block, ordered, i):
    turned = block.T
    pairs = block.shape[0] // 4
    for group in range(turned.shape[0] // (2 * pairs)):
        for odd in range(2):
            at = (2 * group + odd) * pairs
            ordered[i, pl.ds(2 * group * pairs + odd, pairs, stride=2), :] = turned[at : at + pairs]


def at_sub(place, x, axis):
    zero = jnp.zeros_like(x)
    return by_sub(place, x, zero, axis)


def by_sub(place, own, other, axis):
    return jnp.where(
        place[2] == 0, jnp.concatenate([own, other], axis=axis), jnp.concatenate([other, own], axis=axis)
    )


def fold(place, own, other, ordered):
    unfold(by_sub(place, own, other, 0), ordered, 0)
    back = ordered[0].T
    half = own.shape[0]
    return jnp.concatenate([back[:half], back[half:]], axis=1)


def meet_own(place, sides, *refs, count):
    refs, (direct, back, *backs, tensor, ordered) = refs[: 4 * count - 1], refs[4 * count - 1 :]
    pieces = [refs[:1], refs[1:2]] + [refs[i : i + 2] for i in range(2, 4 * count - 2, 2)] + [refs[-1:]]
    half = refs[0].shape[1]
    rows = sides.shape[0] // 2
    relay(pieces, tensor)
    direct[...] = products(tensor[...], sides[:rows, :], half)
    rest = products(tensor[4 * half :, :], sides[rows:, :], half)
    for i, back_ref in enumerate(backs):
        back_ref[...] = fold(
            place, rest[2 * i * half : (2 * i + 1) * half], rest[(2 * i + 1) * half : 2 * (i + 1) * half], ordered
        )
    back[...] = rest[-half:]


def meet_back(place, sides, own, piece, tensor, back_ref, ordered):
    half = piece.shape[1]
    relay([[piece]], tensor)
    other = products(tensor[...], sides[sides.shape[0] // 2 :, :], half)
    back_ref[...] = fold(place, own[...], other, ordered)


def meet_direct(place, sides, own, tensor, out_ref, ordered, *, nt, naux):
    count = ordered.shape[0]
    block = ordered.shape[2]
    half = block // 2
    other = products(tensor[...], sides[: sides.shape[0] // 2, :], half)
    for i in range(count):
        first_half = own[i * block : i * block + half, :]
        second_half = own[i * block + half : (i + 1) * block, :] if i < count - 1 else other
        unfold(by_sub(place, first_half, second_half, 0), ordered, i)
    for tau in range(nt):
        here = [jnp.zeros((half, block), F32)] * naux
        for shift in range(count):
            here[(naux - shift) % naux] = ordered[shift, tau * half : (tau + 1) * half, :]
        out_ref[tau] = at_sub(place, jnp.concatenate(here, axis=1), 0)


def complete(place, early, *refs):
    backs, out_ref = refs[:-1], refs[-1]
    nt, block, wide = early.shape
    naux = wide // block
    half = block // 2
    for tau in range(nt):
        parts = [jnp.zeros((block, block), F32)] * naux
        for shift, ref in enumerate(backs, 1):
            upper = ref[:, tau * half : (tau + 1) * half]
            lower = ref[:, (nt + tau) * half : (nt + tau + 1) * half]
            parts[shift] = at_sub(place, jnp.concatenate([upper, lower], axis=0), 1)
        total = early[tau] + jnp.concatenate(parts, axis=1)
        out_ref[tau] = pltpu.roll(total, place[3] * block, 1)


def local(three_center, occupied_green, virtual_green, block_list, sizes):
    nt, naux, nob, nsub = sizes
    slots = three_center.shape[2]
    width = three_center.shape[3]
    columns = three_center.shape[4]
    rows_aux = columns // width
    block_aux = rows_aux * nsub
    norb = occupied_green.shape[1]
    listed = slots * width
    share = width // nt
    nauxf = naux * block_aux
    tensor = three_center.reshape(listed, columns)
    limit = 24 + 3 * max(nob - 2, 0)

    def call(kernel, outs, scratch, flops, *arguments, **options):
        shapes = [jax.ShapeDtypeStruct(shape, kind) for shape, kind in outs]
        size = sum(4 * math.prod(x.shape) for x in arguments)

        def here(*refs):
            kernel([lax.axis_index(axis) for axis in ("orb", "tau", "sub", "aux")], *refs, **options)

        return pl.pallas_call(
            here,
            out_shape=shapes,
            in_specs=[VMEM] * len(arguments),
            out_specs=[VMEM] * len(shapes),
            scratch_shapes=[pltpu.VMEM(shape, kind) for shape, kind in scratch],
            compiler_params=pltpu.CompilerParams(vmem_limit_bytes=limit * MIB),
            cost_estimate=pl.CostEstimate(flops=flops, bytes_accessed=size, transcendentals=0),
            name=kernel.__name__,
        )(*arguments)

    tensors = [lax.ppermute(tensor, "orb", ring(nob, shift)) for shift in range(1, nob)]
    mine, again = call(
        prepare, [((share, rows_aux, listed), F32)] * 2, [((columns, listed), F32)], 0, tensor, share=share
    )
    plan = shifts_of(naux)
    swap = ring(nsub, 1)
    mine_other = lax.ppermute(mine, "sub", swap)
    small = jnp.concatenate(
        [
            occupied_green,
            virtual_green,
            jnp.pad(block_list.astype(F32), ((0, LIST_ROWS - 1), (0, norb - slots))),
        ]
    )
    near = jnp.stack([small] + [lax.ppermute(small, "tau", ring(nt, shift)) for shift in range(1, nt)])
    groups = 2 * nt
    work = 6 * groups * share * columns * listed * 3
    rows = groups * rows_aux
    depth = share * listed
    options = dict(slots=slots, width=width, share=share)
    acc, token = call(
        first,
        [((groups, rows_aux // 2 * share, 2 * listed), F32), ((8, 128), F32)],
        [((groups * rows_aux // 2 * share, 2 * width), F32)],
        work,
        near,
        tensor,
        **options,
    )
    early = [mine_other]
    for pairs in plan[:-1]:
        parts = call(
            halve, [((share // 2, rows_aux, listed), F32)] * 2, [], 0, lax.ppermute(mine, "aux", pairs), token
        )
        early += [*parts, *(lax.ppermute(part, "sub", swap) for part in parts)]
    last = lax.ppermute(after(again, *early[1:2]), "aux", plan[-1])
    fars = []
    late_near = after(near, *early)
    for shift in range(1, nob):
        pairs = [(a * nsub + c, b * nsub + (c + 1) % nsub) for a, b in ring(nob, shift) for c in range(nsub)]
        fars.append(lax.ppermute(late_near, ("orb", "sub"), pairs))
    sides, token_late = call(
        second,
        [((2 * rows, depth), BF16), ((8, 128), F32)],
        [((groups * rows_aux // 2 * share, 2 * width), F32)],
        work * 2,
        near,
        acc,
        *tensors,
        *fars,
        *early,
        others=nob - 1,
        **options,
    )
    last = after(last, token_late)
    last_other = lax.ppermute(last, "sub", swap)
    count = 1 + len(plan)
    work = 8 * rows * depth * rows_aux
    wide = nt * rows_aux
    shape = ((rows_aux, 2 * wide), F32)
    scratch = lambda count: ((count, wide, block_aux), F32)
    direct, back, *backs = call(
        meet_own,
        [(((2 * count - 1) * rows_aux, wide), F32), ((rows_aux, wide), F32)] + [shape] * (len(plan) - 1),
        [((2 * (2 * count - 1) * rows_aux, depth), BF16), scratch(1)],
        work * (2 * count - 1) * 2,
        sides,
        mine,
        *early,
        last,
        count=len(plan),
    )
    tensor, *last_back = call(
        meet_back,
        [((2 * rows_aux, depth), BF16), shape],
        [scratch(1)],
        work,
        sides,
        back,
        last_other,
    )
    backs += last_back
    returned = [lax.ppermute(back, "aux", ring(naux, i)) for i, back in enumerate(backs, 1)]
    shape = ((nt, block_aux, nauxf), F32)
    (direct,) = call(
        meet_direct, [shape], [scratch(count)], work, sides, direct, tensor, nt=nt, naux=naux
    )
    (partial_chi,) = call(complete, [shape], [], 0, direct, *returned)
    owners = nt * nob * nsub
    received = lax.all_to_all(
        partial_chi.reshape(owners, nt * block_aux // owners, nauxf),
        ("tau", "orb", "sub"),
        split_axis=0,
        concat_axis=0,
        tiled=True,
    )
    return received.sum(axis=0) * (-2.0 / math.sqrt(norb * slots * width))


def solution(mesh):
    sizes = tuple(mesh.shape[axis] for axis in ("tau", "aux", "orb", "sub"))
    in_specs = (
        P("aux", "orb", None, None, "sub"),
        P(("tau", "orb"), None),
        P(("tau", "orb"), None),
        P("orb", None),
    )
    out_specs = P(("tau", "aux", "orb", "sub"), None)
    return jax.shard_map(
        functools.partial(local, sizes=sizes), mesh=mesh, in_specs=in_specs, out_specs=out_specs, check_vma=False
    )
```

```python
import functools
import math

import jax
import jax.numpy as jnp
from jax import lax
from jax.experimental import pallas as pl
from jax.experimental.pallas import tpu as pltpu
from jax.sharding import PartitionSpec as P

VMEM = pl.BlockSpec(memory_space=pltpu.VMEM)
ANY = pl.BlockSpec(memory_space=pl.ANY)
HBM = pl.BlockSpec(memory_space=pltpu.HBM)
F32 = jnp.float32
BF16 = jnp.bfloat16
LIST_ROWS = 8
MIB = 1024 * 1024


def halves(x):
    high = x.astype(BF16)
    return high, (x - high.astype(F32)).astype(BF16)


def dot(a, b):
    return lax.dot_general(a, b, (((1,), (0,)), ((), ())), preferred_element_type=F32)


def dot_nt(a, b):
    return lax.dot_general(a, b, (((1,), (1,)), ((), ())), preferred_element_type=F32)


def ring(count, shift):
    return [((target + shift) % count, target) for target in range(count)]


def prepare(place, tensor, mine, again, turned, *, share):
    some = mine.shape[1]
    turned[...] = tensor[...].T
    start = place[1] * share
    for at in range(share):
        rows = turned[pl.ds(start + at, some, stride=turned.shape[0] // some), :]
        mine[at] = rows
        again[at] = rows


def halve(place, block, token, *outs):
    some = outs[0].shape[0]
    for i, out in enumerate(outs):
        out[...] = block[i * some : (i + 1) * some]


def after(block, *tokens):
    return pl.pallas_call(
        lambda *refs: None,
        out_shape=jax.ShapeDtypeStruct(block.shape, block.dtype),
        in_specs=[ANY] * (1 + len(tokens)),
        out_specs=ANY,
        input_output_aliases={0: 0},
        compiler_params=pltpu.CompilerParams(vmem_limit_bytes=MIB),
        name="after",
    )(block, *tokens)


def shifts_of(naux):
    plan = []
    for shift in range(1, naux // 2 + 1):
        if 2 * shift < naux:
            plan.append([(source, (source + shift) % naux) for source in range(naux)])
        else:
            plan.append([(z, z + shift) if z % 2 == 0 else (z + shift, z) for z in range(shift)])
    return plan


def select(block, list_rows, slots, width):
    parts = []
    for slot in range(slots):
        entry = list_rows[:1, slot : slot + 1]
        chosen = jnp.zeros((block.shape[0], width), F32)
        for j in range(block.shape[1] // width):
            chosen = jnp.where(entry == float(j), block[:, j * width : (j + 1) * width], chosen)
        parts.append(chosen)
    return jnp.concatenate(parts, axis=1)


def mix(place, near, far, tensor, rows, slots, width, share):
    nt = near.shape[0]
    pairs = tensor.shape[1] // (2 * width)
    near_list, far_list = near[0, 2 * width :, :], far[0, 2 * width :, :]
    which = [lax.rem(tau + nt - place[1], nt) for tau in range(nt)]
    left = []
    for kind in range(2):
        for tau in range(nt):
            start = pl.multiple_of(kind * width + place[1] * share, share)
            left.append(select(near[which[tau], pl.ds(start, share), :], far_list, slots, width))
    left_high, left_low = halves(jnp.concatenate(left, axis=0))
    high, low = halves(tensor[...])
    middle = dot(
        jnp.concatenate([left_high, left_high, left_low], axis=1), jnp.concatenate([high, low, high], axis=0)
    )
    for group in range(2 * nt):
        for at in range(pairs):
            rows[(group * pairs + at) * share : (group * pairs + at + 1) * share, :] = middle[
                group * share : (group + 1) * share, 2 * width * at : 2 * width * (at + 1)
            ]
    results = []
    for group in range(2 * nt):
        kind, tau = group // nt, group % nt
        right = select(far[which[tau], (1 - kind) * width : (2 - kind) * width, :], near_list, slots, width)
        zero = jnp.zeros_like(right)
        right_high, right_low = halves(
            jnp.concatenate([jnp.concatenate([right, zero], axis=1), jnp.concatenate([zero, right], axis=1)], axis=0)
        )

        rows_high, rows_low = halves(
            jnp.concatenate(
                [rows[pl.ds(group * pairs * share + at, pairs, stride=share), :] for at in range(share)], axis=0
            )
        )
        results.append(
            dot(
                jnp.concatenate([rows_high, rows_high, rows_low], axis=1),
                jnp.concatenate([right_high, right_low, right_high], axis=0),
            )
        )
    return results


def first(place, near, tensor, acc, token, rows, *, slots, width, share):
    token[...] = jnp.zeros_like(token)
    for group, result in enumerate(mix(place, near, near, tensor, rows, slots, width, share)):
        acc[group] = result


def second(place, near, acc, *refs, slots, width, share, others):
    refs, (sides, token, rows) = refs[: 2 * others], refs[-3:]
    tensors, fars = refs[: len(refs) // 2], refs[len(refs) // 2 :]
    token[...] = jnp.zeros_like(token)
    listed = slots * width
    groups, tall, _ = acc.shape
    pairs = tall // share
    total = [acc[group] for group in range(groups)]
    for tensor, far in zip(tensors, fars):
        term = mix(place, near, far, tensor, rows, slots, width, share)
        total = [x + y for x, y in zip(total, term)]
    for group in range(groups):
        height = groups * pairs
        high, low = halves(total[group])
        for odd in range(2):
            row = (2 * (group % (groups // 2)) + odd) * pairs + 2 * height * (group * 2 // groups)
            for at in range(share):
                for part, array in enumerate((high, low)):
                    sides[
                        part * height + row : part * height + row + pairs, at * listed : (at + 1) * listed
                    ] = array[at * pairs : (at + 1) * pairs, odd * listed : (odd + 1) * listed]


def relay(pieces, tensor):
    for i, parts in enumerate(pieces):
        at = 0
        for part in parts:
            per, half, listed = part.shape
            for inner in range(per):
                high, low = halves(part[inner])
                tensor[2 * i * half : (2 * i + 1) * half, at * listed : (at + 1) * listed] = high
                tensor[(2 * i + 1) * half : 2 * (i + 1) * half, at * listed : (at + 1) * listed] = low
                at += 1


def products(tensor, side, half):
    all_parts = dot_nt(tensor, side)
    width = side.shape[0] // 2
    rows = []
    for i in range(tensor.shape[0] // (2 * half)):
        block = all_parts[2 * i * half : (2 * i + 1) * half] + all_parts[(2 * i + 1) * half : 2 * (i + 1) * half]
        rows.append(block[:, :width] + block[:, width:])
    return jnp.concatenate(rows, axis=0)


def unfold(block, ordered, i):
    turned = block.T
    pairs = block.shape[0] // 4
    for group in range(turned.shape[0] // (2 * pairs)):
        for odd in range(2):
            at = (2 * group + odd) * pairs
            ordered[i, pl.ds(2 * group * pairs + odd, pairs, stride=2), :] = turned[at : at + pairs]


def at_sub(place, x, axis):
    zero = jnp.zeros_like(x)
    return by_sub(place, x, zero, axis)


def by_sub(place, own, other, axis):
    return jnp.where(
        place[2] == 0, jnp.concatenate([own, other], axis=axis), jnp.concatenate([other, own], axis=axis)
    )


def fold(place, own, other, ordered):
    unfold(by_sub(place, own, other, 0), ordered, 0)
    back = ordered[0].T
    half = own.shape[0]
    return jnp.concatenate([back[:half], back[half:]], axis=1)


def meet_own(place, sides, *refs, count):
    refs, (direct, back, *backs, tensor, ordered) = refs[: 4 * count - 1], refs[4 * count - 1 :]
    pieces = [refs[:1], refs[1:2]] + [refs[i : i + 2] for i in range(2, 4 * count - 2, 2)] + [refs[-1:]]
    half = refs[0].shape[1]
    rows = sides.shape[0] // 2
    relay(pieces, tensor)
    direct[...] = products(tensor[...], sides[:rows, :], half)
    rest = products(tensor[4 * half :, :], sides[rows:, :], half)
    for i, back_ref in enumerate(backs):
        back_ref[...] = fold(
            place, rest[2 * i * half : (2 * i + 1) * half], rest[(2 * i + 1) * half : 2 * (i + 1) * half], ordered
        )
    back[...] = rest[-half:]


def meet_back(place, sides, own, piece, tensor, back_ref, ordered):
    half = piece.shape[1]
    relay([[piece]], tensor)
    other = products(tensor[...], sides[sides.shape[0] // 2 :, :], half)
    back_ref[...] = fold(place, own[...], other, ordered)


def meet_direct(place, sides, own, tensor, out_ref, ordered, *, nt, naux):
    count = ordered.shape[0]
    block = ordered.shape[2]
    half = block // 2
    other = products(tensor[...], sides[: sides.shape[0] // 2, :], half)
    for i in range(count):
        first_half = own[i * block : i * block + half, :]
        second_half = own[i * block + half : (i + 1) * block, :] if i < count - 1 else other
        unfold(by_sub(place, first_half, second_half, 0), ordered, i)
    for tau in range(nt):
        here = [jnp.zeros((half, block), F32)] * naux
        for shift in range(count):
            here[(naux - shift) % naux] = ordered[shift, tau * half : (tau + 1) * half, :]
        out_ref[tau] = at_sub(place, jnp.concatenate(here, axis=1), 0)


def complete(place, early, *refs):
    backs, out_ref = refs[:-1], refs[-1]
    nt, block, wide = early.shape
    naux = wide // block
    half = block // 2
    for tau in range(nt):
        parts = [jnp.zeros((block, block), F32)] * naux
        for shift, ref in enumerate(backs, 1):
            upper = ref[:, tau * half : (tau + 1) * half]
            lower = ref[:, (nt + tau) * half : (nt + tau + 1) * half]
            parts[shift] = at_sub(place, jnp.concatenate([upper, lower], axis=0), 1)
        total = early[tau] + jnp.concatenate(parts, axis=1)
        out_ref[tau] = pltpu.roll(total, place[3] * block, 1)


def local(three_center, occupied_green, virtual_green, block_list, sizes):
    nt, naux, nob, nsub = sizes
    slots = three_center.shape[2]
    width = three_center.shape[3]
    columns = three_center.shape[4]
    rows_aux = columns // width
    block_aux = rows_aux * nsub
    norb = occupied_green.shape[1]
    listed = slots * width
    share = width // nt
    nauxf = naux * block_aux
    tensor = three_center.reshape(listed, columns)
    limit = 24 + 3 * max(nob - 2, 0)

    def call(kernel, outs, scratch, flops, *arguments, **options):
        shapes = [jax.ShapeDtypeStruct(shape, kind) for shape, kind in outs]
        size = sum(4 * math.prod(x.shape) for x in arguments)

        def here(*refs):
            kernel([lax.axis_index(axis) for axis in ("orb", "tau", "sub", "aux")], *refs, **options)

        return pl.pallas_call(
            here,
            out_shape=shapes,
            in_specs=[VMEM] * len(arguments),
            out_specs=[VMEM] * len(shapes),
            scratch_shapes=[pltpu.VMEM(shape, kind) for shape, kind in scratch],
            compiler_params=pltpu.CompilerParams(vmem_limit_bytes=limit * MIB),
            cost_estimate=pl.CostEstimate(flops=flops, bytes_accessed=size, transcendentals=0),
            name=kernel.__name__,
        )(*arguments)

    tensors = [lax.ppermute(tensor, "orb", ring(nob, shift)) for shift in range(1, nob)]
    mine, again = call(
        prepare, [((share, rows_aux, listed), F32)] * 2, [((columns, listed), F32)], 0, tensor, share=share
    )
    plan = shifts_of(naux)
    swap = ring(nsub, 1)
    small = jnp.concatenate(
        [
            occupied_green,
            virtual_green,
            jnp.pad(block_list.astype(F32), ((0, LIST_ROWS - 1), (0, norb - slots))),
        ]
    )
    near = jnp.stack([small] + [lax.ppermute(small, "tau", ring(nt, shift)) for shift in range(1, nt)])
    groups = 2 * nt
    work = 6 * groups * share * columns * listed * 3
    rows = groups * rows_aux
    depth = share * listed
    options = dict(slots=slots, width=width, share=share)
    acc, token = call(
        first,
        [((groups, rows_aux // 2 * share, 2 * listed), F32), ((8, 128), F32)],
        [((groups * rows_aux // 2 * share, 2 * width), F32)],
        0,
        near,
        tensor,
        **options,
    )
    mine_other = lax.ppermute(mine, "sub", swap)
    early = [mine_other]
    for pairs in plan[:-1]:
        parts = call(
            halve, [((share // 2, rows_aux, listed), F32)] * 2, [], 0, lax.ppermute(mine, "aux", pairs), token
        )
        early += [*parts, *(lax.ppermute(part, "sub", swap) for part in parts)]
    last = lax.ppermute(after(again, lax.ppermute(token, "sub", swap)), "aux", plan[-1])
    fars = []
    late_near = after(near, *early)
    for shift in range(1, nob):
        pairs = [(a * nsub + c, b * nsub + (c + 1) % nsub) for a, b in ring(nob, shift) for c in range(nsub)]
        fars.append(lax.ppermute(late_near, ("orb", "sub"), pairs))
    sides, token_late = call(
        second,
        [((2 * rows, depth), BF16), ((8, 128), F32)],
        [((groups * rows_aux // 2 * share, 2 * width), F32)],
        work,
        near,
        acc,
        *tensors,
        *fars,
        *early,
        others=nob - 1,
        **options,
    )
    last = after(last, token_late)
    last_other = lax.ppermute(last, "sub", swap)
    count = 1 + len(plan)
    work = 8 * rows * depth * rows_aux
    wide = nt * rows_aux
    shape = ((rows_aux, 2 * wide), F32)
    scratch = lambda count: ((count, wide, block_aux), F32)
    direct, back, *backs = call(
        meet_own,
        [(((2 * count - 1) * rows_aux, wide), F32), ((rows_aux, wide), F32)] + [shape] * (len(plan) - 1),
        [((2 * (2 * count - 1) * rows_aux, depth), BF16), scratch(1)],
        work * (2 * count - 1) * 2,
        sides,
        mine,
        *early,
        last,
        count=len(plan),
    )
    tensor, *last_back = call(
        meet_back,
        [((2 * rows_aux, depth), BF16), shape],
        [scratch(1)],
        work,
        sides,
        back,
        last_other,
    )
    backs += last_back
    returned = [lax.ppermute(back, "aux", ring(naux, i)) for i, back in enumerate(backs, 1)]
    shape = ((nt, block_aux, nauxf), F32)
    (direct,) = call(
        meet_direct, [shape], [scratch(count)], work, sides, direct, tensor, nt=nt, naux=naux
    )
    (partial_chi,) = call(complete, [shape], [], 0, direct, *returned)
    owners = nt * nob * nsub
    received = lax.all_to_all(
        partial_chi.reshape(owners, nt * block_aux // owners, nauxf),
        ("tau", "orb", "sub"),
        split_axis=0,
        concat_axis=0,
        tiled=True,
    )
    return received.sum(axis=0) * (-2.0 / math.sqrt(norb * slots * width))


def solution(mesh):
    sizes = tuple(mesh.shape[axis] for axis in ("tau", "aux", "orb", "sub"))
    in_specs = (
        P("aux", "orb", None, None, "sub"),
        P(("tau", "orb"), None),
        P(("tau", "orb"), None),
        P("orb", None),
    )
    out_specs = P(("tau", "aux", "orb", "sub"), None)
    return jax.shard_map(
        functools.partial(local, sizes=sizes), mesh=mesh, in_specs=in_specs, out_specs=out_specs, check_vma=False
    )
```

```python
import functools
import math

import jax
import jax.numpy as jnp
from jax import lax
from jax.experimental import pallas as pl
from jax.experimental.pallas import tpu as pltpu
from jax.sharding import PartitionSpec as P

VMEM = pl.BlockSpec(memory_space=pltpu.VMEM)
ANY = pl.BlockSpec(memory_space=pl.ANY)
HBM = pl.BlockSpec(memory_space=pltpu.HBM)
F32 = jnp.float32
BF16 = jnp.bfloat16
LIST_ROWS = 8
MIB = 1024 * 1024


def halves(x):
    high = x.astype(BF16)
    return high, (x - high.astype(F32)).astype(BF16)


def dot(a, b):
    return lax.dot_general(a, b, (((1,), (0,)), ((), ())), preferred_element_type=F32)


def dot_nt(a, b):
    return lax.dot_general(a, b, (((1,), (1,)), ((), ())), preferred_element_type=F32)


def ring(count, shift):
    return [((target + shift) % count, target) for target in range(count)]


def prepare(place, tensor, mine, again, turned, *, share):
    some = mine.shape[1]
    turned[...] = tensor[...].T
    start = place[1] * share
    for at in range(share):
        rows = turned[pl.ds(start + at, some, stride=turned.shape[0] // some), :]
        mine[at] = rows
        again[at] = rows


def halve(place, block, token, *outs):
    some = outs[0].shape[0]
    for i, out in enumerate(outs):
        out[...] = block[i * some : (i + 1) * some]


def after(block, *tokens):
    return pl.pallas_call(
        lambda *refs: None,
        out_shape=jax.ShapeDtypeStruct(block.shape, block.dtype),
        in_specs=[ANY] * (1 + len(tokens)),
        out_specs=ANY,
        input_output_aliases={0: 0},
        compiler_params=pltpu.CompilerParams(vmem_limit_bytes=MIB),
        name="after",
    )(block, *tokens)


def shifts_of(naux):
    plan = []
    for shift in range(1, naux // 2 + 1):
        if 2 * shift < naux:
            plan.append((shift, [(source, (source + shift) % naux) for source in range(naux)]))
        else:
            plan.append((shift, [(z, z + shift) if z % 2 == 0 else (z + shift, z) for z in range(shift)]))
    return plan[::-1]


def select(block, list_rows, slots, width):
    parts = []
    for slot in range(slots):
        entry = list_rows[:1, slot : slot + 1]
        chosen = jnp.zeros((block.shape[0], width), F32)
        for j in range(block.shape[1] // width):
            chosen = jnp.where(entry == float(j), block[:, j * width : (j + 1) * width], chosen)
        parts.append(chosen)
    return jnp.concatenate(parts, axis=1)


def mix(place, near, far, tensor, rows, slots, width, share):
    nt = near.shape[0]
    pairs = tensor.shape[1] // (2 * width)
    near_list, far_list = near[0, 2 * width :, :], far[0, 2 * width :, :]
    which = [lax.rem(tau + nt - place[1], nt) for tau in range(nt)]
    left = []
    for kind in range(2):
        for tau in range(nt):
            start = pl.multiple_of(kind * width + place[1] * share, share)
            left.append(select(near[which[tau], pl.ds(start, share), :], far_list, slots, width))
    left_high, left_low = halves(jnp.concatenate(left, axis=0))
    high, low = halves(tensor[...])
    middle = dot(
        jnp.concatenate([left_high, left_high, left_low], axis=1), jnp.concatenate([high, low, high], axis=0)
    )
    for group in range(2 * nt):
        for at in range(pairs):
            rows[(group * pairs + at) * share : (group * pairs + at + 1) * share, :] = middle[
                group * share : (group + 1) * share, 2 * width * at : 2 * width * (at + 1)
            ]
    results = []
    for group in range(2 * nt):
        kind, tau = group // nt, group % nt
        right = select(far[which[tau], (1 - kind) * width : (2 - kind) * width, :], near_list, slots, width)
        zero = jnp.zeros_like(right)
        right_high, right_low = halves(
            jnp.concatenate([jnp.concatenate([right, zero], axis=1), jnp.concatenate([zero, right], axis=1)], axis=0)
        )

        rows_high, rows_low = halves(
            jnp.concatenate(
                [rows[pl.ds(group * pairs * share + at, pairs, stride=share), :] for at in range(share)], axis=0
            )
        )
        results.append(
            dot(
                jnp.concatenate([rows_high, rows_high, rows_low], axis=1),
                jnp.concatenate([right_high, right_low, right_high], axis=0),
            )
        )
    return results


def first(place, near, tensor, acc, token, rows, *, slots, width, share):
    token[...] = jnp.zeros_like(token)
    for group, result in enumerate(mix(place, near, near, tensor, rows, slots, width, share)):
        acc[group] = result


def second(place, near, acc, *refs, slots, width, share, others):
    refs, (sides, token, rows) = refs[: 2 * others], refs[-3:]
    tensors, fars = refs[: len(refs) // 2], refs[len(refs) // 2 :]
    token[...] = jnp.zeros_like(token)
    listed = slots * width
    groups, tall, _ = acc.shape
    pairs = tall // share
    total = [acc[group] for group in range(groups)]
    for tensor, far in zip(tensors, fars):
        term = mix(place, near, far, tensor, rows, slots, width, share)
        total = [x + y for x, y in zip(total, term)]
    for group in range(groups):
        height = groups * pairs
        high, low = halves(total[group])
        for odd in range(2):
            row = (2 * (group % (groups // 2)) + odd) * pairs + 2 * height * (group * 2 // groups)
            for at in range(share):
                for part, array in enumerate((high, low)):
                    sides[
                        part * height + row : part * height + row + pairs, at * listed : (at + 1) * listed
                    ] = array[at * pairs : (at + 1) * pairs, odd * listed : (odd + 1) * listed]


def relay(pieces, tensor):
    for i, parts in enumerate(pieces):
        at = 0
        for part in parts:
            per, half, listed = part.shape
            for inner in range(per):
                high, low = halves(part[inner])
                tensor[2 * i * half : (2 * i + 1) * half, at * listed : (at + 1) * listed] = high
                tensor[(2 * i + 1) * half : 2 * (i + 1) * half, at * listed : (at + 1) * listed] = low
                at += 1


def products(tensor, side, half):
    all_parts = dot_nt(tensor, side)
    width = side.shape[0] // 2
    rows = []
    for i in range(tensor.shape[0] // (2 * half)):
        block = all_parts[2 * i * half : (2 * i + 1) * half] + all_parts[(2 * i + 1) * half : 2 * (i + 1) * half]
        rows.append(block[:, :width] + block[:, width:])
    return jnp.concatenate(rows, axis=0)


def unfold(block, ordered, i):
    turned = block.T
    pairs = block.shape[0] // 4
    for group in range(turned.shape[0] // (2 * pairs)):
        for odd in range(2):
            at = (2 * group + odd) * pairs
            ordered[i, pl.ds(2 * group * pairs + odd, pairs, stride=2), :] = turned[at : at + pairs]


def at_sub(place, x, axis):
    zero = jnp.zeros_like(x)
    return by_sub(place, x, zero, axis)


def by_sub(place, own, other, axis):
    return jnp.where(
        place[2] == 0, jnp.concatenate([own, other], axis=axis), jnp.concatenate([other, own], axis=axis)
    )


def fold(place, own, other, ordered):
    unfold(by_sub(place, own, other, 0), ordered, 0)
    back = ordered[0].T
    half = own.shape[0]
    return jnp.concatenate([back[:half], back[half:]], axis=1)


def meet_own(place, sides, *refs, count):
    refs, (direct, back, *backs, tensor, ordered) = refs[: 4 * count - 1], refs[4 * count - 1 :]
    pieces = [refs[:1], refs[1:2]] + [refs[i : i + 2] for i in range(2, 4 * count - 2, 2)] + [refs[-1:]]
    half = refs[0].shape[1]
    rows = sides.shape[0] // 2
    relay(pieces, tensor)
    direct[...] = products(tensor[...], sides[:rows, :], half)
    rest = products(tensor[4 * half :, :], sides[rows:, :], half)
    for i, back_ref in enumerate(backs):
        back_ref[...] = fold(
            place, rest[2 * i * half : (2 * i + 1) * half], rest[(2 * i + 1) * half : 2 * (i + 1) * half], ordered
        )
    back[...] = rest[-half:]


def meet_back(place, sides, own, piece, tensor, back_ref, ordered):
    half = piece.shape[1]
    relay([[piece]], tensor)
    other = products(tensor[...], sides[sides.shape[0] // 2 :, :], half)
    back_ref[...] = fold(place, own[...], other, ordered)


def meet_direct(place, sides, own, tensor, out_ref, ordered, *, nt, naux):
    count = ordered.shape[0]
    block = ordered.shape[2]
    half = block // 2
    other = products(tensor[...], sides[: sides.shape[0] // 2, :], half)
    for i in range(count):
        first_half = own[i * block : i * block + half, :]
        second_half = own[i * block + half : (i + 1) * block, :] if i < count - 1 else other
        unfold(by_sub(place, first_half, second_half, 0), ordered, i)
    for tau in range(nt):
        here = [jnp.zeros((half, block), F32)] * naux
        for i in range(count):
            here[(naux - count + i) % naux if i else 0] = ordered[i, tau * half : (tau + 1) * half, :]
        out_ref[tau] = at_sub(place, jnp.concatenate(here, axis=1), 0)


def complete(place, early, *refs):
    backs, out_ref = refs[:-1], refs[-1]
    nt, block, wide = early.shape
    naux = wide // block
    half = block // 2
    for tau in range(nt):
        parts = [jnp.zeros((block, block), F32)] * naux
        for shift, ref in enumerate(backs[::-1], 1):
            upper = ref[:, tau * half : (tau + 1) * half]
            lower = ref[:, (nt + tau) * half : (nt + tau + 1) * half]
            parts[shift] = at_sub(place, jnp.concatenate([upper, lower], axis=0), 1)
        total = early[tau] + jnp.concatenate(parts, axis=1)
        out_ref[tau] = pltpu.roll(total, place[3] * block, 1)


def local(three_center, occupied_green, virtual_green, block_list, sizes):
    nt, naux, nob, nsub = sizes
    slots = three_center.shape[2]
    width = three_center.shape[3]
    columns = three_center.shape[4]
    rows_aux = columns // width
    block_aux = rows_aux * nsub
    norb = occupied_green.shape[1]
    listed = slots * width
    share = width // nt
    nauxf = naux * block_aux
    tensor = three_center.reshape(listed, columns)
    limit = 24 + 3 * max(nob - 2, 0)

    def call(kernel, outs, scratch, flops, *arguments, **options):
        shapes = [jax.ShapeDtypeStruct(shape, kind) for shape, kind in outs]
        size = sum(4 * math.prod(x.shape) for x in arguments)

        def here(*refs):
            kernel([lax.axis_index(axis) for axis in ("orb", "tau", "sub", "aux")], *refs, **options)

        return pl.pallas_call(
            here,
            out_shape=shapes,
            in_specs=[VMEM] * len(arguments),
            out_specs=[VMEM] * len(shapes),
            scratch_shapes=[pltpu.VMEM(shape, kind) for shape, kind in scratch],
            compiler_params=pltpu.CompilerParams(vmem_limit_bytes=limit * MIB),
            cost_estimate=pl.CostEstimate(flops=flops, bytes_accessed=size, transcendentals=0),
            name=kernel.__name__,
        )(*arguments)

    tensors = [lax.ppermute(tensor, "orb", ring(nob, shift)) for shift in range(1, nob)]
    mine, again = call(
        prepare, [((share, rows_aux, listed), F32)] * 2, [((columns, listed), F32)], 0, tensor, share=share
    )
    plan = shifts_of(naux)
    swap = ring(nsub, 1)
    small = jnp.concatenate(
        [
            occupied_green,
            virtual_green,
            jnp.pad(block_list.astype(F32), ((0, LIST_ROWS - 1), (0, norb - slots))),
        ]
    )
    near = jnp.stack([small] + [lax.ppermute(small, "tau", ring(nt, shift)) for shift in range(1, nt)])
    groups = 2 * nt
    work = 6 * groups * share * columns * listed * 3
    rows = groups * rows_aux
    depth = share * listed
    options = dict(slots=slots, width=width, share=share)
    acc, token = call(
        first,
        [((groups, rows_aux // 2 * share, 2 * listed), F32), ((8, 128), F32)],
        [((groups * rows_aux // 2 * share, 2 * width), F32)],
        0,
        near,
        tensor,
        **options,
    )
    mine_other = lax.ppermute(mine, "sub", swap)
    early = [mine_other]
    for _, pairs in plan[:-1]:
        parts = call(
            halve, [((share // 2, rows_aux, listed), F32)] * 2, [], 0, lax.ppermute(mine, "aux", pairs), token
        )
        early += [*parts, *(lax.ppermute(part, "sub", swap) for part in parts)]
    last = lax.ppermute(after(again, lax.ppermute(token, "sub", swap)), "aux", plan[-1][1])
    fars = []
    late_near = after(near, *early)
    for shift in range(1, nob):
        pairs = [(a * nsub + c, b * nsub + (c + 1) % nsub) for a, b in ring(nob, shift) for c in range(nsub)]
        fars.append(lax.ppermute(late_near, ("orb", "sub"), pairs))
    sides, token_late = call(
        second,
        [((2 * rows, depth), BF16), ((8, 128), F32)],
        [((groups * rows_aux // 2 * share, 2 * width), F32)],
        work,
        near,
        acc,
        *tensors,
        *fars,
        *early,
        others=nob - 1,
        **options,
    )
    last = after(last, token_late)
    last_other = lax.ppermute(last, "sub", swap)
    count = 1 + len(plan)
    work = 8 * rows * depth * rows_aux
    wide = nt * rows_aux
    shape = ((rows_aux, 2 * wide), F32)
    scratch = lambda count: ((count, wide, block_aux), F32)
    direct, back, *backs = call(
        meet_own,
        [(((2 * count - 1) * rows_aux, wide), F32), ((rows_aux, wide), F32)] + [shape] * (len(plan) - 1),
        [((2 * (2 * count - 1) * rows_aux, depth), BF16), scratch(1)],
        work * (2 * count - 1) * 2,
        sides,
        mine,
        *early,
        last,
        count=len(plan),
    )
    tensor, *last_back = call(
        meet_back,
        [((2 * rows_aux, depth), BF16), shape],
        [scratch(1)],
        work,
        sides,
        back,
        last_other,
    )
    backs += last_back
    returned = [
        lax.ppermute(back, "aux", [(target, source) for source, target in pairs])
        for back, (_, pairs) in zip(backs, plan)
    ]
    shape = ((nt, block_aux, nauxf), F32)
    (direct,) = call(
        meet_direct, [shape], [scratch(count)], work, sides, direct, tensor, nt=nt, naux=naux
    )
    (partial_chi,) = call(complete, [shape], [], 0, direct, *returned)
    owners = nt * nob * nsub
    received = lax.all_to_all(
        partial_chi.reshape(owners, nt * block_aux // owners, nauxf),
        ("tau", "orb", "sub"),
        split_axis=0,
        concat_axis=0,
        tiled=True,
    )
    return received.sum(axis=0) * (-2.0 / math.sqrt(norb * slots * width))


def solution(mesh):
    sizes = tuple(mesh.shape[axis] for axis in ("tau", "aux", "orb", "sub"))
    in_specs = (
        P("aux", "orb", None, None, "sub"),
        P(("tau", "orb"), None),
        P(("tau", "orb"), None),
        P("orb", None),
    )
    out_specs = P(("tau", "aux", "orb", "sub"), None)
    return jax.shard_map(
        functools.partial(local, sizes=sizes), mesh=mesh, in_specs=in_specs, out_specs=out_specs, check_vma=False
    )
```

```python
import functools
import math

import jax
import jax.numpy as jnp
from jax import lax
from jax.experimental import pallas as pl
from jax.experimental.pallas import tpu as pltpu
from jax.sharding import PartitionSpec as P

VMEM = pl.BlockSpec(memory_space=pltpu.VMEM)
ANY = pl.BlockSpec(memory_space=pl.ANY)
HBM = pl.BlockSpec(memory_space=pltpu.HBM)
F32 = jnp.float32
BF16 = jnp.bfloat16
LIST_ROWS = 8
MIB = 1024 * 1024


def halves(x):
    high = x.astype(BF16)
    return high, (x - high.astype(F32)).astype(BF16)


def dot(a, b):
    return lax.dot_general(a, b, (((1,), (0,)), ((), ())), preferred_element_type=F32)


def dot_nt(a, b):
    return lax.dot_general(a, b, (((1,), (1,)), ((), ())), preferred_element_type=F32)


def ring(count, shift):
    return [((target + shift) % count, target) for target in range(count)]


def prepare(place, tensor, mine, again, turned, *, share):
    some = mine.shape[1]
    turned[...] = tensor[...].T
    start = place[1] * share
    for at in range(share):
        rows = turned[pl.ds(start + at, some, stride=turned.shape[0] // some), :]
        mine[at] = rows
        again[at] = rows


def halve(place, block, token, *outs):
    some = outs[0].shape[0]
    for i, out in enumerate(outs):
        out[...] = block[i * some : (i + 1) * some]


def after(block, *tokens):
    return pl.pallas_call(
        lambda *refs: None,
        out_shape=jax.ShapeDtypeStruct(block.shape, block.dtype),
        in_specs=[ANY] * (1 + len(tokens)),
        out_specs=ANY,
        input_output_aliases={0: 0},
        compiler_params=pltpu.CompilerParams(vmem_limit_bytes=MIB),
        name="after",
    )(block, *tokens)


def shifts_of(naux):
    plan = []
    for shift in range(1, naux // 2 + 1):
        if 2 * shift < naux:
            plan.append([(source, (source + shift) % naux) for source in range(naux)])
        else:
            plan.append([(z, z + shift) if z % 2 == 0 else (z + shift, z) for z in range(shift)])
    return plan


def select(block, list_rows, slots, width):
    parts = []
    for slot in range(slots):
        entry = list_rows[:1, slot : slot + 1]
        chosen = jnp.zeros((block.shape[0], width), F32)
        for j in range(block.shape[1] // width):
            chosen = jnp.where(entry == float(j), block[:, j * width : (j + 1) * width], chosen)
        parts.append(chosen)
    return jnp.concatenate(parts, axis=1)


def mix(place, near, far, tensor, rows, slots, width, share):
    nt = near.shape[0]
    pairs = tensor.shape[1] // (2 * width)
    near_list, far_list = near[0, 2 * width :, :], far[0, 2 * width :, :]
    which = [lax.rem(tau + nt - place[1], nt) for tau in range(nt)]
    left = []
    for kind in range(2):
        for tau in range(nt):
            start = pl.multiple_of(kind * width + place[1] * share, share)
            left.append(select(near[which[tau], pl.ds(start, share), :], far_list, slots, width))
    left_high, left_low = halves(jnp.concatenate(left, axis=0))
    high, low = halves(tensor[...])
    middle = dot(
        jnp.concatenate([left_high, left_high, left_low], axis=1), jnp.concatenate([high, low, high], axis=0)
    )
    for group in range(2 * nt):
        for at in range(pairs):
            rows[(group * pairs + at) * share : (group * pairs + at + 1) * share, :] = middle[
                group * share : (group + 1) * share, 2 * width * at : 2 * width * (at + 1)
            ]
    results = []
    for group in range(2 * nt):
        kind, tau = group // nt, group % nt
        right = select(far[which[tau], (1 - kind) * width : (2 - kind) * width, :], near_list, slots, width)
        zero = jnp.zeros_like(right)
        right_high, right_low = halves(
            jnp.concatenate([jnp.concatenate([right, zero], axis=1), jnp.concatenate([zero, right], axis=1)], axis=0)
        )

        rows_high, rows_low = halves(
            jnp.concatenate(
                [rows[pl.ds(group * pairs * share + at, pairs, stride=share), :] for at in range(share)], axis=0
            )
        )
        results.append(
            dot(
                jnp.concatenate([rows_high, rows_high, rows_low], axis=1),
                jnp.concatenate([right_high, right_low, right_high], axis=0),
            )
        )
    return results


def first(place, near, tensor, acc, token, rows, *, slots, width, share):
    token[...] = jnp.zeros_like(token)
    for group, result in enumerate(mix(place, near, near, tensor, rows, slots, width, share)):
        acc[group] = result


def second(place, near, acc, *refs, slots, width, share, others):
    refs, (sides, token, rows) = refs[: 2 * others], refs[-3:]
    tensors, fars = refs[: len(refs) // 2], refs[len(refs) // 2 :]
    token[...] = jnp.zeros_like(token)
    listed = slots * width
    groups, tall, _ = acc.shape
    pairs = tall // share
    total = [acc[group] for group in range(groups)]
    for tensor, far in zip(tensors, fars):
        term = mix(place, near, far, tensor, rows, slots, width, share)
        total = [x + y for x, y in zip(total, term)]
    for group in range(groups):
        height = groups * pairs
        high, low = halves(total[group])
        for odd in range(2):
            row = (2 * (group % (groups // 2)) + odd) * pairs + 2 * height * (group * 2 // groups)
            for at in range(share):
                for part, array in enumerate((high, low)):
                    sides[
                        part * height + row : part * height + row + pairs, at * listed : (at + 1) * listed
                    ] = array[at * pairs : (at + 1) * pairs, odd * listed : (odd + 1) * listed]


def relay(pieces, tensor):
    for i, parts in enumerate(pieces):
        at = 0
        for part in parts:
            per, half, listed = part.shape
            for inner in range(per):
                high, low = halves(part[inner])
                tensor[2 * i * half : (2 * i + 1) * half, at * listed : (at + 1) * listed] = high
                tensor[(2 * i + 1) * half : 2 * (i + 1) * half, at * listed : (at + 1) * listed] = low
                at += 1


def products(tensor, side, half):
    all_parts = dot_nt(tensor, side)
    width = side.shape[0] // 2
    rows = []
    for i in range(tensor.shape[0] // (2 * half)):
        block = all_parts[2 * i * half : (2 * i + 1) * half] + all_parts[(2 * i + 1) * half : 2 * (i + 1) * half]
        rows.append(block[:, :width] + block[:, width:])
    return jnp.concatenate(rows, axis=0)


def unfold(block, ordered, i):
    turned = block.T
    pairs = block.shape[0] // 4
    for group in range(turned.shape[0] // (2 * pairs)):
        for odd in range(2):
            at = (2 * group + odd) * pairs
            ordered[i, pl.ds(2 * group * pairs + odd, pairs, stride=2), :] = turned[at : at + pairs]


def at_sub(place, x, axis):
    zero = jnp.zeros_like(x)
    return by_sub(place, x, zero, axis)


def by_sub(place, own, other, axis):
    return jnp.where(
        place[2] == 0, jnp.concatenate([own, other], axis=axis), jnp.concatenate([other, own], axis=axis)
    )


def fold(place, own, other, ordered):
    unfold(by_sub(place, own, other, 0), ordered, 0)
    back = ordered[0].T
    half = own.shape[0]
    return jnp.concatenate([back[:half], back[half:]], axis=1)


def meet_own(place, sides, *refs, count):
    refs, (direct, back, *backs, tensor, ordered) = refs[: 4 * count - 1], refs[4 * count - 1 :]
    pieces = [refs[:1], refs[1:2]] + [refs[i : i + 2] for i in range(2, 4 * count - 2, 2)] + [refs[-1:]]
    half = refs[0].shape[1]
    rows = sides.shape[0] // 2
    relay(pieces, tensor)
    direct[...] = products(tensor[...], sides[:rows, :], half)
    rest = products(tensor[4 * half :, :], sides[rows:, :], half)
    for i, back_ref in enumerate(backs):
        back_ref[...] = fold(
            place, rest[2 * i * half : (2 * i + 1) * half], rest[(2 * i + 1) * half : 2 * (i + 1) * half], ordered
        )
    back[...] = rest[-half:]


def meet_back(place, sides, own, piece, tensor, back_ref, ordered):
    half = piece.shape[1]
    relay([[piece]], tensor)
    other = products(tensor[...], sides[sides.shape[0] // 2 :, :], half)
    back_ref[...] = fold(place, own[...], other, ordered)


def meet_direct(place, sides, own, tensor, out_ref, ordered, *, nt, naux):
    count = ordered.shape[0]
    block = ordered.shape[2]
    half = block // 2
    other = products(tensor[...], sides[: sides.shape[0] // 2, :], half)
    for i in range(count):
        first_half = own[i * block : i * block + half, :]
        second_half = own[i * block + half : (i + 1) * block, :] if i < count - 1 else other
        unfold(by_sub(place, first_half, second_half, 0), ordered, i)
    for tau in range(nt):
        here = [jnp.zeros((half, block), F32)] * naux
        for shift in range(count):
            here[(naux - shift) % naux] = ordered[shift, tau * half : (tau + 1) * half, :]
        out_ref[tau] = at_sub(place, jnp.concatenate(here, axis=1), 0)


def add(place, early, back, out_ref, *, shift, last):
    nt, block, wide = early.shape
    half = block // 2
    for tau in range(nt):
        upper = back[:, tau * half : (tau + 1) * half]
        lower = back[:, (nt + tau) * half : (nt + tau + 1) * half]
        parts = [jnp.zeros((block, block), F32)] * (wide // block)
        parts[shift] = at_sub(place, jnp.concatenate([upper, lower], axis=0), 1)
        total = early[tau] + jnp.concatenate(parts, axis=1)
        out_ref[tau] = pltpu.roll(total, place[3] * block, 1) if last else total


def local(three_center, occupied_green, virtual_green, block_list, sizes):
    nt, naux, nob, nsub = sizes
    slots = three_center.shape[2]
    width = three_center.shape[3]
    columns = three_center.shape[4]
    rows_aux = columns // width
    block_aux = rows_aux * nsub
    norb = occupied_green.shape[1]
    listed = slots * width
    share = width // nt
    nauxf = naux * block_aux
    tensor = three_center.reshape(listed, columns)
    limit = 24 + 3 * max(nob - 2, 0)

    def call(kernel, outs, scratch, flops, *arguments, **options):
        shapes = [jax.ShapeDtypeStruct(shape, kind) for shape, kind in outs]
        size = sum(4 * math.prod(x.shape) for x in arguments)

        def here(*refs):
            kernel([lax.axis_index(axis) for axis in ("orb", "tau", "sub", "aux")], *refs, **options)

        return pl.pallas_call(
            here,
            out_shape=shapes,
            in_specs=[VMEM] * len(arguments),
            out_specs=[VMEM] * len(shapes),
            scratch_shapes=[pltpu.VMEM(shape, kind) for shape, kind in scratch],
            compiler_params=pltpu.CompilerParams(vmem_limit_bytes=limit * MIB),
            cost_estimate=pl.CostEstimate(flops=flops, bytes_accessed=size, transcendentals=0),
            name=kernel.__name__,
        )(*arguments)

    tensors = [lax.ppermute(tensor, "orb", ring(nob, shift)) for shift in range(1, nob)]
    mine, again = call(
        prepare, [((share, rows_aux, listed), F32)] * 2, [((columns, listed), F32)], 0, tensor, share=share
    )
    plan = shifts_of(naux)
    swap = ring(nsub, 1)
    small = jnp.concatenate(
        [
            occupied_green,
            virtual_green,
            jnp.pad(block_list.astype(F32), ((0, LIST_ROWS - 1), (0, norb - slots))),
        ]
    )
    near = jnp.stack([small] + [lax.ppermute(small, "tau", ring(nt, shift)) for shift in range(1, nt)])
    groups = 2 * nt
    work = 6 * groups * share * columns * listed * 3
    rows = groups * rows_aux
    depth = share * listed
    options = dict(slots=slots, width=width, share=share)
    acc, token = call(
        first,
        [((groups, rows_aux // 2 * share, 2 * listed), F32), ((8, 128), F32)],
        [((groups * rows_aux // 2 * share, 2 * width), F32)],
        0,
        near,
        tensor,
        **options,
    )
    mine_other = lax.ppermute(mine, "sub", swap)
    early = [mine_other]
    for pairs in plan[:-1]:
        parts = call(
            halve, [((share // 2, rows_aux, listed), F32)] * 2, [], 0, lax.ppermute(mine, "aux", pairs), token
        )
        early += [*parts, *(lax.ppermute(part, "sub", swap) for part in parts)]
    last = lax.ppermute(after(again, lax.ppermute(token, "sub", swap)), "aux", plan[-1])
    fars = []
    late_near = after(near, *early)
    for shift in range(1, nob):
        pairs = [(a * nsub + c, b * nsub + (c + 1) % nsub) for a, b in ring(nob, shift) for c in range(nsub)]
        fars.append(lax.ppermute(late_near, ("orb", "sub"), pairs))
    sides, token_late = call(
        second,
        [((2 * rows, depth), BF16), ((8, 128), F32)],
        [((groups * rows_aux // 2 * share, 2 * width), F32)],
        work,
        near,
        acc,
        *tensors,
        *fars,
        *early,
        others=nob - 1,
        **options,
    )
    last = after(last, token_late)
    last_other = lax.ppermute(last, "sub", swap)
    count = 1 + len(plan)
    work = 8 * rows * depth * rows_aux
    wide = nt * rows_aux
    shape = ((rows_aux, 2 * wide), F32)
    scratch = lambda count: ((count, wide, block_aux), F32)
    direct, back, *backs = call(
        meet_own,
        [(((2 * count - 1) * rows_aux, wide), F32), ((rows_aux, wide), F32)] + [shape] * (len(plan) - 1),
        [((2 * (2 * count - 1) * rows_aux, depth), BF16), scratch(1)],
        work * (2 * count - 1) * 2,
        sides,
        mine,
        *early,
        last,
        count=len(plan),
    )
    tensor, *last_back = call(
        meet_back,
        [((2 * rows_aux, depth), BF16), shape],
        [scratch(1)],
        work,
        sides,
        back,
        last_other,
    )
    backs += last_back
    backs[:-1] = [after(back, backs[-1]) for back in backs[:-1]]
    returned = [
        lax.ppermute(back, "aux", [(target, source) for source, target in pairs]) for back, pairs in zip(backs, plan)
    ]
    shape = ((nt, block_aux, nauxf), F32)
    (direct,) = call(
        meet_direct, [shape], [scratch(count)], work, sides, direct, tensor, nt=nt, naux=naux
    )
    partial_chi = direct
    for i in range(len(plan), 0, -1):
        (partial_chi,) = call(add, [shape], [], 0, partial_chi, returned[i - 1], shift=i, last=i == 1)
    owners = nt * nob * nsub
    received = lax.all_to_all(
        partial_chi.reshape(owners, nt * block_aux // owners, nauxf),
        ("tau", "orb", "sub"),
        split_axis=0,
        concat_axis=0,
        tiled=True,
    )
    return received.sum(axis=0) * (-2.0 / math.sqrt(norb * slots * width))


def solution(mesh):
    sizes = tuple(mesh.shape[axis] for axis in ("tau", "aux", "orb", "sub"))
    in_specs = (
        P("aux", "orb", None, None, "sub"),
        P(("tau", "orb"), None),
        P(("tau", "orb"), None),
        P("orb", None),
    )
    out_specs = P(("tau", "aux", "orb", "sub"), None)
    return jax.shard_map(
        functools.partial(local, sizes=sizes), mesh=mesh, in_specs=in_specs, out_specs=out_specs, check_vma=False
    )
```

```python
import functools
import math

import jax
import jax.numpy as jnp
from jax import lax
from jax.experimental import pallas as pl
from jax.experimental.pallas import tpu as pltpu
from jax.sharding import PartitionSpec as P

VMEM = pl.BlockSpec(memory_space=pltpu.VMEM)
ANY = pl.BlockSpec(memory_space=pl.ANY)
HBM = pl.BlockSpec(memory_space=pltpu.HBM)
F32 = jnp.float32
BF16 = jnp.bfloat16
LIST_ROWS = 8
MIB = 1024 * 1024


def halves(x):
    high = x.astype(BF16)
    return high, (x - high.astype(F32)).astype(BF16)


def dot(a, b):
    return lax.dot_general(a, b, (((1,), (0,)), ((), ())), preferred_element_type=F32)


def dot_nt(a, b):
    return lax.dot_general(a, b, (((1,), (1,)), ((), ())), preferred_element_type=F32)


def ring(count, shift):
    return [((target + shift) % count, target) for target in range(count)]


def prepare(place, tensor, mine, again, turned, *, share):
    some = mine.shape[1]
    turned[...] = tensor[...].T
    start = place[1] * share
    for at in range(share):
        rows = turned[pl.ds(start + at, some, stride=turned.shape[0] // some), :]
        mine[at] = rows
        again[at] = rows


def halve(place, block, token, *outs):
    some = outs[0].shape[0]
    for i, out in enumerate(outs):
        out[...] = block[i * some : (i + 1) * some]


def after(block, *tokens):
    return pl.pallas_call(
        lambda *refs: None,
        out_shape=jax.ShapeDtypeStruct(block.shape, block.dtype),
        in_specs=[ANY] * (1 + len(tokens)),
        out_specs=ANY,
        input_output_aliases={0: 0},
        compiler_params=pltpu.CompilerParams(vmem_limit_bytes=MIB),
        name="after",
    )(block, *tokens)


def shifts_of(naux):
    plan = []
    for shift in range(1, naux // 2 + 1):
        if 2 * shift < naux:
            plan.append([(source, (source + shift) % naux) for source in range(naux)])
        else:
            plan.append([(z, z + shift) if z % 2 else (z + shift, z) for z in range(shift)])
    return plan


def select(block, list_rows, slots, width):
    parts = []
    for slot in range(slots):
        entry = list_rows[:1, slot : slot + 1]
        chosen = jnp.zeros((block.shape[0], width), F32)
        for j in range(block.shape[1] // width):
            chosen = jnp.where(entry == float(j), block[:, j * width : (j + 1) * width], chosen)
        parts.append(chosen)
    return jnp.concatenate(parts, axis=1)


def mix(place, near, far, tensor, rows, slots, width, share):
    nt = near.shape[0]
    pairs = tensor.shape[1] // (2 * width)
    near_list, far_list = near[0, 2 * width :, :], far[0, 2 * width :, :]
    which = [lax.rem(tau + nt - place[1], nt) for tau in range(nt)]
    left = []
    for kind in range(2):
        for tau in range(nt):
            start = pl.multiple_of(kind * width + place[1] * share, share)
            left.append(select(near[which[tau], pl.ds(start, share), :], far_list, slots, width))
    left_high, left_low = halves(jnp.concatenate(left, axis=0))
    high, low = halves(tensor[...])
    middle = dot(
        jnp.concatenate([left_high, left_high, left_low], axis=1), jnp.concatenate([high, low, high], axis=0)
    )
    for group in range(2 * nt):
        for at in range(pairs):
            rows[(group * pairs + at) * share : (group * pairs + at + 1) * share, :] = middle[
                group * share : (group + 1) * share, 2 * width * at : 2 * width * (at + 1)
            ]
    results = []
    for group in range(2 * nt):
        kind, tau = group // nt, group % nt
        right = select(far[which[tau], (1 - kind) * width : (2 - kind) * width, :], near_list, slots, width)
        zero = jnp.zeros_like(right)
        right_high, right_low = halves(
            jnp.concatenate([jnp.concatenate([right, zero], axis=1), jnp.concatenate([zero, right], axis=1)], axis=0)
        )

        rows_high, rows_low = halves(
            jnp.concatenate(
                [rows[pl.ds(group * pairs * share + at, pairs, stride=share), :] for at in range(share)], axis=0
            )
        )
        results.append(
            dot(
                jnp.concatenate([rows_high, rows_high, rows_low], axis=1),
                jnp.concatenate([right_high, right_low, right_high], axis=0),
            )
        )
    return results


def first(place, near, tensor, acc, token, rows, *, slots, width, share):
    token[...] = jnp.zeros_like(token)
    for group, result in enumerate(mix(place, near, near, tensor, rows, slots, width, share)):
        acc[group] = result


def second(place, near, acc, *refs, slots, width, share, others):
    refs, (sides, token, rows) = refs[: 2 * others], refs[-3:]
    tensors, fars = refs[: len(refs) // 2], refs[len(refs) // 2 :]
    token[...] = jnp.zeros_like(token)
    listed = slots * width
    groups, tall, _ = acc.shape
    pairs = tall // share
    total = [acc[group] for group in range(groups)]
    for tensor, far in zip(tensors, fars):
        term = mix(place, near, far, tensor, rows, slots, width, share)
        total = [x + y for x, y in zip(total, term)]
    for group in range(groups):
        height = groups * pairs
        high, low = halves(total[group])
        for odd in range(2):
            row = (2 * (group % (groups // 2)) + odd) * pairs + 2 * height * (group * 2 // groups)
            for at in range(share):
                for part, array in enumerate((high, low)):
                    sides[
                        part * height + row : part * height + row + pairs, at * listed : (at + 1) * listed
                    ] = array[at * pairs : (at + 1) * pairs, odd * listed : (odd + 1) * listed]


def relay(pieces, tensor):
    for i, parts in enumerate(pieces):
        at = 0
        for part in parts:
            per, half, listed = part.shape
            for inner in range(per):
                high, low = halves(part[inner])
                tensor[2 * i * half : (2 * i + 1) * half, at * listed : (at + 1) * listed] = high
                tensor[(2 * i + 1) * half : 2 * (i + 1) * half, at * listed : (at + 1) * listed] = low
                at += 1


def products(tensor, side, half):
    all_parts = dot_nt(tensor, side)
    width = side.shape[0] // 2
    rows = []
    for i in range(tensor.shape[0] // (2 * half)):
        block = all_parts[2 * i * half : (2 * i + 1) * half] + all_parts[(2 * i + 1) * half : 2 * (i + 1) * half]
        rows.append(block[:, :width] + block[:, width:])
    return jnp.concatenate(rows, axis=0)


def unfold(block, ordered, i):
    turned = block.T
    pairs = block.shape[0] // 4
    for group in range(turned.shape[0] // (2 * pairs)):
        for odd in range(2):
            at = (2 * group + odd) * pairs
            ordered[i, pl.ds(2 * group * pairs + odd, pairs, stride=2), :] = turned[at : at + pairs]


def at_sub(place, x, axis):
    zero = jnp.zeros_like(x)
    return by_sub(place, x, zero, axis)


def by_sub(place, own, other, axis):
    return jnp.where(
        place[2] == 0, jnp.concatenate([own, other], axis=axis), jnp.concatenate([other, own], axis=axis)
    )


def fold(place, own, other, ordered):
    unfold(by_sub(place, own, other, 0), ordered, 0)
    back = ordered[0].T
    half = own.shape[0]
    return jnp.concatenate([back[:half], back[half:]], axis=1)


def meet_own(place, sides, *refs, count):
    refs, (direct, back, *backs, tensor, ordered) = refs[: 4 * count - 1], refs[4 * count - 1 :]
    pieces = [refs[:1], refs[1:2]] + [refs[i : i + 2] for i in range(2, 4 * count - 2, 2)] + [refs[-1:]]
    half = refs[0].shape[1]
    rows = sides.shape[0] // 2
    relay(pieces, tensor)
    direct[...] = products(tensor[...], sides[:rows, :], half)
    rest = products(tensor[4 * half :, :], sides[rows:, :], half)
    for i, back_ref in enumerate(backs):
        back_ref[...] = fold(
            place, rest[2 * i * half : (2 * i + 1) * half], rest[(2 * i + 1) * half : 2 * (i + 1) * half], ordered
        )
    back[...] = rest[-half:]


def meet_back(place, sides, own, piece, tensor, back_ref, ordered):
    half = piece.shape[1]
    relay([[piece]], tensor)
    other = products(tensor[...], sides[sides.shape[0] // 2 :, :], half)
    back_ref[...] = fold(place, own[...], other, ordered)


def meet_direct(place, sides, own, tensor, out_ref, ordered, *, nt, naux):
    count = ordered.shape[0]
    block = ordered.shape[2]
    half = block // 2
    other = products(tensor[...], sides[: sides.shape[0] // 2, :], half)
    for i in range(count):
        first_half = own[i * block : i * block + half, :]
        second_half = own[i * block + half : (i + 1) * block, :] if i < count - 1 else other
        unfold(by_sub(place, first_half, second_half, 0), ordered, i)
    for tau in range(nt):
        here = [jnp.zeros((half, block), F32)] * naux
        for shift in range(count):
            here[(naux - shift) % naux] = ordered[shift, tau * half : (tau + 1) * half, :]
        out_ref[tau] = at_sub(place, jnp.concatenate(here, axis=1), 0)


def complete(place, early, *refs):
    backs, out_ref = refs[:-1], refs[-1]
    nt, block, wide = early.shape
    naux = wide // block
    half = block // 2
    for tau in range(nt):
        parts = [jnp.zeros((block, block), F32)] * naux
        for shift, ref in enumerate(backs, 1):
            upper = ref[:, tau * half : (tau + 1) * half]
            lower = ref[:, (nt + tau) * half : (nt + tau + 1) * half]
            parts[shift] = at_sub(place, jnp.concatenate([upper, lower], axis=0), 1)
        total = early[tau] + jnp.concatenate(parts, axis=1)
        out_ref[tau] = pltpu.roll(total, place[3] * block, 1)


def local(three_center, occupied_green, virtual_green, block_list, sizes):
    nt, naux, nob, nsub = sizes
    slots = three_center.shape[2]
    width = three_center.shape[3]
    columns = three_center.shape[4]
    rows_aux = columns // width
    block_aux = rows_aux * nsub
    norb = occupied_green.shape[1]
    listed = slots * width
    share = width // nt
    nauxf = naux * block_aux
    tensor = three_center.reshape(listed, columns)
    limit = 24 + 3 * max(nob - 2, 0)

    def call(kernel, outs, scratch, flops, *arguments, **options):
        shapes = [jax.ShapeDtypeStruct(shape, kind) for shape, kind in outs]
        size = sum(4 * math.prod(x.shape) for x in arguments)

        def here(*refs):
            kernel([lax.axis_index(axis) for axis in ("orb", "tau", "sub", "aux")], *refs, **options)

        return pl.pallas_call(
            here,
            out_shape=shapes,
            in_specs=[VMEM] * len(arguments),
            out_specs=[VMEM] * len(shapes),
            scratch_shapes=[pltpu.VMEM(shape, kind) for shape, kind in scratch],
            compiler_params=pltpu.CompilerParams(vmem_limit_bytes=limit * MIB),
            cost_estimate=pl.CostEstimate(flops=flops, bytes_accessed=size, transcendentals=0),
            name=kernel.__name__,
        )(*arguments)

    tensors = [lax.ppermute(tensor, "orb", ring(nob, shift)) for shift in range(1, nob)]
    mine, again = call(
        prepare, [((share, rows_aux, listed), F32)] * 2, [((columns, listed), F32)], 0, tensor, share=share
    )
    plan = shifts_of(naux)
    swap = ring(nsub, 1)
    small = jnp.concatenate(
        [
            occupied_green,
            virtual_green,
            jnp.pad(block_list.astype(F32), ((0, LIST_ROWS - 1), (0, norb - slots))),
        ]
    )
    near = jnp.stack([small] + [lax.ppermute(small, "tau", ring(nt, shift)) for shift in range(1, nt)])
    groups = 2 * nt
    work = 6 * groups * share * columns * listed * 3
    rows = groups * rows_aux
    depth = share * listed
    options = dict(slots=slots, width=width, share=share)
    acc, token = call(
        first,
        [((groups, rows_aux // 2 * share, 2 * listed), F32), ((8, 128), F32)],
        [((groups * rows_aux // 2 * share, 2 * width), F32)],
        0,
        near,
        tensor,
        **options,
    )
    mine_other = lax.ppermute(mine, "sub", swap)
    early = [mine_other]
    for pairs in plan[:-1]:
        parts = call(
            halve, [((share // 2, rows_aux, listed), F32)] * 2, [], 0, lax.ppermute(mine, "aux", pairs), token
        )
        early += [*parts, *(lax.ppermute(part, "sub", swap) for part in parts)]
    last = lax.ppermute(after(again, lax.ppermute(token, "sub", swap)), "aux", plan[-1])
    fars = []
    late_near = after(near, *early)
    for shift in range(1, nob):
        pairs = [(a * nsub + c, b * nsub + (c + 1) % nsub) for a, b in ring(nob, shift) for c in range(nsub)]
        fars.append(lax.ppermute(late_near, ("orb", "sub"), pairs))
    sides, token_late = call(
        second,
        [((2 * rows, depth), BF16), ((8, 128), F32)],
        [((groups * rows_aux // 2 * share, 2 * width), F32)],
        work,
        near,
        acc,
        *tensors,
        *fars,
        *early,
        others=nob - 1,
        **options,
    )
    last = after(last, token_late)
    last_other = lax.ppermute(last, "sub", swap)
    count = 1 + len(plan)
    work = 8 * rows * depth * rows_aux
    wide = nt * rows_aux
    shape = ((rows_aux, 2 * wide), F32)
    scratch = lambda count: ((count, wide, block_aux), F32)
    direct, back, *backs = call(
        meet_own,
        [(((2 * count - 1) * rows_aux, wide), F32), ((rows_aux, wide), F32)] + [shape] * (len(plan) - 1),
        [((2 * (2 * count - 1) * rows_aux, depth), BF16), scratch(1)],
        work * (2 * count - 1) * 2,
        sides,
        mine,
        *early,
        last,
        count=len(plan),
    )
    tensor, *last_back = call(
        meet_back,
        [((2 * rows_aux, depth), BF16), shape],
        [scratch(1)],
        work,
        sides,
        back,
        last_other,
    )
    backs += last_back
    returned = [
        lax.ppermute(back, "aux", [(target, source) for source, target in pairs]) for back, pairs in zip(backs, plan)
    ]
    shape = ((nt, block_aux, nauxf), F32)
    (direct,) = call(
        meet_direct, [shape], [scratch(count)], work, sides, direct, tensor, nt=nt, naux=naux
    )
    (partial_chi,) = call(complete, [shape], [], 0, direct, *returned)
    owners = nt * nob * nsub
    received = lax.all_to_all(
        partial_chi.reshape(owners, nt * block_aux // owners, nauxf),
        ("tau", "orb", "sub"),
        split_axis=0,
        concat_axis=0,
        tiled=True,
    )
    return received.sum(axis=0) * (-2.0 / math.sqrt(norb * slots * width))


def solution(mesh):
    sizes = tuple(mesh.shape[axis] for axis in ("tau", "aux", "orb", "sub"))
    in_specs = (
        P("aux", "orb", None, None, "sub"),
        P(("tau", "orb"), None),
        P(("tau", "orb"), None),
        P("orb", None),
    )
    out_specs = P(("tau", "aux", "orb", "sub"), None)
    return jax.shard_map(
        functools.partial(local, sizes=sizes), mesh=mesh, in_specs=in_specs, out_specs=out_specs, check_vma=False
    )
```

```python
import functools
import math

import jax
import jax.numpy as jnp
from jax import lax
from jax.experimental import pallas as pl
from jax.experimental.pallas import tpu as pltpu
from jax.sharding import PartitionSpec as P

VMEM = pl.BlockSpec(memory_space=pltpu.VMEM)
ANY = pl.BlockSpec(memory_space=pl.ANY)
HBM = pl.BlockSpec(memory_space=pltpu.HBM)
F32 = jnp.float32
BF16 = jnp.bfloat16
LIST_ROWS = 8
MIB = 1024 * 1024


def halves(x):
    high = x.astype(BF16)
    return high, (x - high.astype(F32)).astype(BF16)


def dot(a, b):
    return lax.dot_general(a, b, (((1,), (0,)), ((), ())), preferred_element_type=F32)


def dot_nt(a, b):
    return lax.dot_general(a, b, (((1,), (1,)), ((), ())), preferred_element_type=F32)


def ring(count, shift):
    return [((target + shift) % count, target) for target in range(count)]


def prepare(place, tensor, mine, again, turned, *, share):
    some = mine.shape[1]
    turned[...] = tensor[...].T
    start = place[1] * share
    for at in range(share):
        rows = turned[pl.ds(start + at, some, stride=turned.shape[0] // some), :]
        mine[at] = rows
        again[at] = rows


def halve(place, block, token, *outs):
    some = outs[0].shape[0]
    for i, out in enumerate(outs):
        out[...] = block[i * some : (i + 1) * some]


def after(block, *tokens):
    return pl.pallas_call(
        lambda *refs: None,
        out_shape=jax.ShapeDtypeStruct(block.shape, block.dtype),
        in_specs=[ANY] * (1 + len(tokens)),
        out_specs=ANY,
        input_output_aliases={0: 0},
        compiler_params=pltpu.CompilerParams(vmem_limit_bytes=MIB),
        name="after",
    )(block, *tokens)


def shifts_of(naux):
    plan = []
    for shift in range(1, naux // 2 + 1):
        if 2 * shift < naux:
            plan.append([(source, (source + shift) % naux) for source in range(naux)])
        else:
            plan.append([(z, z + shift) if z % 2 else (z + shift, z) for z in range(shift)])
    return plan


def select(block, list_rows, slots, width):
    parts = []
    for slot in range(slots):
        entry = list_rows[:1, slot : slot + 1]
        chosen = jnp.zeros((block.shape[0], width), F32)
        for j in range(block.shape[1] // width):
            chosen = jnp.where(entry == float(j), block[:, j * width : (j + 1) * width], chosen)
        parts.append(chosen)
    return jnp.concatenate(parts, axis=1)


def mix(place, near, far, tensor, rows, slots, width, share):
    nt = near.shape[0]
    pairs = tensor.shape[1] // (2 * width)
    near_list, far_list = near[0, 2 * width :, :], far[0, 2 * width :, :]
    which = [lax.rem(tau + nt - place[1], nt) for tau in range(nt)]
    left = []
    for kind in range(2):
        for tau in range(nt):
            start = pl.multiple_of(kind * width + place[1] * share, share)
            left.append(select(near[which[tau], pl.ds(start, share), :], far_list, slots, width))
    left_high, left_low = halves(jnp.concatenate(left, axis=0))
    high, low = halves(tensor[...])
    middle = dot(
        jnp.concatenate([left_high, left_high, left_low], axis=1), jnp.concatenate([high, low, high], axis=0)
    )
    for group in range(2 * nt):
        for at in range(pairs):
            rows[(group * pairs + at) * share : (group * pairs + at + 1) * share, :] = middle[
                group * share : (group + 1) * share, 2 * width * at : 2 * width * (at + 1)
            ]
    results = []
    for group in range(2 * nt):
        kind, tau = group // nt, group % nt
        right = select(far[which[tau], (1 - kind) * width : (2 - kind) * width, :], near_list, slots, width)
        zero = jnp.zeros_like(right)
        right_high, right_low = halves(
            jnp.concatenate([jnp.concatenate([right, zero], axis=1), jnp.concatenate([zero, right], axis=1)], axis=0)
        )

        rows_high, rows_low = halves(
            jnp.concatenate(
                [rows[pl.ds(group * pairs * share + at, pairs, stride=share), :] for at in range(share)], axis=0
            )
        )
        results.append(
            dot(
                jnp.concatenate([rows_high, rows_high, rows_low], axis=1),
                jnp.concatenate([right_high, right_low, right_high], axis=0),
            )
        )
    return results


def first(place, near, tensor, acc, token, rows, *, slots, width, share):
    token[...] = jnp.zeros_like(token)
    for group, result in enumerate(mix(place, near, near, tensor, rows, slots, width, share)):
        acc[group] = result


def second(place, near, acc, *refs, slots, width, share, others):
    refs, (sides, token, rows) = refs[: 2 * others], refs[-3:]
    tensors, fars = refs[: len(refs) // 2], refs[len(refs) // 2 :]
    token[...] = jnp.zeros_like(token)
    listed = slots * width
    groups, tall, _ = acc.shape
    pairs = tall // share
    total = [acc[group] for group in range(groups)]
    for tensor, far in zip(tensors, fars):
        term = mix(place, near, far, tensor, rows, slots, width, share)
        total = [x + y for x, y in zip(total, term)]
    for group in range(groups):
        height = groups * pairs
        high, low = halves(total[group])
        for odd in range(2):
            row = (2 * (group % (groups // 2)) + odd) * pairs + 2 * height * (group * 2 // groups)
            for at in range(share):
                for part, array in enumerate((high, low)):
                    sides[
                        part * height + row : part * height + row + pairs, at * listed : (at + 1) * listed
                    ] = array[at * pairs : (at + 1) * pairs, odd * listed : (odd + 1) * listed]


def relay(pieces, tensor):
    for i, parts in enumerate(pieces):
        at = 0
        for part in parts:
            per, half, listed = part.shape
            for inner in range(per):
                high, low = halves(part[inner])
                tensor[2 * i * half : (2 * i + 1) * half, at * listed : (at + 1) * listed] = high
                tensor[(2 * i + 1) * half : 2 * (i + 1) * half, at * listed : (at + 1) * listed] = low
                at += 1


def products(tensor, side, half):
    all_parts = dot_nt(tensor, side)
    width = side.shape[0] // 2
    rows = []
    for i in range(tensor.shape[0] // (2 * half)):
        block = all_parts[2 * i * half : (2 * i + 1) * half] + all_parts[(2 * i + 1) * half : 2 * (i + 1) * half]
        rows.append(block[:, :width] + block[:, width:])
    return jnp.concatenate(rows, axis=0)


def unfold(block, ordered, i):
    turned = block.T
    pairs = block.shape[0] // 4
    for group in range(turned.shape[0] // (2 * pairs)):
        for odd in range(2):
            at = (2 * group + odd) * pairs
            ordered[i, pl.ds(2 * group * pairs + odd, pairs, stride=2), :] = turned[at : at + pairs]


def at_sub(place, x, axis):
    zero = jnp.zeros_like(x)
    return by_sub(place, x, zero, axis)


def by_sub(place, own, other, axis):
    return jnp.where(
        place[2] == 0, jnp.concatenate([own, other], axis=axis), jnp.concatenate([other, own], axis=axis)
    )


def fold(place, own, other, ordered):
    unfold(by_sub(place, own, other, 0), ordered, 0)
    back = ordered[0].T
    half = own.shape[0]
    return jnp.concatenate([back[:half], back[half:]], axis=1)


def meet_own(place, sides, *refs, count):
    refs, (tensor, back, *backs, ordered) = refs[: 4 * count - 3], refs[4 * count - 3 :]
    pieces = [refs[i : i + 2] for i in range(0, 4 * count - 4, 2)] + [refs[-1:]]
    half = refs[0].shape[1]
    relay(pieces, tensor)
    rest = products(tensor[...], sides[sides.shape[0] // 2 :, :], half)
    for i, back_ref in enumerate(backs):
        back_ref[...] = fold(
            place, rest[2 * i * half : (2 * i + 1) * half], rest[(2 * i + 1) * half : 2 * (i + 1) * half], ordered
        )
    back[...] = rest[-half:]


def meet_back(place, sides, own, piece, tensor, back_ref, ordered):
    half = piece.shape[1]
    relay([[piece]], tensor)
    other = products(tensor[...], sides[sides.shape[0] // 2 :, :], half)
    back_ref[...] = fold(place, own[...], other, ordered)


def meet_direct(place, sides, mine, mine_other, own, last, out_ref, tensor, ordered, *, nt, naux):
    count = ordered.shape[0]
    block = ordered.shape[2]
    half = block // 2
    side = sides[: sides.shape[0] // 2, :]
    relay([[mine], [mine_other]], tensor)
    tensor[4 * half :, :] = last[...]
    some = products(tensor[...], side, half)
    own = jnp.concatenate([some[:block], products(own[...], side, half)], axis=0)
    other = some[block:]
    for i in range(count):
        first_half = own[i * block : i * block + half]
        second_half = own[i * block + half : (i + 1) * block] if i < count - 1 else other
        unfold(by_sub(place, first_half, second_half, 0), ordered, i)
    for tau in range(nt):
        here = [jnp.zeros((half, block), F32)] * naux
        for shift in range(count):
            here[(naux - shift) % naux] = ordered[shift, tau * half : (tau + 1) * half, :]
        out_ref[tau] = at_sub(place, jnp.concatenate(here, axis=1), 0)


def complete(place, early, *refs):
    backs, out_ref = refs[:-1], refs[-1]
    nt, block, wide = early.shape
    naux = wide // block
    half = block // 2
    for tau in range(nt):
        parts = [jnp.zeros((block, block), F32)] * naux
        for shift, ref in enumerate(backs, 1):
            upper = ref[:, tau * half : (tau + 1) * half]
            lower = ref[:, (nt + tau) * half : (nt + tau + 1) * half]
            parts[shift] = at_sub(place, jnp.concatenate([upper, lower], axis=0), 1)
        total = early[tau] + jnp.concatenate(parts, axis=1)
        out_ref[tau] = pltpu.roll(total, place[3] * block, 1)


def local(three_center, occupied_green, virtual_green, block_list, sizes):
    nt, naux, nob, nsub = sizes
    slots = three_center.shape[2]
    width = three_center.shape[3]
    columns = three_center.shape[4]
    rows_aux = columns // width
    block_aux = rows_aux * nsub
    norb = occupied_green.shape[1]
    listed = slots * width
    share = width // nt
    nauxf = naux * block_aux
    tensor = three_center.reshape(listed, columns)
    limit = 24 + 3 * max(nob - 2, 0)

    def call(kernel, outs, scratch, flops, *arguments, **options):
        shapes = [jax.ShapeDtypeStruct(shape, kind) for shape, kind in outs]
        size = sum(4 * math.prod(x.shape) for x in arguments)

        def here(*refs):
            kernel([lax.axis_index(axis) for axis in ("orb", "tau", "sub", "aux")], *refs, **options)

        return pl.pallas_call(
            here,
            out_shape=shapes,
            in_specs=[VMEM] * len(arguments),
            out_specs=[VMEM] * len(shapes),
            scratch_shapes=[pltpu.VMEM(shape, kind) for shape, kind in scratch],
            compiler_params=pltpu.CompilerParams(vmem_limit_bytes=limit * MIB),
            cost_estimate=pl.CostEstimate(flops=flops, bytes_accessed=size, transcendentals=0),
            name=kernel.__name__,
        )(*arguments)

    tensors = [lax.ppermute(tensor, "orb", ring(nob, shift)) for shift in range(1, nob)]
    mine, again = call(
        prepare, [((share, rows_aux, listed), F32)] * 2, [((columns, listed), F32)], 0, tensor, share=share
    )
    plan = shifts_of(naux)
    swap = ring(nsub, 1)
    small = jnp.concatenate(
        [
            occupied_green,
            virtual_green,
            jnp.pad(block_list.astype(F32), ((0, LIST_ROWS - 1), (0, norb - slots))),
        ]
    )
    near = jnp.stack([small] + [lax.ppermute(small, "tau", ring(nt, shift)) for shift in range(1, nt)])
    groups = 2 * nt
    work = 6 * groups * share * columns * listed * 3
    rows = groups * rows_aux
    depth = share * listed
    options = dict(slots=slots, width=width, share=share)
    acc, token = call(
        first,
        [((groups, rows_aux // 2 * share, 2 * listed), F32), ((8, 128), F32)],
        [((groups * rows_aux // 2 * share, 2 * width), F32)],
        0,
        near,
        tensor,
        **options,
    )
    mine_other = lax.ppermute(mine, "sub", swap)
    early = [mine_other]
    for pairs in plan[:-1]:
        parts = call(
            halve, [((share // 2, rows_aux, listed), F32)] * 2, [], 0, lax.ppermute(mine, "aux", pairs), token
        )
        early += [*parts, *(lax.ppermute(part, "sub", swap) for part in parts)]
    last = lax.ppermute(after(again, lax.ppermute(token, "sub", swap)), "aux", plan[-1])
    fars = []
    late_near = after(near, *early)
    for shift in range(1, nob):
        pairs = [(a * nsub + c, b * nsub + (c + 1) % nsub) for a, b in ring(nob, shift) for c in range(nsub)]
        fars.append(lax.ppermute(late_near, ("orb", "sub"), pairs))
    sides, token_late = call(
        second,
        [((2 * rows, depth), BF16), ((8, 128), F32)],
        [((groups * rows_aux // 2 * share, 2 * width), F32)],
        work,
        near,
        acc,
        *tensors,
        *fars,
        *early,
        others=nob - 1,
        **options,
    )
    last = after(last, token_late)
    last_other = lax.ppermute(last, "sub", swap)
    count = 1 + len(plan)
    work = 8 * rows * depth * rows_aux
    wide = nt * rows_aux
    shape = ((rows_aux, 2 * wide), F32)
    scratch = lambda count: ((count, wide, block_aux), F32)
    own_rows = 2 * (2 * count - 3) * rows_aux
    own, back, *backs = call(
        meet_own,
        [((own_rows, depth), BF16), ((rows_aux, wide), F32)] + [shape] * (len(plan) - 1),
        [scratch(1)],
        work * (2 * count - 3),
        sides,
        *early[1:],
        last,
        count=len(plan),
    )
    tensor, *last_back = call(
        meet_back,
        [((2 * rows_aux, depth), BF16), shape],
        [scratch(1)],
        work,
        sides,
        back,
        last_other,
    )
    backs += last_back
    returned = [
        lax.ppermute(back, "aux", [(target, source) for source, target in pairs]) for back, pairs in zip(backs, plan)
    ]
    shape = ((nt, block_aux, nauxf), F32)
    (direct,) = call(
        meet_direct,
        [shape],
        [((6 * rows_aux, depth), BF16), ((count, wide, block_aux), F32)],
        work * (2 * count),
        sides,
        mine,
        mine_other,
        own,
        tensor,
        nt=nt,
        naux=naux,
    )
    (partial_chi,) = call(complete, [shape], [], 0, direct, *returned)
    owners = nt * nob * nsub
    received = lax.all_to_all(
        partial_chi.reshape(owners, nt * block_aux // owners, nauxf),
        ("tau", "orb", "sub"),
        split_axis=0,
        concat_axis=0,
        tiled=True,
    )
    return received.sum(axis=0) * (-2.0 / math.sqrt(norb * slots * width))


def solution(mesh):
    sizes = tuple(mesh.shape[axis] for axis in ("tau", "aux", "orb", "sub"))
    in_specs = (
        P("aux", "orb", None, None, "sub"),
        P(("tau", "orb"), None),
        P(("tau", "orb"), None),
        P("orb", None),
    )
    out_specs = P(("tau", "aux", "orb", "sub"), None)
    return jax.shard_map(
        functools.partial(local, sizes=sizes), mesh=mesh, in_specs=in_specs, out_specs=out_specs, check_vma=False
    )
```

```python
import functools
import math

import jax
import jax.numpy as jnp
from jax import lax
from jax.experimental import pallas as pl
from jax.experimental.pallas import tpu as pltpu
from jax.sharding import PartitionSpec as P

VMEM = pl.BlockSpec(memory_space=pltpu.VMEM)
ANY = pl.BlockSpec(memory_space=pl.ANY)
HBM = pl.BlockSpec(memory_space=pltpu.HBM)
F32 = jnp.float32
BF16 = jnp.bfloat16
LIST_ROWS = 8
MIB = 1024 * 1024


def halves(x):
    high = x.astype(BF16)
    return high, (x - high.astype(F32)).astype(BF16)


def dot(a, b):
    return lax.dot_general(a, b, (((1,), (0,)), ((), ())), preferred_element_type=F32)


def dot_nt(a, b):
    return lax.dot_general(a, b, (((1,), (1,)), ((), ())), preferred_element_type=F32)


def ring(count, shift):
    return [((target + shift) % count, target) for target in range(count)]


def prepare(place, tensor, mine, again, turned, *, share):
    some = mine.shape[1]
    turned[...] = tensor[...].T
    start = place[1] * share
    for at in range(share):
        rows = turned[pl.ds(start + at, some, stride=turned.shape[0] // some), :]
        mine[at] = rows
        again[at] = rows


def halve(place, block, token, *outs):
    some = outs[0].shape[0]
    for i, out in enumerate(outs):
        out[...] = block[i * some : (i + 1) * some]


def after(block, *tokens):
    return pl.pallas_call(
        lambda *refs: None,
        out_shape=jax.ShapeDtypeStruct(block.shape, block.dtype),
        in_specs=[ANY] * (1 + len(tokens)),
        out_specs=ANY,
        input_output_aliases={0: 0},
        compiler_params=pltpu.CompilerParams(vmem_limit_bytes=MIB),
        name="after",
    )(block, *tokens)


def shifts_of(naux):
    plan = []
    for shift in range(1, naux // 2 + 1):
        if 2 * shift < naux:
            plan.append([((target + shift) % naux, target) for target in range(naux)])
        else:
            plan.append([(z, z + shift) if z % 2 else (z + shift, z) for z in range(shift)])
    return plan


def select(block, list_rows, slots, width):
    parts = []
    for slot in range(slots):
        entry = list_rows[:1, slot : slot + 1]
        chosen = jnp.zeros((block.shape[0], width), F32)
        for j in range(block.shape[1] // width):
            chosen = jnp.where(entry == float(j), block[:, j * width : (j + 1) * width], chosen)
        parts.append(chosen)
    return jnp.concatenate(parts, axis=1)


def mix(place, near, far, tensor, rows, slots, width, share):
    nt = near.shape[0]
    pairs = tensor.shape[1] // (2 * width)
    near_list, far_list = near[0, 2 * width :, :], far[0, 2 * width :, :]
    which = [lax.rem(tau + nt - place[1], nt) for tau in range(nt)]
    left = []
    for kind in range(2):
        for tau in range(nt):
            start = pl.multiple_of(kind * width + place[1] * share, share)
            left.append(select(near[which[tau], pl.ds(start, share), :], far_list, slots, width))
    left_high, left_low = halves(jnp.concatenate(left, axis=0))
    high, low = halves(tensor[...])
    middle = dot(
        jnp.concatenate([left_high, left_high, left_low], axis=1), jnp.concatenate([high, low, high], axis=0)
    )
    for group in range(2 * nt):
        for at in range(pairs):
            rows[(group * pairs + at) * share : (group * pairs + at + 1) * share, :] = middle[
                group * share : (group + 1) * share, 2 * width * at : 2 * width * (at + 1)
            ]
    results = []
    for group in range(2 * nt):
        kind, tau = group // nt, group % nt
        right = select(far[which[tau], (1 - kind) * width : (2 - kind) * width, :], near_list, slots, width)
        zero = jnp.zeros_like(right)
        right_high, right_low = halves(
            jnp.concatenate([jnp.concatenate([right, zero], axis=1), jnp.concatenate([zero, right], axis=1)], axis=0)
        )

        rows_high, rows_low = halves(
            jnp.concatenate(
                [rows[pl.ds(group * pairs * share + at, pairs, stride=share), :] for at in range(share)], axis=0
            )
        )
        results.append(
            dot(
                jnp.concatenate([rows_high, rows_high, rows_low], axis=1),
                jnp.concatenate([right_high, right_low, right_high], axis=0),
            )
        )
    return results


def first(place, near, tensor, acc, token, rows, *, slots, width, share):
    token[...] = jnp.zeros_like(token)
    for group, result in enumerate(mix(place, near, near, tensor, rows, slots, width, share)):
        acc[group] = result


def second(place, near, acc, *refs, slots, width, share, others):
    refs, (sides, token, rows) = refs[: 2 * others], refs[-3:]
    tensors, fars = refs[: len(refs) // 2], refs[len(refs) // 2 :]
    token[...] = jnp.zeros_like(token)
    listed = slots * width
    groups, tall, _ = acc.shape
    pairs = tall // share
    total = [acc[group] for group in range(groups)]
    for tensor, far in zip(tensors, fars):
        term = mix(place, near, far, tensor, rows, slots, width, share)
        total = [x + y for x, y in zip(total, term)]
    for group in range(groups):
        height = groups * pairs
        high, low = halves(total[group])
        for odd in range(2):
            row = (2 * (group % (groups // 2)) + odd) * pairs + 2 * height * (group * 2 // groups)
            for at in range(share):
                for part, array in enumerate((high, low)):
                    sides[
                        part * height + row : part * height + row + pairs, at * listed : (at + 1) * listed
                    ] = array[at * pairs : (at + 1) * pairs, odd * listed : (odd + 1) * listed]


def relay(pieces, tensor):
    for i, parts in enumerate(pieces):
        at = 0
        for part in parts:
            per, half, listed = part.shape
            for inner in range(per):
                high, low = halves(part[inner])
                tensor[2 * i * half : (2 * i + 1) * half, at * listed : (at + 1) * listed] = high
                tensor[(2 * i + 1) * half : 2 * (i + 1) * half, at * listed : (at + 1) * listed] = low
                at += 1


def products(tensor, side, half):
    all_parts = dot_nt(tensor, side)
    width = side.shape[0] // 2
    rows = []
    for i in range(tensor.shape[0] // (2 * half)):
        block = all_parts[2 * i * half : (2 * i + 1) * half] + all_parts[(2 * i + 1) * half : 2 * (i + 1) * half]
        rows.append(block[:, :width] + block[:, width:])
    return jnp.concatenate(rows, axis=0)


def unfold(block, ordered, i):
    turned = block.T
    pairs = block.shape[0] // 4
    for group in range(turned.shape[0] // (2 * pairs)):
        for odd in range(2):
            at = (2 * group + odd) * pairs
            ordered[i, pl.ds(2 * group * pairs + odd, pairs, stride=2), :] = turned[at : at + pairs]


def at_sub(place, x, axis):
    zero = jnp.zeros_like(x)
    return by_sub(place, x, zero, axis)


def by_sub(place, own, other, axis):
    return jnp.where(
        place[2] == 0, jnp.concatenate([own, other], axis=axis), jnp.concatenate([other, own], axis=axis)
    )


def fold(place, own, other, ordered):
    unfold(by_sub(place, own, other, 0), ordered, 0)
    back = ordered[0].T
    half = own.shape[0]
    return jnp.concatenate([back[:half], back[half:]], axis=1)


def meet_own(place, sides, *refs, count):
    refs, (tensor, back, *backs, ordered) = refs[: 4 * count - 3], refs[4 * count - 3 :]
    pieces = [refs[i : i + 2] for i in range(0, 4 * count - 4, 2)] + [refs[-1:]]
    half = refs[0].shape[1]
    relay(pieces, tensor)
    rest = products(tensor[...], sides[sides.shape[0] // 2 :, :], half)
    for i, back_ref in enumerate(backs):
        back_ref[...] = fold(
            place, rest[2 * i * half : (2 * i + 1) * half], rest[(2 * i + 1) * half : 2 * (i + 1) * half], ordered
        )
    back[...] = rest[-half:]


def meet_back(place, sides, own, piece, tensor, back_ref, ordered):
    half = piece.shape[1]
    relay([[piece]], tensor)
    other = products(tensor[...], sides[sides.shape[0] // 2 :, :], half)
    back_ref[...] = fold(place, own[...], other, ordered)


def meet_direct(place, sides, mine, mine_other, own, last, out_ref, tensor, ordered, *, nt, naux):
    count = ordered.shape[0]
    block = ordered.shape[2]
    half = block // 2
    side = sides[: sides.shape[0] // 2, :]
    relay([[mine], [mine_other]], tensor)
    tensor[4 * half :, :] = last[...]
    some = products(tensor[...], side, half)
    own = jnp.concatenate([some[:block], products(own[...], side, half)], axis=0)
    other = some[block:]
    for i in range(count):
        first_half = own[i * block : i * block + half]
        second_half = own[i * block + half : (i + 1) * block] if i < count - 1 else other
        unfold(by_sub(place, first_half, second_half, 0), ordered, i)
    for tau in range(nt):
        here = [jnp.zeros((half, block), F32)] * naux
        for shift in range(count):
            here[shift] = ordered[shift, tau * half : (tau + 1) * half, :]
        out_ref[tau] = at_sub(place, jnp.concatenate(here, axis=1), 0)


def complete(place, early, *refs):
    backs, out_ref = refs[:-1], refs[-1]
    nt, block, wide = early.shape
    naux = wide // block
    half = block // 2
    for tau in range(nt):
        parts = [jnp.zeros((block, block), F32)] * naux
        for shift, ref in enumerate(backs, 1):
            upper = ref[:, tau * half : (tau + 1) * half]
            lower = ref[:, (nt + tau) * half : (nt + tau + 1) * half]
            parts[naux - shift] = at_sub(place, jnp.concatenate([upper, lower], axis=0), 1)
        total = early[tau] + jnp.concatenate(parts, axis=1)
        out_ref[tau] = pltpu.roll(total, place[3] * block, 1)


def local(three_center, occupied_green, virtual_green, block_list, sizes):
    nt, naux, nob, nsub = sizes
    slots = three_center.shape[2]
    width = three_center.shape[3]
    columns = three_center.shape[4]
    rows_aux = columns // width
    block_aux = rows_aux * nsub
    norb = occupied_green.shape[1]
    listed = slots * width
    share = width // nt
    nauxf = naux * block_aux
    tensor = three_center.reshape(listed, columns)
    limit = 24 + 3 * max(nob - 2, 0)

    def call(kernel, outs, scratch, flops, *arguments, **options):
        shapes = [jax.ShapeDtypeStruct(shape, kind) for shape, kind in outs]
        size = sum(4 * math.prod(x.shape) for x in arguments)

        def here(*refs):
            kernel([lax.axis_index(axis) for axis in ("orb", "tau", "sub", "aux")], *refs, **options)

        return pl.pallas_call(
            here,
            out_shape=shapes,
            in_specs=[VMEM] * len(arguments),
            out_specs=[VMEM] * len(shapes),
            scratch_shapes=[pltpu.VMEM(shape, kind) for shape, kind in scratch],
            compiler_params=pltpu.CompilerParams(vmem_limit_bytes=limit * MIB),
            cost_estimate=pl.CostEstimate(flops=flops, bytes_accessed=size, transcendentals=0),
            name=kernel.__name__,
        )(*arguments)

    tensors = [lax.ppermute(tensor, "orb", ring(nob, shift)) for shift in range(1, nob)]
    mine, again = call(
        prepare, [((share, rows_aux, listed), F32)] * 2, [((columns, listed), F32)], 0, tensor, share=share
    )
    plan = shifts_of(naux)
    swap = ring(nsub, 1)
    small = jnp.concatenate(
        [
            occupied_green,
            virtual_green,
            jnp.pad(block_list.astype(F32), ((0, LIST_ROWS - 1), (0, norb - slots))),
        ]
    )
    near = jnp.stack([small] + [lax.ppermute(small, "tau", ring(nt, shift)) for shift in range(1, nt)])
    groups = 2 * nt
    work = 6 * groups * share * columns * listed * 3
    rows = groups * rows_aux
    depth = share * listed
    options = dict(slots=slots, width=width, share=share)
    acc, token = call(
        first,
        [((groups, rows_aux // 2 * share, 2 * listed), F32), ((8, 128), F32)],
        [((groups * rows_aux // 2 * share, 2 * width), F32)],
        0,
        near,
        tensor,
        **options,
    )
    mine_other = lax.ppermute(mine, "sub", swap)
    early = [mine_other]
    for pairs in plan[:-1]:
        parts = call(
            halve, [((share // 2, rows_aux, listed), F32)] * 2, [], 0, lax.ppermute(mine, "aux", pairs), token
        )
        early += [*parts, *(lax.ppermute(part, "sub", swap) for part in parts)]
    last = lax.ppermute(after(again, lax.ppermute(token, "sub", swap)), "aux", plan[-1])
    fars = []
    late_near = after(near, *early)
    for shift in range(1, nob):
        pairs = [(a * nsub + c, b * nsub + (c + 1) % nsub) for a, b in ring(nob, shift) for c in range(nsub)]
        fars.append(lax.ppermute(late_near, ("orb", "sub"), pairs))
    sides, token_late = call(
        second,
        [((2 * rows, depth), BF16), ((8, 128), F32)],
        [((groups * rows_aux // 2 * share, 2 * width), F32)],
        work,
        near,
        acc,
        *tensors,
        *fars,
        *early,
        others=nob - 1,
        **options,
    )
    last = after(last, token_late)
    last_other = lax.ppermute(last, "sub", swap)
    count = 1 + len(plan)
    work = 8 * rows * depth * rows_aux
    wide = nt * rows_aux
    shape = ((rows_aux, 2 * wide), F32)
    scratch = lambda count: ((count, wide, block_aux), F32)
    own_rows = 2 * (2 * count - 3) * rows_aux
    own, back, *backs = call(
        meet_own,
        [((own_rows, depth), BF16), ((rows_aux, wide), F32)] + [shape] * (len(plan) - 1),
        [scratch(1)],
        work * (2 * count - 3),
        sides,
        *early[1:],
        last,
        count=len(plan),
    )
    tensor, *last_back = call(
        meet_back,
        [((2 * rows_aux, depth), BF16), shape],
        [scratch(1)],
        work,
        sides,
        back,
        last_other,
    )
    backs += last_back
    returned = [
        lax.ppermute(back, "aux", [(target, source) for source, target in pairs]) for back, pairs in zip(backs, plan)
    ]
    shape = ((nt, block_aux, nauxf), F32)
    (direct,) = call(
        meet_direct,
        [shape],
        [((6 * rows_aux, depth), BF16), ((count, wide, block_aux), F32)],
        work * (2 * count),
        sides,
        mine,
        mine_other,
        own,
        tensor,
        nt=nt,
        naux=naux,
    )
    (partial_chi,) = call(complete, [shape], [], 0, direct, *returned)
    owners = nt * nob * nsub
    received = lax.all_to_all(
        partial_chi.reshape(owners, nt * block_aux // owners, nauxf),
        ("tau", "orb", "sub"),
        split_axis=0,
        concat_axis=0,
        tiled=True,
    )
    return received.sum(axis=0) * (-2.0 / math.sqrt(norb * slots * width))


def solution(mesh):
    sizes = tuple(mesh.shape[axis] for axis in ("tau", "aux", "orb", "sub"))
    in_specs = (
        P("aux", "orb", None, None, "sub"),
        P(("tau", "orb"), None),
        P(("tau", "orb"), None),
        P("orb", None),
    )
    out_specs = P(("tau", "aux", "orb", "sub"), None)
    return jax.shard_map(
        functools.partial(local, sizes=sizes), mesh=mesh, in_specs=in_specs, out_specs=out_specs, check_vma=False
    )
```

```python
import functools
import math

import jax
import jax.numpy as jnp
from jax import lax
from jax.experimental import pallas as pl
from jax.experimental.pallas import tpu as pltpu
from jax.sharding import PartitionSpec as P

VMEM = pl.BlockSpec(memory_space=pltpu.VMEM)
ANY = pl.BlockSpec(memory_space=pl.ANY)
HBM = pl.BlockSpec(memory_space=pltpu.HBM)
F32 = jnp.float32
BF16 = jnp.bfloat16
LIST_ROWS = 8
MIB = 1024 * 1024


def halves(x):
    high = x.astype(BF16)
    return high, (x - high.astype(F32)).astype(BF16)


def dot(a, b):
    return lax.dot_general(a, b, (((1,), (0,)), ((), ())), preferred_element_type=F32)


def dot_nt(a, b):
    return lax.dot_general(a, b, (((1,), (1,)), ((), ())), preferred_element_type=F32)


def ring(count, shift):
    return [((target + shift) % count, target) for target in range(count)]


def prepare(place, tensor, mine, again, turned, *, share):
    some = mine.shape[1]
    turned[...] = tensor[...].T
    start = place[1] * share
    for at in range(share):
        rows = turned[pl.ds(start + at, some, stride=turned.shape[0] // some), :]
        mine[at] = rows
        again[at] = rows


def halve(place, block, token, *outs):
    some = outs[0].shape[0]
    for i, out in enumerate(outs):
        out[...] = block[i * some : (i + 1) * some]


def after(block, *tokens):
    return pl.pallas_call(
        lambda *refs: None,
        out_shape=jax.ShapeDtypeStruct(block.shape, block.dtype),
        in_specs=[ANY] * (1 + len(tokens)),
        out_specs=ANY,
        input_output_aliases={0: 0},
        compiler_params=pltpu.CompilerParams(vmem_limit_bytes=MIB),
        name="after",
    )(block, *tokens)


def shifts_of(naux):
    plan = []
    for shift in range(1, naux // 2 + 1):
        if 2 * shift < naux:
            plan.append([(source, (source + shift) % naux) for source in range(naux)])
        else:
            plan.append([(z, z + shift) if z % 2 else (z + shift, z) for z in range(shift)])
    return plan


def select(block, list_rows, slots, width):
    parts = []
    for slot in range(slots):
        entry = list_rows[:1, slot : slot + 1]
        chosen = jnp.zeros((block.shape[0], width), F32)
        for j in range(block.shape[1] // width):
            chosen = jnp.where(entry == float(j), block[:, j * width : (j + 1) * width], chosen)
        parts.append(chosen)
    return jnp.concatenate(parts, axis=1)


def mix(place, near, far, tensor, rows, slots, width, share):
    nt = near.shape[0]
    pairs = tensor.shape[1] // (2 * width)
    near_list, far_list = near[0, 2 * width :, :], far[0, 2 * width :, :]
    which = [lax.rem(tau + nt - place[1], nt) for tau in range(nt)]
    left = []
    for kind in range(2):
        for tau in range(nt):
            start = pl.multiple_of(kind * width + place[1] * share, share)
            left.append(select(near[which[tau], pl.ds(start, share), :], far_list, slots, width))
    left_high, left_low = halves(jnp.concatenate(left, axis=0))
    high, low = halves(tensor[...])
    middle = dot(
        jnp.concatenate([left_high, left_high, left_low], axis=1), jnp.concatenate([high, low, high], axis=0)
    )
    for group in range(2 * nt):
        for at in range(pairs):
            rows[(group * pairs + at) * share : (group * pairs + at + 1) * share, :] = middle[
                group * share : (group + 1) * share, 2 * width * at : 2 * width * (at + 1)
            ]
    results = []
    for group in range(2 * nt):
        kind, tau = group // nt, group % nt
        right = select(far[which[tau], (1 - kind) * width : (2 - kind) * width, :], near_list, slots, width)
        zero = jnp.zeros_like(right)
        right_high, right_low = halves(
            jnp.concatenate([jnp.concatenate([right, zero], axis=1), jnp.concatenate([zero, right], axis=1)], axis=0)
        )

        rows_high, rows_low = halves(
            jnp.concatenate(
                [rows[pl.ds(group * pairs * share + at, pairs, stride=share), :] for at in range(share)], axis=0
            )
        )
        results.append(
            dot(
                jnp.concatenate([rows_high, rows_high, rows_low], axis=1),
                jnp.concatenate([right_high, right_low, right_high], axis=0),
            )
        )
    return results


def first(place, near, tensor, acc, token, rows, *, slots, width, share):
    token[...] = jnp.zeros_like(token)
    for group, result in enumerate(mix(place, near, near, tensor, rows, slots, width, share)):
        acc[group] = result


def second(place, near, acc, *refs, slots, width, share, others):
    refs, (sides, token, rows) = refs[: 2 * others], refs[-3:]
    tensors, fars = refs[: len(refs) // 2], refs[len(refs) // 2 :]
    token[...] = jnp.zeros_like(token)
    listed = slots * width
    groups, tall, _ = acc.shape
    pairs = tall // share
    total = [acc[group] for group in range(groups)]
    for tensor, far in zip(tensors, fars):
        term = mix(place, near, far, tensor, rows, slots, width, share)
        total = [x + y for x, y in zip(total, term)]
    for group in range(groups):
        height = groups * pairs
        high, low = halves(total[group])
        for odd in range(2):
            row = (2 * (group % (groups // 2)) + odd) * pairs + 2 * height * (group * 2 // groups)
            for at in range(share):
                for part, array in enumerate((high, low)):
                    sides[
                        part * height + row : part * height + row + pairs, at * listed : (at + 1) * listed
                    ] = array[at * pairs : (at + 1) * pairs, odd * listed : (odd + 1) * listed]


def relay(pieces, tensor):
    for i, parts in enumerate(pieces):
        at = 0
        for part in parts:
            per, half, listed = part.shape
            for inner in range(per):
                high, low = halves(part[inner])
                tensor[2 * i * half : (2 * i + 1) * half, at * listed : (at + 1) * listed] = high
                tensor[(2 * i + 1) * half : 2 * (i + 1) * half, at * listed : (at + 1) * listed] = low
                at += 1


def products(tensor, side, half):
    all_parts = dot_nt(tensor, side)
    width = side.shape[0] // 2
    rows = []
    for i in range(tensor.shape[0] // (2 * half)):
        block = all_parts[2 * i * half : (2 * i + 1) * half] + all_parts[(2 * i + 1) * half : 2 * (i + 1) * half]
        rows.append(block[:, :width] + block[:, width:])
    return jnp.concatenate(rows, axis=0)


def unfold(block, ordered, i):
    turned = block.T
    pairs = block.shape[0] // 4
    for group in range(turned.shape[0] // (2 * pairs)):
        for odd in range(2):
            at = (2 * group + odd) * pairs
            ordered[i, pl.ds(2 * group * pairs + odd, pairs, stride=2), :] = turned[at : at + pairs]


def at_sub(place, x, axis):
    zero = jnp.zeros_like(x)
    return by_sub(place, x, zero, axis)


def by_sub(place, own, other, axis):
    return jnp.where(
        place[2] == 0, jnp.concatenate([own, other], axis=axis), jnp.concatenate([other, own], axis=axis)
    )


def fold(place, own, other, ordered):
    unfold(by_sub(place, own, other, 0), ordered, 0)
    back = ordered[0].T
    half = own.shape[0]
    return jnp.concatenate([back[:half], back[half:]], axis=1)


def meet_own(place, sides, *refs, count):
    refs, (tensor, back, *backs, ordered) = refs[: 4 * count - 3], refs[4 * count - 3 :]
    pieces = [refs[i : i + 2] for i in range(0, 4 * count - 4, 2)] + [refs[-1:]]
    half = refs[0].shape[1]
    relay(pieces, tensor)
    rest = products(tensor[...], sides[sides.shape[0] // 2 :, :], half)
    for i, back_ref in enumerate(backs):
        back_ref[...] = fold(
            place, rest[2 * i * half : (2 * i + 1) * half], rest[(2 * i + 1) * half : 2 * (i + 1) * half], ordered
        )
    back[...] = rest[-half:]


def meet_back(place, sides, own, piece, tensor, back_ref, ordered):
    half = piece.shape[1]
    relay([[piece]], tensor)
    other = products(tensor[...], sides[sides.shape[0] // 2 :, :], half)
    back_ref[...] = fold(place, own[...], other, ordered)


def meet_direct(place, sides, mine, mine_other, own, last, out_ref, tensor, ordered, *, nt, naux):
    count = ordered.shape[0]
    block = ordered.shape[2]
    half = block // 2
    side = sides[: sides.shape[0] // 2, :]
    relay([[mine], [mine_other]], tensor)
    tensor[4 * half :, :] = last[...]
    some = products(tensor[...], side, half)
    own = jnp.concatenate([some[:block], products(own[...], side, half)], axis=0)
    other = some[block:]
    for i in range(count):
        first_half = own[i * block : i * block + half]
        second_half = own[i * block + half : (i + 1) * block] if i < count - 1 else other
        unfold(by_sub(place, first_half, second_half, 0), ordered, i)
    for tau in range(nt):
        here = [jnp.zeros((half, block), F32)] * naux
        for shift in range(count):
            here[(naux - shift) % naux] = ordered[shift, tau * half : (tau + 1) * half, :]
        out_ref[tau] = at_sub(place, jnp.concatenate(here, axis=1), 0)


def complete(place, early, *refs):
    backs, keep, give = refs[:-2], refs[-2], refs[-1]
    nt, block, wide = early.shape
    naux = wide // block
    half = block // 2
    for tau in range(nt):
        parts = [jnp.zeros((block, block), F32)] * naux
        for shift, ref in enumerate(backs, 1):
            upper = ref[:, tau * half : (tau + 1) * half]
            lower = ref[:, (nt + tau) * half : (nt + tau + 1) * half]
            parts[shift] = at_sub(place, jnp.concatenate([upper, lower], axis=0), 1)
        total = early[tau] + jnp.concatenate(parts, axis=1)
        total = pltpu.roll(total, place[3] * block, 1)
        owners, rows, _ = keep.shape
        for i in range(owners // nt):
            first_rows = total[2 * i * rows : (2 * i + 1) * rows]
            second_rows = total[(2 * i + 1) * rows : 2 * (i + 1) * rows]
            keep[tau * (owners // nt) + i] = jnp.where(place[2] == 0, first_rows, second_rows)
            give[tau * (owners // nt) + i] = jnp.where(place[2] == 0, second_rows, first_rows)


def local(three_center, occupied_green, virtual_green, block_list, sizes):
    nt, naux, nob, nsub = sizes
    slots = three_center.shape[2]
    width = three_center.shape[3]
    columns = three_center.shape[4]
    rows_aux = columns // width
    block_aux = rows_aux * nsub
    norb = occupied_green.shape[1]
    listed = slots * width
    share = width // nt
    nauxf = naux * block_aux
    tensor = three_center.reshape(listed, columns)
    limit = 24 + 3 * max(nob - 2, 0)

    def call(kernel, outs, scratch, flops, *arguments, **options):
        shapes = [jax.ShapeDtypeStruct(shape, kind) for shape, kind in outs]
        size = sum(4 * math.prod(x.shape) for x in arguments)

        def here(*refs):
            kernel([lax.axis_index(axis) for axis in ("orb", "tau", "sub", "aux")], *refs, **options)

        return pl.pallas_call(
            here,
            out_shape=shapes,
            in_specs=[VMEM] * len(arguments),
            out_specs=[VMEM] * len(shapes),
            scratch_shapes=[pltpu.VMEM(shape, kind) for shape, kind in scratch],
            compiler_params=pltpu.CompilerParams(vmem_limit_bytes=limit * MIB),
            cost_estimate=pl.CostEstimate(flops=flops, bytes_accessed=size, transcendentals=0),
            name=kernel.__name__,
        )(*arguments)

    tensors = [lax.ppermute(tensor, "orb", ring(nob, shift)) for shift in range(1, nob)]
    mine, again = call(
        prepare, [((share, rows_aux, listed), F32)] * 2, [((columns, listed), F32)], 0, tensor, share=share
    )
    plan = shifts_of(naux)
    swap = ring(nsub, 1)
    small = jnp.concatenate(
        [
            occupied_green,
            virtual_green,
            jnp.pad(block_list.astype(F32), ((0, LIST_ROWS - 1), (0, norb - slots))),
        ]
    )
    near = jnp.stack([small] + [lax.ppermute(small, "tau", ring(nt, shift)) for shift in range(1, nt)])
    groups = 2 * nt
    work = 6 * groups * share * columns * listed * 3
    rows = groups * rows_aux
    depth = share * listed
    options = dict(slots=slots, width=width, share=share)
    acc, token = call(
        first,
        [((groups, rows_aux // 2 * share, 2 * listed), F32), ((8, 128), F32)],
        [((groups * rows_aux // 2 * share, 2 * width), F32)],
        0,
        near,
        tensor,
        **options,
    )
    mine_other = lax.ppermute(mine, "sub", swap)
    early = [mine_other]
    for pairs in plan[:-1]:
        parts = call(
            halve, [((share // 2, rows_aux, listed), F32)] * 2, [], 0, lax.ppermute(mine, "aux", pairs), token
        )
        early += [*parts, *(lax.ppermute(part, "sub", swap) for part in parts)]
    last = lax.ppermute(after(again, lax.ppermute(token, "sub", swap)), "aux", plan[-1])
    fars = []
    late_near = after(near, *early)
    for shift in range(1, nob):
        pairs = [(a * nsub + c, b * nsub + (c + 1) % nsub) for a, b in ring(nob, shift) for c in range(nsub)]
        fars.append(lax.ppermute(late_near, ("orb", "sub"), pairs))
    sides, token_late = call(
        second,
        [((2 * rows, depth), BF16), ((8, 128), F32)],
        [((groups * rows_aux // 2 * share, 2 * width), F32)],
        work,
        near,
        acc,
        *tensors,
        *fars,
        *early,
        others=nob - 1,
        **options,
    )
    last = after(last, token_late)
    last_other = lax.ppermute(last, "sub", swap)
    count = 1 + len(plan)
    work = 8 * rows * depth * rows_aux
    wide = nt * rows_aux
    shape = ((rows_aux, 2 * wide), F32)
    scratch = lambda count: ((count, wide, block_aux), F32)
    own_rows = 2 * (2 * count - 3) * rows_aux
    own, back, *backs = call(
        meet_own,
        [((own_rows, depth), BF16), ((rows_aux, wide), F32)] + [shape] * (len(plan) - 1),
        [scratch(1)],
        work * (2 * count - 3),
        sides,
        *early[1:],
        last,
        count=len(plan),
    )
    tensor, *last_back = call(
        meet_back,
        [((2 * rows_aux, depth), BF16), shape],
        [scratch(1)],
        work,
        sides,
        back,
        last_other,
    )
    backs += last_back
    returned = [
        lax.ppermute(back, "aux", [(target, source) for source, target in pairs]) for back, pairs in zip(backs, plan)
    ]
    shape = ((nt, block_aux, nauxf), F32)
    (direct,) = call(
        meet_direct,
        [shape],
        [((6 * rows_aux, depth), BF16), ((count, wide, block_aux), F32)],
        work * (2 * count),
        sides,
        mine,
        mine_other,
        own,
        tensor,
        nt=nt,
        naux=naux,
    )
    owners = nt * nob
    shape = ((owners, block_aux // (nob * nsub), nauxf), F32)
    keep, give = call(complete, [shape] * 2, [], 0, direct, *returned)
    received = lax.all_to_all(
        keep + lax.ppermute(give, "sub", swap), ("tau", "orb"), split_axis=0, concat_axis=0, tiled=True
    )
    return received.sum(axis=0) * (-2.0 / math.sqrt(norb * slots * width))


def solution(mesh):
    sizes = tuple(mesh.shape[axis] for axis in ("tau", "aux", "orb", "sub"))
    in_specs = (
        P("aux", "orb", None, None, "sub"),
        P(("tau", "orb"), None),
        P(("tau", "orb"), None),
        P("orb", None),
    )
    out_specs = P(("tau", "aux", "orb", "sub"), None)
    return jax.shard_map(
        functools.partial(local, sizes=sizes), mesh=mesh, in_specs=in_specs, out_specs=out_specs, check_vma=False
    )
```

```python
import functools
import math

import jax
import jax.numpy as jnp
from jax import lax
from jax.experimental import pallas as pl
from jax.experimental.pallas import tpu as pltpu
from jax.sharding import PartitionSpec as P

VMEM = pl.BlockSpec(memory_space=pltpu.VMEM)
ANY = pl.BlockSpec(memory_space=pl.ANY)
HBM = pl.BlockSpec(memory_space=pltpu.HBM)
F32 = jnp.float32
BF16 = jnp.bfloat16
LIST_ROWS = 8
MIB = 1024 * 1024


def halves(x):
    high = x.astype(BF16)
    return high, (x - high.astype(F32)).astype(BF16)


def dot(a, b):
    return lax.dot_general(a, b, (((1,), (0,)), ((), ())), preferred_element_type=F32)


def dot_nt(a, b):
    return lax.dot_general(a, b, (((1,), (1,)), ((), ())), preferred_element_type=F32)


def ring(count, shift):
    return [((target + shift) % count, target) for target in range(count)]


def prepare(place, tensor, mine, again, turned, *, share):
    some = mine.shape[1]
    columns = tensor.shape[1]
    turned[:columns, :] = tensor[...].T
    start = place[1] * share
    for at in range(share):
        rows = turned[pl.ds(start + at, some, stride=columns // some), :]
        mine[at] = rows
        again[at] = rows


def halve(place, block, token, *outs):
    some = outs[0].shape[0]
    for i, out in enumerate(outs):
        out[...] = block[i * some : (i + 1) * some]


def after(block, *tokens):
    return pl.pallas_call(
        lambda *refs: None,
        out_shape=jax.ShapeDtypeStruct(block.shape, block.dtype),
        in_specs=[ANY] * (1 + len(tokens)),
        out_specs=ANY,
        input_output_aliases={0: 0},
        compiler_params=pltpu.CompilerParams(vmem_limit_bytes=MIB),
        name="after",
    )(block, *tokens)


def shifts_of(naux):
    plan = []
    for shift in range(1, naux // 2 + 1):
        if 2 * shift < naux:
            plan.append([(source, (source + shift) % naux) for source in range(naux)])
        else:
            plan.append([(z, z + shift) if z % 2 else (z + shift, z) for z in range(shift)])
    return plan


def select(block, list_rows, slots, width):
    parts = []
    for slot in range(slots):
        entry = list_rows[:1, slot : slot + 1]
        chosen = jnp.zeros((block.shape[0], width), F32)
        for j in range(block.shape[1] // width):
            chosen = jnp.where(entry == float(j), block[:, j * width : (j + 1) * width], chosen)
        parts.append(chosen)
    return jnp.concatenate(parts, axis=1)


def mix(place, near, far, tensor, rows, slots, width, share):
    nt = near.shape[0]
    pairs = tensor.shape[1] // (2 * width)
    near_list, far_list = near[0, 2 * width :, :], far[0, 2 * width :, :]
    which = [lax.rem(tau + nt - place[1], nt) for tau in range(nt)]
    left = []
    for kind in range(2):
        for tau in range(nt):
            start = pl.multiple_of(kind * width + place[1] * share, share)
            left.append(select(near[which[tau], pl.ds(start, share), :], far_list, slots, width))
    left_high, left_low = halves(jnp.concatenate(left, axis=0))
    high, low = halves(tensor[...])
    middle = dot(
        jnp.concatenate([left_high, left_high, left_low], axis=1), jnp.concatenate([high, low, high], axis=0)
    )
    for group in range(2 * nt):
        for at in range(pairs):
            rows[(group * pairs + at) * share : (group * pairs + at + 1) * share, :] = middle[
                group * share : (group + 1) * share, 2 * width * at : 2 * width * (at + 1)
            ]
    results = []
    for group in range(2 * nt):
        kind, tau = group // nt, group % nt
        right = select(far[which[tau], (1 - kind) * width : (2 - kind) * width, :], near_list, slots, width)
        zero = jnp.zeros_like(right)
        right_high, right_low = halves(
            jnp.concatenate([jnp.concatenate([right, zero], axis=1), jnp.concatenate([zero, right], axis=1)], axis=0)
        )

        rows_high, rows_low = halves(
            jnp.concatenate(
                [rows[pl.ds(group * pairs * share + at, pairs, stride=share), :] for at in range(share)], axis=0
            )
        )
        results.append(
            dot(
                jnp.concatenate([rows_high, rows_high, rows_low], axis=1),
                jnp.concatenate([right_high, right_low, right_high], axis=0),
            )
        )
    return results


def first(place, near, tensor, acc, token, rows, *, slots, width, share):
    token[...] = jnp.zeros_like(token)
    for group, result in enumerate(mix(place, near, near, tensor, rows, slots, width, share)):
        acc[group] = result


def second(place, near, acc, *refs, slots, width, share, others):
    refs, (sides, token, rows) = refs[: 2 * others], refs[-3:]
    tensors, fars = refs[: len(refs) // 2], refs[len(refs) // 2 :]
    token[...] = jnp.zeros_like(token)
    listed = slots * width
    groups, tall, _ = acc.shape
    pairs = tall // share
    total = [acc[group] for group in range(groups)]
    for tensor, far in zip(tensors, fars):
        term = mix(place, near, far, tensor, rows, slots, width, share)
        total = [x + y for x, y in zip(total, term)]
    for group in range(groups):
        height = groups * pairs
        high, low = halves(total[group])
        for odd in range(2):
            row = (2 * (group % (groups // 2)) + odd) * pairs + 2 * height * (group * 2 // groups)
            for at in range(share):
                for part, array in enumerate((high, low)):
                    sides[
                        part * height + row : part * height + row + pairs, at * listed : (at + 1) * listed
                    ] = array[at * pairs : (at + 1) * pairs, odd * listed : (odd + 1) * listed]


def relay(pieces, tensor):
    for i, parts in enumerate(pieces):
        at = 0
        for part in parts:
            per, half, listed = part.shape
            for inner in range(per):
                high, low = halves(part[inner])
                tensor[2 * i * half : (2 * i + 1) * half, at * listed : (at + 1) * listed] = high
                tensor[(2 * i + 1) * half : 2 * (i + 1) * half, at * listed : (at + 1) * listed] = low
                at += 1


def products(tensor, side, half):
    all_parts = dot_nt(tensor, side)
    width = side.shape[0] // 2
    rows = []
    for i in range(tensor.shape[0] // (2 * half)):
        block = all_parts[2 * i * half : (2 * i + 1) * half] + all_parts[(2 * i + 1) * half : 2 * (i + 1) * half]
        rows.append(block[:, :width] + block[:, width:])
    return jnp.concatenate(rows, axis=0)


def unfold(block, ordered, i):
    turned = block.T
    pairs = block.shape[0] // 4
    for group in range(turned.shape[0] // (2 * pairs)):
        for odd in range(2):
            at = (2 * group + odd) * pairs
            ordered[i, pl.ds(2 * group * pairs + odd, pairs, stride=2), :] = turned[at : at + pairs]


def at_sub(place, x, axis):
    zero = jnp.zeros_like(x)
    return by_sub(place, x, zero, axis)


def by_sub(place, own, other, axis):
    return jnp.where(
        place[2] == 0, jnp.concatenate([own, other], axis=axis), jnp.concatenate([other, own], axis=axis)
    )


def fold(place, own, other, ordered):
    unfold(by_sub(place, own, other, 0), ordered, 0)
    back = ordered[0, : own.shape[1], :].T
    half = own.shape[0]
    return jnp.concatenate([back[:half], back[half:]], axis=1)


def meet_own(place, sides, *refs, count):
    refs, (tensor, back, *backs, ordered) = refs[: 4 * count - 3], refs[4 * count - 3 :]
    pieces = [refs[i : i + 2] for i in range(0, 4 * count - 4, 2)] + [refs[-1:]]
    half = refs[0].shape[1]
    relay(pieces, tensor)
    rest = products(tensor[...], sides[sides.shape[0] // 2 :, :], half)
    for i, back_ref in enumerate(backs):
        back_ref[...] = fold(
            place, rest[2 * i * half : (2 * i + 1) * half], rest[(2 * i + 1) * half : 2 * (i + 1) * half], ordered
        )
    back[...] = rest[-half:]


def meet_back(place, sides, own, piece, tensor, back_ref, ordered):
    half = piece.shape[1]
    relay([[piece]], tensor)
    other = products(tensor[...], sides[sides.shape[0] // 2 :, :], half)
    back_ref[...] = fold(place, own[...], other, ordered)


def meet_direct(place, sides, mine, mine_other, own, last, out_ref, tensor, ordered, *, nt, naux):
    count = ordered.shape[0]
    block = ordered.shape[2]
    half = block // 2
    side = sides[: sides.shape[0] // 2, :]
    relay([[mine], [mine_other]], tensor)
    tensor[4 * half :, :] = last[...]
    some = products(tensor[...], side, half)
    own = jnp.concatenate([some[:block], products(own[...], side, half)], axis=0)
    other = some[block:]
    for i in range(count):
        first_half = own[i * block : i * block + half]
        second_half = own[i * block + half : (i + 1) * block] if i < count - 1 else other
        unfold(by_sub(place, first_half, second_half, 0), ordered, i)
    for tau in range(nt):
        here = [jnp.zeros((half, block), F32)] * naux
        for shift in range(count):
            here[(naux - shift) % naux] = ordered[shift, tau * half : (tau + 1) * half, :]
        out_ref[tau] = at_sub(place, jnp.concatenate(here, axis=1), 0)


def complete(place, early, *refs):
    backs, out_ref = refs[:-1], refs[-1]
    nt, block, wide = early.shape
    naux = wide // block
    half = block // 2
    for tau in range(nt):
        parts = [jnp.zeros((block, block), F32)] * naux
        for shift, ref in enumerate(backs, 1):
            upper = ref[:, tau * half : (tau + 1) * half]
            lower = ref[:, (nt + tau) * half : (nt + tau + 1) * half]
            parts[shift] = at_sub(place, jnp.concatenate([upper, lower], axis=0), 1)
        total = early[tau] + jnp.concatenate(parts, axis=1)
        out_ref[tau] = pltpu.roll(total, place[3] * block, 1)


def local(three_center, occupied_green, virtual_green, block_list, sizes):
    nt, naux, nob, nsub = sizes
    slots = three_center.shape[2]
    width = three_center.shape[3]
    columns = three_center.shape[4]
    rows_aux = columns // width
    block_aux = rows_aux * nsub
    norb = occupied_green.shape[1]
    listed = slots * width
    share = width // nt
    nauxf = naux * block_aux
    tensor = three_center.reshape(listed, columns)
    limit = 24 + 3 * max(nob - 2, 0)

    def call(kernel, outs, scratch, flops, *arguments, **options):
        shapes = [jax.ShapeDtypeStruct(shape, kind) for shape, kind in outs]
        size = sum(4 * math.prod(x.shape) for x in arguments)

        def here(*refs):
            kernel([lax.axis_index(axis) for axis in ("orb", "tau", "sub", "aux")], *refs, **options)

        return pl.pallas_call(
            here,
            out_shape=shapes,
            in_specs=[VMEM] * len(arguments),
            out_specs=[VMEM] * len(shapes),
            scratch_shapes=[pltpu.VMEM(shape, kind) for shape, kind in scratch],
            compiler_params=pltpu.CompilerParams(vmem_limit_bytes=limit * MIB),
            cost_estimate=pl.CostEstimate(flops=flops, bytes_accessed=size, transcendentals=0),
            name=kernel.__name__,
        )(*arguments)

    tensors = [lax.ppermute(tensor, "orb", ring(nob, shift)) for shift in range(1, nob)]
    mine, again = call(
        prepare, [((share, rows_aux, listed), F32)] * 2, [((columns + width, listed), F32)], 0, tensor, share=share
    )
    plan = shifts_of(naux)
    swap = ring(nsub, 1)
    small = jnp.concatenate(
        [
            occupied_green,
            virtual_green,
            jnp.pad(block_list.astype(F32), ((0, LIST_ROWS - 1), (0, norb - slots))),
        ]
    )
    near = jnp.stack([small] + [lax.ppermute(small, "tau", ring(nt, shift)) for shift in range(1, nt)])
    groups = 2 * nt
    work = 6 * groups * share * columns * listed * 3
    rows = groups * rows_aux
    depth = share * listed
    options = dict(slots=slots, width=width, share=share)
    acc, token = call(
        first,
        [((groups, rows_aux // 2 * share, 2 * listed), F32), ((8, 128), F32)],
        [((groups * rows_aux // 2 * share + share, 2 * width), F32)],
        0,
        near,
        tensor,
        **options,
    )
    mine_other = lax.ppermute(mine, "sub", swap)
    early = [mine_other]
    for pairs in plan[:-1]:
        parts = call(
            halve, [((share // 2, rows_aux, listed), F32)] * 2, [], 0, lax.ppermute(mine, "aux", pairs), token
        )
        early += [*parts, *(lax.ppermute(part, "sub", swap) for part in parts)]
    last = lax.ppermute(after(again, lax.ppermute(token, "sub", swap)), "aux", plan[-1])
    fars = []
    late_near = after(near, *early)
    for shift in range(1, nob):
        pairs = [(a * nsub + c, b * nsub + (c + 1) % nsub) for a, b in ring(nob, shift) for c in range(nsub)]
        fars.append(lax.ppermute(late_near, ("orb", "sub"), pairs))
    sides, token_late = call(
        second,
        [((2 * rows, depth), BF16), ((8, 128), F32)],
        [((groups * rows_aux // 2 * share + share, 2 * width), F32)],
        work,
        near,
        acc,
        *tensors,
        *fars,
        *early,
        others=nob - 1,
        **options,
    )
    last = after(last, token_late)
    last_other = lax.ppermute(last, "sub", swap)
    count = 1 + len(plan)
    work = 8 * rows * depth * rows_aux
    wide = nt * rows_aux
    shape = ((rows_aux, 2 * wide), F32)
    scratch = lambda count: ((count, wide + 8, block_aux), F32)
    own_rows = 2 * (2 * count - 3) * rows_aux
    own, back, *backs = call(
        meet_own,
        [((own_rows, depth), BF16), ((rows_aux, wide), F32)] + [shape] * (len(plan) - 1),
        [scratch(1)],
        work * (2 * count - 3),
        sides,
        *early[1:],
        last,
        count=len(plan),
    )
    tensor, *last_back = call(
        meet_back,
        [((2 * rows_aux, depth), BF16), shape],
        [scratch(1)],
        work,
        sides,
        back,
        last_other,
    )
    backs += last_back
    returned = [
        lax.ppermute(back, "aux", [(target, source) for source, target in pairs]) for back, pairs in zip(backs, plan)
    ]
    shape = ((nt, block_aux, nauxf), F32)
    (direct,) = call(
        meet_direct,
        [shape],
        [((6 * rows_aux, depth), BF16), scratch(count)],
        work * (2 * count),
        sides,
        mine,
        mine_other,
        own,
        tensor,
        nt=nt,
        naux=naux,
    )
    (partial_chi,) = call(complete, [shape], [], 0, direct, *returned)
    owners = nt * nob * nsub
    received = lax.all_to_all(
        partial_chi.reshape(owners, nt * block_aux // owners, nauxf),
        ("tau", "orb", "sub"),
        split_axis=0,
        concat_axis=0,
        tiled=True,
    )
    return received.sum(axis=0) * (-2.0 / math.sqrt(norb * slots * width))


def solution(mesh):
    sizes = tuple(mesh.shape[axis] for axis in ("tau", "aux", "orb", "sub"))
    in_specs = (
        P("aux", "orb", None, None, "sub"),
        P(("tau", "orb"), None),
        P(("tau", "orb"), None),
        P("orb", None),
    )
    out_specs = P(("tau", "aux", "orb", "sub"), None)
    return jax.shard_map(
        functools.partial(local, sizes=sizes), mesh=mesh, in_specs=in_specs, out_specs=out_specs, check_vma=False
    )
```

```python
import functools
import math

import jax
import jax.numpy as jnp
from jax import lax
from jax.experimental import pallas as pl
from jax.experimental.pallas import tpu as pltpu
from jax.sharding import PartitionSpec as P

VMEM = pl.BlockSpec(memory_space=pltpu.VMEM)
ANY = pl.BlockSpec(memory_space=pl.ANY)
HBM = pl.BlockSpec(memory_space=pltpu.HBM)
F32 = jnp.float32
BF16 = jnp.bfloat16
LIST_ROWS = 8
MIB = 1024 * 1024


def halves(x):
    high = x.astype(BF16)
    return high, (x - high.astype(F32)).astype(BF16)


def dot(a, b):
    return lax.dot_general(a, b, (((1,), (0,)), ((), ())), preferred_element_type=F32)


def dot_nt(a, b):
    return lax.dot_general(a, b, (((1,), (1,)), ((), ())), preferred_element_type=F32)


def ring(count, shift):
    return [((target + shift) % count, target) for target in range(count)]


def prepare(place, tensor, mine, again, turned, *, share):
    some = mine.shape[1]
    columns = tensor.shape[1]
    turned[:columns, :] = tensor[...].T
    start = place[1] * share
    for at in range(share):
        rows = turned[pl.ds(start + at, some, stride=columns // some), :]
        mine[at] = rows
        again[at] = rows


def halve(place, block, token, *outs):
    some = outs[0].shape[0]
    for i, out in enumerate(outs):
        out[...] = block[i * some : (i + 1) * some]


def after(block, *tokens):
    return pl.pallas_call(
        lambda *refs: None,
        out_shape=jax.ShapeDtypeStruct(block.shape, block.dtype),
        in_specs=[ANY] * (1 + len(tokens)),
        out_specs=ANY,
        input_output_aliases={0: 0},
        compiler_params=pltpu.CompilerParams(vmem_limit_bytes=MIB),
        name="after",
    )(block, *tokens)


def shifts_of(naux):
    plan = []
    for shift in range(1, naux // 2 + 1):
        if 2 * shift < naux:
            plan.append([(source, (source + shift) % naux) for source in range(naux)])
        else:
            plan.append([(z, z + shift) if z % 2 else (z + shift, z) for z in range(shift)])
    return plan


def select(block, list_rows, slots, width):
    parts = []
    for slot in range(slots):
        entry = list_rows[:1, slot : slot + 1]
        chosen = jnp.zeros((block.shape[0], width), F32)
        for j in range(block.shape[1] // width):
            chosen = jnp.where(entry == float(j), block[:, j * width : (j + 1) * width], chosen)
        parts.append(chosen)
    return jnp.concatenate(parts, axis=1)


def mix(place, near, far, tensor, rows, slots, width, share):
    nt = near.shape[0]
    pairs = tensor.shape[1] // (2 * width)
    near_list, far_list = near[0, 2 * width :, :], far[0, 2 * width :, :]
    which = [lax.rem(tau + nt - place[1], nt) for tau in range(nt)]
    left = []
    for kind in range(2):
        for tau in range(nt):
            start = pl.multiple_of(kind * width + place[1] * share, share)
            left.append(select(near[which[tau], pl.ds(start, share), :], far_list, slots, width))
    left_high, left_low = halves(jnp.concatenate(left, axis=0))
    high, low = halves(tensor[...])
    middle = dot(
        jnp.concatenate([left_high, left_high, left_low], axis=1), jnp.concatenate([high, low, high], axis=0)
    )
    for group in range(2 * nt):
        for at in range(pairs):
            rows[(group * pairs + at) * share : (group * pairs + at + 1) * share, :] = middle[
                group * share : (group + 1) * share, 2 * width * at : 2 * width * (at + 1)
            ]
    results = []
    for group in range(2 * nt):
        kind, tau = group // nt, group % nt
        right = select(far[which[tau], (1 - kind) * width : (2 - kind) * width, :], near_list, slots, width)
        zero = jnp.zeros_like(right)
        right_high, right_low = halves(
            jnp.concatenate([jnp.concatenate([right, zero], axis=1), jnp.concatenate([zero, right], axis=1)], axis=0)
        )

        rows_high, rows_low = halves(
            jnp.concatenate(
                [rows[pl.ds(group * pairs * share + at, pairs, stride=share), :] for at in range(share)], axis=0
            )
        )
        results.append(
            dot(
                jnp.concatenate([rows_high, rows_high, rows_low], axis=1),
                jnp.concatenate([right_high, right_low, right_high], axis=0),
            )
        )
    return results


def first(place, near, tensor, acc, token, rows, *, slots, width, share):
    token[...] = jnp.zeros_like(token)
    for group, result in enumerate(mix(place, near, near, tensor, rows, slots, width, share)):
        acc[group] = result


def second(place, near, acc, *refs, slots, width, share, others):
    refs, (sides, token, rows) = refs[: 2 * others], refs[-3:]
    tensors, fars = refs[: len(refs) // 2], refs[len(refs) // 2 :]
    token[...] = jnp.zeros_like(token)
    listed = slots * width
    groups, tall, _ = acc.shape
    pairs = tall // share
    total = [acc[group] for group in range(groups)]
    for tensor, far in zip(tensors, fars):
        term = mix(place, near, far, tensor, rows, slots, width, share)
        total = [x + y for x, y in zip(total, term)]
    for group in range(groups):
        height = groups * pairs
        high, low = halves(total[group])
        for odd in range(2):
            row = (2 * (group % (groups // 2)) + odd) * pairs + 2 * height * (group * 2 // groups)
            for at in range(share):
                for part, array in enumerate((high, low)):
                    sides[
                        part * height + row : part * height + row + pairs, at * listed : (at + 1) * listed
                    ] = array[at * pairs : (at + 1) * pairs, odd * listed : (odd + 1) * listed]


def relay(pieces, tensor):
    for i, parts in enumerate(pieces):
        at = 0
        for part in parts:
            per, half, listed = part.shape
            for inner in range(per):
                high, low = halves(part[inner])
                tensor[2 * i * half : (2 * i + 1) * half, at * listed : (at + 1) * listed] = high
                tensor[(2 * i + 1) * half : 2 * (i + 1) * half, at * listed : (at + 1) * listed] = low
                at += 1


def products(tensor, side, half):
    all_parts = dot_nt(tensor, side)
    width = side.shape[0] // 2
    rows = []
    for i in range(tensor.shape[0] // (2 * half)):
        block = all_parts[2 * i * half : (2 * i + 1) * half] + all_parts[(2 * i + 1) * half : 2 * (i + 1) * half]
        rows.append(block[:, :width] + block[:, width:])
    return jnp.concatenate(rows, axis=0)


def unfold(block, ordered, i):
    turned = block.T
    pairs = block.shape[0] // 4
    for group in range(turned.shape[0] // (2 * pairs)):
        for odd in range(2):
            at = (2 * group + odd) * pairs
            ordered[i, pl.ds(2 * group * pairs + odd, pairs, stride=2), :] = turned[at : at + pairs]


def at_sub(place, x, axis):
    zero = jnp.zeros_like(x)
    return by_sub(place, x, zero, axis)


def by_sub(place, own, other, axis):
    return jnp.where(
        place[2] == 0, jnp.concatenate([own, other], axis=axis), jnp.concatenate([other, own], axis=axis)
    )


def fold(place, own, other, ordered):
    unfold(by_sub(place, own, other, 0), ordered, 0)
    back = ordered[0, : own.shape[1], :].T
    half = own.shape[0]
    return jnp.concatenate([back[:half], back[half:]], axis=1)


def meet_own(place, sides, *refs, count):
    refs, (tensor, back, *backs, ordered) = refs[: 4 * count - 3], refs[4 * count - 3 :]
    pieces = [refs[i : i + 2] for i in range(0, 4 * count - 4, 2)] + [refs[-1:]]
    half = refs[0].shape[1]
    relay(pieces, tensor)
    rest = products(tensor[...], sides[sides.shape[0] // 2 :, :], half)
    for i, back_ref in enumerate(backs):
        back_ref[...] = fold(
            place, rest[2 * i * half : (2 * i + 1) * half], rest[(2 * i + 1) * half : 2 * (i + 1) * half], ordered
        )
    back[...] = rest[-half:]


def meet_back(place, sides, own, piece, tensor, back_ref, ordered):
    half = piece.shape[1]
    relay([[piece]], tensor)
    other = products(tensor[...], sides[sides.shape[0] // 2 :, :], half)
    back_ref[...] = fold(place, own[...], other, ordered)


def meet_direct(place, sides, mine, mine_other, own, last, out_ref, tensor, ordered, *, nt, naux):
    count = ordered.shape[0]
    block = ordered.shape[2]
    half = block // 2
    side = sides[: sides.shape[0] // 2, :]
    relay([[mine], [mine_other]], tensor)
    tensor[4 * half :, :] = last[...]
    some = products(tensor[...], side, half)
    own = jnp.concatenate([some[:block], products(own[...], side, half)], axis=0)
    other = some[block:]
    for i in range(count):
        first_half = own[i * block : i * block + half]
        second_half = own[i * block + half : (i + 1) * block] if i < count - 1 else other
        unfold(by_sub(place, first_half, second_half, 0), ordered, i)
    for tau in range(nt):
        here = [jnp.zeros((half, block), F32)] * naux
        for shift in range(count):
            here[(naux - shift) % naux] = ordered[shift, tau * half : (tau + 1) * half, :]
        out_ref[tau] = at_sub(place, jnp.concatenate(here, axis=1), 0)


def complete(place, early, *refs):
    backs, out_ref = refs[:-1], refs[-1]
    nt, block, wide = early.shape
    naux = wide // block
    half = block // 2
    for tau in range(nt):
        parts = [jnp.zeros((block, block), F32)] * naux
        for shift, ref in enumerate(backs, 1):
            upper = ref[:, tau * half : (tau + 1) * half]
            lower = ref[:, (nt + tau) * half : (nt + tau + 1) * half]
            parts[shift] = at_sub(place, jnp.concatenate([upper, lower], axis=0), 1)
        total = early[tau] + jnp.concatenate(parts, axis=1)
        out_ref[tau] = pltpu.roll(total, place[3] * block, 1)


def local(three_center, occupied_green, virtual_green, block_list, sizes):
    nt, naux, nob, nsub = sizes
    slots = three_center.shape[2]
    width = three_center.shape[3]
    columns = three_center.shape[4]
    rows_aux = columns // width
    block_aux = rows_aux * nsub
    norb = occupied_green.shape[1]
    listed = slots * width
    share = width // nt
    nauxf = naux * block_aux
    tensor = three_center.reshape(listed, columns)
    limit = 24 + 3 * max(nob - 2, 0)

    def call(kernel, outs, scratch, flops, *arguments, **options):
        shapes = [jax.ShapeDtypeStruct(shape, kind) for shape, kind in outs]
        size = sum(4 * math.prod(x.shape) for x in arguments)

        def here(*refs):
            kernel([lax.axis_index(axis) for axis in ("orb", "tau", "sub", "aux")], *refs, **options)

        return pl.pallas_call(
            here,
            out_shape=shapes,
            in_specs=[VMEM] * len(arguments),
            out_specs=[VMEM] * len(shapes),
            scratch_shapes=[pltpu.VMEM(shape, kind) for shape, kind in scratch],
            compiler_params=pltpu.CompilerParams(vmem_limit_bytes=limit * MIB),
            cost_estimate=pl.CostEstimate(flops=flops, bytes_accessed=size, transcendentals=0),
            name=kernel.__name__,
        )(*arguments)

    tensors = [lax.ppermute(tensor, "orb", ring(nob, shift)) for shift in range(1, nob)]
    mine, again = call(
        prepare, [((share, rows_aux, listed), F32)] * 2, [((columns + width, listed), F32)], 0, tensor, share=share
    )
    plan = shifts_of(naux)
    swap = ring(nsub, 1)
    small = jnp.concatenate(
        [
            occupied_green,
            virtual_green,
            jnp.pad(block_list.astype(F32), ((0, LIST_ROWS - 1), (0, norb - slots))),
        ]
    )
    near = jnp.stack([small] + [lax.ppermute(small, "tau", ring(nt, shift)) for shift in range(1, nt)])
    groups = 2 * nt
    work = 6 * groups * share * columns * listed * 3
    rows = groups * rows_aux
    depth = share * listed
    options = dict(slots=slots, width=width, share=share)
    acc, token = call(
        first,
        [((groups, rows_aux // 2 * share, 2 * listed), F32), ((8, 128), F32)],
        [((groups * rows_aux // 2 * share + share, 2 * width), F32)],
        0,
        near,
        tensor,
        **options,
    )
    mine_other = lax.ppermute(mine, "sub", swap)
    early = [mine_other]
    for pairs in plan[:-1]:
        parts = call(
            halve, [((share // 2, rows_aux, listed), F32)] * 2, [], 0, lax.ppermute(mine, "aux", pairs), token
        )
        early += [*parts, *(lax.ppermute(part, "sub", swap) for part in parts)]
    last = lax.ppermute(after(again, token), "aux", plan[-1])
    fars = []
    late_near = after(near, *early)
    for shift in range(1, nob):
        pairs = [(a * nsub + c, b * nsub + (c + 1) % nsub) for a, b in ring(nob, shift) for c in range(nsub)]
        fars.append(lax.ppermute(late_near, ("orb", "sub"), pairs))
    sides, token_late = call(
        second,
        [((2 * rows, depth), BF16), ((8, 128), F32)],
        [((groups * rows_aux // 2 * share + share, 2 * width), F32)],
        work,
        near,
        acc,
        *tensors,
        *fars,
        *early,
        others=nob - 1,
        **options,
    )
    last = after(last, token_late)
    last_other = lax.ppermute(last, "sub", swap)
    count = 1 + len(plan)
    work = 8 * rows * depth * rows_aux
    wide = nt * rows_aux
    shape = ((rows_aux, 2 * wide), F32)
    scratch = lambda count: ((count, wide + 8, block_aux), F32)
    own_rows = 2 * (2 * count - 3) * rows_aux
    own, back, *backs = call(
        meet_own,
        [((own_rows, depth), BF16), ((rows_aux, wide), F32)] + [shape] * (len(plan) - 1),
        [scratch(1)],
        work * (2 * count - 3),
        sides,
        *early[1:],
        last,
        count=len(plan),
    )
    tensor, *last_back = call(
        meet_back,
        [((2 * rows_aux, depth), BF16), shape],
        [scratch(1)],
        work,
        sides,
        back,
        last_other,
    )
    backs += last_back
    returned = [
        lax.ppermute(back, "aux", [(target, source) for source, target in pairs]) for back, pairs in zip(backs, plan)
    ]
    shape = ((nt, block_aux, nauxf), F32)
    (direct,) = call(
        meet_direct,
        [shape],
        [((6 * rows_aux, depth), BF16), scratch(count)],
        work * (2 * count),
        sides,
        mine,
        mine_other,
        own,
        tensor,
        nt=nt,
        naux=naux,
    )
    (partial_chi,) = call(complete, [shape], [], 0, direct, *returned)
    owners = nt * nob * nsub
    received = lax.all_to_all(
        partial_chi.reshape(owners, nt * block_aux // owners, nauxf),
        ("tau", "orb", "sub"),
        split_axis=0,
        concat_axis=0,
        tiled=True,
    )
    return received.sum(axis=0) * (-2.0 / math.sqrt(norb * slots * width))


def solution(mesh):
    sizes = tuple(mesh.shape[axis] for axis in ("tau", "aux", "orb", "sub"))
    in_specs = (
        P("aux", "orb", None, None, "sub"),
        P(("tau", "orb"), None),
        P(("tau", "orb"), None),
        P("orb", None),
    )
    out_specs = P(("tau", "aux", "orb", "sub"), None)
    return jax.shard_map(
        functools.partial(local, sizes=sizes), mesh=mesh, in_specs=in_specs, out_specs=out_specs, check_vma=False
    )
```

```python
import functools
import math

import jax
import jax.numpy as jnp
from jax import lax
from jax.experimental import pallas as pl
from jax.experimental.pallas import tpu as pltpu
from jax.sharding import PartitionSpec as P

VMEM = pl.BlockSpec(memory_space=pltpu.VMEM)
ANY = pl.BlockSpec(memory_space=pl.ANY)
HBM = pl.BlockSpec(memory_space=pltpu.HBM)
F32 = jnp.float32
BF16 = jnp.bfloat16
LIST_ROWS = 8
MIB = 1024 * 1024


def halves(x):
    high = x.astype(BF16)
    return high, (x - high.astype(F32)).astype(BF16)


def dot(a, b):
    return lax.dot_general(a, b, (((1,), (0,)), ((), ())), preferred_element_type=F32)


def dot_nt(a, b):
    return lax.dot_general(a, b, (((1,), (1,)), ((), ())), preferred_element_type=F32)


def ring(count, shift):
    return [((target + shift) % count, target) for target in range(count)]


def prepare(place, tensor, mine, again, turned, *, share):
    some = mine.shape[1]
    columns = tensor.shape[1]
    turned[:columns, :] = tensor[...].T
    start = place[1] * share
    for at in range(share):
        rows = turned[pl.ds(start + at, some, stride=columns // some), :]
        mine[at] = rows
        again[at] = rows


def halve(place, block, token, *outs):
    some = outs[0].shape[0]
    for i, out in enumerate(outs):
        out[...] = block[i * some : (i + 1) * some]


def hold(place, block, token, out):
    out[...] = block[...]


def after(block, *tokens):
    return pl.pallas_call(
        lambda *refs: None,
        out_shape=jax.ShapeDtypeStruct(block.shape, block.dtype),
        in_specs=[ANY] * (1 + len(tokens)),
        out_specs=ANY,
        input_output_aliases={0: 0},
        compiler_params=pltpu.CompilerParams(vmem_limit_bytes=MIB),
        name="after",
    )(block, *tokens)


def shifts_of(naux):
    plan = []
    for shift in range(1, naux // 2 + 1):
        if 2 * shift < naux:
            plan.append([(source, (source + shift) % naux) for source in range(naux)])
        else:
            plan.append([(z, z + shift) if z % 2 else (z + shift, z) for z in range(shift)])
    return plan


def select(block, list_rows, slots, width):
    parts = []
    for slot in range(slots):
        entry = list_rows[:1, slot : slot + 1]
        chosen = jnp.zeros((block.shape[0], width), F32)
        for j in range(block.shape[1] // width):
            chosen = jnp.where(entry == float(j), block[:, j * width : (j + 1) * width], chosen)
        parts.append(chosen)
    return jnp.concatenate(parts, axis=1)


def mix(place, near, far, tensor, rows, slots, width, share):
    nt = near.shape[0]
    pairs = tensor.shape[1] // (2 * width)
    near_list, far_list = near[0, 2 * width :, :], far[0, 2 * width :, :]
    which = [lax.rem(tau + nt - place[1], nt) for tau in range(nt)]
    left = []
    for kind in range(2):
        for tau in range(nt):
            start = pl.multiple_of(kind * width + place[1] * share, share)
            left.append(select(near[which[tau], pl.ds(start, share), :], far_list, slots, width))
    left_high, left_low = halves(jnp.concatenate(left, axis=0))
    high, low = halves(tensor[...])
    middle = dot(
        jnp.concatenate([left_high, left_high, left_low], axis=1), jnp.concatenate([high, low, high], axis=0)
    )
    for group in range(2 * nt):
        for at in range(pairs):
            rows[(group * pairs + at) * share : (group * pairs + at + 1) * share, :] = middle[
                group * share : (group + 1) * share, 2 * width * at : 2 * width * (at + 1)
            ]
    results = []
    for group in range(2 * nt):
        kind, tau = group // nt, group % nt
        right = select(far[which[tau], (1 - kind) * width : (2 - kind) * width, :], near_list, slots, width)
        zero = jnp.zeros_like(right)
        right_high, right_low = halves(
            jnp.concatenate([jnp.concatenate([right, zero], axis=1), jnp.concatenate([zero, right], axis=1)], axis=0)
        )

        rows_high, rows_low = halves(
            jnp.concatenate(
                [rows[pl.ds(group * pairs * share + at, pairs, stride=share), :] for at in range(share)], axis=0
            )
        )
        results.append(
            dot(
                jnp.concatenate([rows_high, rows_high, rows_low], axis=1),
                jnp.concatenate([right_high, right_low, right_high], axis=0),
            )
        )
    return results


def first(place, near, tensor, acc, token, rows, *, slots, width, share):
    token[...] = jnp.zeros_like(token)
    for group, result in enumerate(mix(place, near, near, tensor, rows, slots, width, share)):
        acc[group] = result


def second(place, near, acc, *refs, slots, width, share, others):
    refs, (sides, token, rows) = refs[: 2 * others], refs[-3:]
    tensors, fars = refs[: len(refs) // 2], refs[len(refs) // 2 :]
    token[...] = jnp.zeros_like(token)
    listed = slots * width
    groups, tall, _ = acc.shape
    pairs = tall // share
    total = [acc[group] for group in range(groups)]
    for tensor, far in zip(tensors, fars):
        term = mix(place, near, far, tensor, rows, slots, width, share)
        total = [x + y for x, y in zip(total, term)]
    for group in range(groups):
        height = groups * pairs
        high, low = halves(total[group])
        for odd in range(2):
            row = (2 * (group % (groups // 2)) + odd) * pairs + 2 * height * (group * 2 // groups)
            for at in range(share):
                for part, array in enumerate((high, low)):
                    sides[
                        part * height + row : part * height + row + pairs, at * listed : (at + 1) * listed
                    ] = array[at * pairs : (at + 1) * pairs, odd * listed : (odd + 1) * listed]


def relay(pieces, tensor):
    for i, parts in enumerate(pieces):
        at = 0
        for part in parts:
            per, half, listed = part.shape
            for inner in range(per):
                high, low = halves(part[inner])
                tensor[2 * i * half : (2 * i + 1) * half, at * listed : (at + 1) * listed] = high
                tensor[(2 * i + 1) * half : 2 * (i + 1) * half, at * listed : (at + 1) * listed] = low
                at += 1


def products(tensor, side, half):
    all_parts = dot_nt(tensor, side)
    width = side.shape[0] // 2
    rows = []
    for i in range(tensor.shape[0] // (2 * half)):
        block = all_parts[2 * i * half : (2 * i + 1) * half] + all_parts[(2 * i + 1) * half : 2 * (i + 1) * half]
        rows.append(block[:, :width] + block[:, width:])
    return jnp.concatenate(rows, axis=0)


def unfold(block, ordered, i):
    turned = block.T
    pairs = block.shape[0] // 4
    for group in range(turned.shape[0] // (2 * pairs)):
        for odd in range(2):
            at = (2 * group + odd) * pairs
            ordered[i, pl.ds(2 * group * pairs + odd, pairs, stride=2), :] = turned[at : at + pairs]


def at_sub(place, x, axis):
    zero = jnp.zeros_like(x)
    return by_sub(place, x, zero, axis)


def by_sub(place, own, other, axis):
    return jnp.where(
        place[2] == 0, jnp.concatenate([own, other], axis=axis), jnp.concatenate([other, own], axis=axis)
    )


def fold(place, own, other, ordered):
    unfold(by_sub(place, own, other, 0), ordered, 0)
    back = ordered[0, : own.shape[1], :].T
    half = own.shape[0]
    return jnp.concatenate([back[:half], back[half:]], axis=1)


def meet_own(place, sides, *refs, count):
    refs, (tensor, back, *backs, ordered) = refs[: 4 * count - 3], refs[4 * count - 3 :]
    pieces = [refs[i : i + 2] for i in range(0, 4 * count - 4, 2)] + [refs[-1:]]
    half = refs[0].shape[1]
    relay(pieces, tensor)
    rest = products(tensor[...], sides[sides.shape[0] // 2 :, :], half)
    for i, back_ref in enumerate(backs):
        back_ref[...] = fold(
            place, rest[2 * i * half : (2 * i + 1) * half], rest[(2 * i + 1) * half : 2 * (i + 1) * half], ordered
        )
    back[...] = rest[-half:]


def meet_back(place, sides, own, piece, tensor, back_ref, ordered):
    half = piece.shape[1]
    relay([[piece]], tensor)
    other = products(tensor[...], sides[sides.shape[0] // 2 :, :], half)
    back_ref[...] = fold(place, own[...], other, ordered)


def meet_direct(place, sides, mine, mine_other, own, last, out_ref, tensor, ordered, *, nt, naux):
    count = ordered.shape[0]
    block = ordered.shape[2]
    half = block // 2
    side = sides[: sides.shape[0] // 2, :]
    relay([[mine], [mine_other]], tensor)
    tensor[4 * half :, :] = last[...]
    some = products(tensor[...], side, half)
    own = jnp.concatenate([some[:block], products(own[...], side, half)], axis=0)
    other = some[block:]
    for i in range(count):
        first_half = own[i * block : i * block + half]
        second_half = own[i * block + half : (i + 1) * block] if i < count - 1 else other
        unfold(by_sub(place, first_half, second_half, 0), ordered, i)
    for tau in range(nt):
        here = [jnp.zeros((half, block), F32)] * naux
        for shift in range(count):
            here[(naux - shift) % naux] = ordered[shift, tau * half : (tau + 1) * half, :]
        out_ref[tau] = at_sub(place, jnp.concatenate(here, axis=1), 0)


def complete(place, early, *refs):
    backs, out_ref = refs[:-1], refs[-1]
    nt, block, wide = early.shape
    naux = wide // block
    half = block // 2
    for tau in range(nt):
        parts = [jnp.zeros((block, block), F32)] * naux
        for shift, ref in enumerate(backs, 1):
            upper = ref[:, tau * half : (tau + 1) * half]
            lower = ref[:, (nt + tau) * half : (nt + tau + 1) * half]
            parts[shift] = at_sub(place, jnp.concatenate([upper, lower], axis=0), 1)
        total = early[tau] + jnp.concatenate(parts, axis=1)
        out_ref[tau] = pltpu.roll(total, place[3] * block, 1)


def local(three_center, occupied_green, virtual_green, block_list, sizes):
    nt, naux, nob, nsub = sizes
    slots = three_center.shape[2]
    width = three_center.shape[3]
    columns = three_center.shape[4]
    rows_aux = columns // width
    block_aux = rows_aux * nsub
    norb = occupied_green.shape[1]
    listed = slots * width
    share = width // nt
    nauxf = naux * block_aux
    tensor = three_center.reshape(listed, columns)
    limit = 24 + 3 * max(nob - 2, 0)

    def call(kernel, outs, scratch, flops, *arguments, **options):
        shapes = [jax.ShapeDtypeStruct(shape, kind) for shape, kind in outs]
        size = sum(4 * math.prod(x.shape) for x in arguments)

        def here(*refs):
            kernel([lax.axis_index(axis) for axis in ("orb", "tau", "sub", "aux")], *refs, **options)

        return pl.pallas_call(
            here,
            out_shape=shapes,
            in_specs=[VMEM] * len(arguments),
            out_specs=[VMEM] * len(shapes),
            scratch_shapes=[pltpu.VMEM(shape, kind) for shape, kind in scratch],
            compiler_params=pltpu.CompilerParams(vmem_limit_bytes=limit * MIB),
            cost_estimate=pl.CostEstimate(flops=flops, bytes_accessed=size, transcendentals=0),
            name=kernel.__name__,
        )(*arguments)

    tensors = [lax.ppermute(tensor, "orb", ring(nob, shift)) for shift in range(1, nob)]
    mine, again = call(
        prepare, [((share, rows_aux, listed), F32)] * 2, [((columns + width, listed), F32)], 0, tensor, share=share
    )
    plan = shifts_of(naux)
    swap = ring(nsub, 1)
    small = jnp.concatenate(
        [
            occupied_green,
            virtual_green,
            jnp.pad(block_list.astype(F32), ((0, LIST_ROWS - 1), (0, norb - slots))),
        ]
    )
    near = jnp.stack([small] + [lax.ppermute(small, "tau", ring(nt, shift)) for shift in range(1, nt)])
    groups = 2 * nt
    work = 6 * groups * share * columns * listed * 3
    rows = groups * rows_aux
    depth = share * listed
    options = dict(slots=slots, width=width, share=share)
    acc, token = call(
        first,
        [((groups, rows_aux // 2 * share, 2 * listed), F32), ((8, 128), F32)],
        [((groups * rows_aux // 2 * share + share, 2 * width), F32)],
        0,
        near,
        tensor,
        **options,
    )
    mine_other = lax.ppermute(mine, "sub", swap)
    early = [mine_other]
    for pairs in plan[:-1]:
        parts = call(
            halve, [((share // 2, rows_aux, listed), F32)] * 2, [], 0, lax.ppermute(mine, "aux", pairs), token
        )
        early += [*parts, *(lax.ppermute(part, "sub", swap) for part in parts)]
    (later,) = call(hold, [(again.shape, F32)], [], 0, again, lax.ppermute(token, "sub", swap))
    last = lax.ppermute(later, "aux", plan[-1])
    fars = []
    late_near = after(near, *early)
    for shift in range(1, nob):
        pairs = [(a * nsub + c, b * nsub + (c + 1) % nsub) for a, b in ring(nob, shift) for c in range(nsub)]
        fars.append(lax.ppermute(late_near, ("orb", "sub"), pairs))
    sides, token_late = call(
        second,
        [((2 * rows, depth), BF16), ((8, 128), F32)],
        [((groups * rows_aux // 2 * share + share, 2 * width), F32)],
        work,
        near,
        acc,
        *tensors,
        *fars,
        *early,
        others=nob - 1,
        **options,
    )
    last = after(last, token_late)
    last_other = lax.ppermute(last, "sub", swap)
    count = 1 + len(plan)
    work = 8 * rows * depth * rows_aux
    wide = nt * rows_aux
    shape = ((rows_aux, 2 * wide), F32)
    scratch = lambda count: ((count, wide + 8, block_aux), F32)
    own_rows = 2 * (2 * count - 3) * rows_aux
    own, back, *backs = call(
        meet_own,
        [((own_rows, depth), BF16), ((rows_aux, wide), F32)] + [shape] * (len(plan) - 1),
        [scratch(1)],
        work * (2 * count - 3),
        sides,
        *early[1:],
        last,
        count=len(plan),
    )
    tensor, *last_back = call(
        meet_back,
        [((2 * rows_aux, depth), BF16), shape],
        [scratch(1)],
        work,
        sides,
        back,
        last_other,
    )
    backs += last_back
    returned = [
        lax.ppermute(back, "aux", [(target, source) for source, target in pairs]) for back, pairs in zip(backs, plan)
    ]
    shape = ((nt, block_aux, nauxf), F32)
    (direct,) = call(
        meet_direct,
        [shape],
        [((6 * rows_aux, depth), BF16), scratch(count)],
        work * (2 * count),
        sides,
        mine,
        mine_other,
        own,
        tensor,
        nt=nt,
        naux=naux,
    )
    (partial_chi,) = call(complete, [shape], [], 0, direct, *returned)
    owners = nt * nob * nsub
    received = lax.all_to_all(
        partial_chi.reshape(owners, nt * block_aux // owners, nauxf),
        ("tau", "orb", "sub"),
        split_axis=0,
        concat_axis=0,
        tiled=True,
    )
    return received.sum(axis=0) * (-2.0 / math.sqrt(norb * slots * width))


def solution(mesh):
    sizes = tuple(mesh.shape[axis] for axis in ("tau", "aux", "orb", "sub"))
    in_specs = (
        P("aux", "orb", None, None, "sub"),
        P(("tau", "orb"), None),
        P(("tau", "orb"), None),
        P("orb", None),
    )
    out_specs = P(("tau", "aux", "orb", "sub"), None)
    return jax.shard_map(
        functools.partial(local, sizes=sizes), mesh=mesh, in_specs=in_specs, out_specs=out_specs, check_vma=False
    )
```

```python
import functools
import math

import jax
import jax.numpy as jnp
from jax import lax
from jax.experimental import pallas as pl
from jax.experimental.pallas import tpu as pltpu
from jax.sharding import PartitionSpec as P

VMEM = pl.BlockSpec(memory_space=pltpu.VMEM)
ANY = pl.BlockSpec(memory_space=pl.ANY)
HBM = pl.BlockSpec(memory_space=pltpu.HBM)
F32 = jnp.float32
BF16 = jnp.bfloat16
LIST_ROWS = 8
MIB = 1024 * 1024


def halves(x):
    high = x.astype(BF16)
    return high, (x - high.astype(F32)).astype(BF16)


def dot(a, b):
    return lax.dot_general(a, b, (((1,), (0,)), ((), ())), preferred_element_type=F32)


def dot_nt(a, b):
    return lax.dot_general(a, b, (((1,), (1,)), ((), ())), preferred_element_type=F32)


def ring(count, shift):
    return [((target + shift) % count, target) for target in range(count)]


def prepare(place, tensor, mine, again, turned, *, share):
    some = mine.shape[1]
    columns = tensor.shape[1]
    turned[:columns, :] = tensor[...].T
    start = place[1] * share
    for at in range(share):
        rows = turned[pl.ds(start + at, some, stride=columns // some), :]
        mine[at] = rows
        again[at] = rows


def halve(place, block, token, *outs):
    some = outs[0].shape[0]
    for i, out in enumerate(outs):
        out[...] = block[i * some : (i + 1) * some]


def after(block, *tokens):
    return pl.pallas_call(
        lambda *refs: None,
        out_shape=jax.ShapeDtypeStruct(block.shape, block.dtype),
        in_specs=[ANY] * (1 + len(tokens)),
        out_specs=ANY,
        input_output_aliases={0: 0},
        compiler_params=pltpu.CompilerParams(vmem_limit_bytes=MIB),
        name="after",
    )(block, *tokens)


def shifts_of(naux):
    plan = []
    for shift in range(1, naux // 2 + 1):
        if 2 * shift < naux:
            plan.append([(source, (source + shift) % naux) for source in range(naux)])
        else:
            plan.append([(z, z + shift) if z % 2 else (z + shift, z) for z in range(shift)])
    return plan


def select(block, list_rows, slots, width):
    parts = []
    for slot in range(slots):
        entry = list_rows[:1, slot : slot + 1]
        chosen = jnp.zeros((block.shape[0], width), F32)
        for j in range(block.shape[1] // width):
            chosen = jnp.where(entry == float(j), block[:, j * width : (j + 1) * width], chosen)
        parts.append(chosen)
    return jnp.concatenate(parts, axis=1)


def mix(place, near, far, tensor, rows, slots, width, share):
    nt = near.shape[0]
    pairs = tensor.shape[1] // (2 * width)
    near_list, far_list = near[0, 2 * width :, :], far[0, 2 * width :, :]
    which = [lax.rem(tau + nt - place[1], nt) for tau in range(nt)]
    left = []
    for kind in range(2):
        for tau in range(nt):
            start = pl.multiple_of(kind * width + place[1] * share, share)
            left.append(select(near[which[tau], pl.ds(start, share), :], far_list, slots, width))
    left_high, left_low = halves(jnp.concatenate(left, axis=0))
    high, low = halves(tensor[...])
    middle = dot(
        jnp.concatenate([left_high, left_high, left_low], axis=1), jnp.concatenate([high, low, high], axis=0)
    )
    for group in range(2 * nt):
        for at in range(pairs):
            rows[(group * pairs + at) * share : (group * pairs + at + 1) * share, :] = middle[
                group * share : (group + 1) * share, 2 * width * at : 2 * width * (at + 1)
            ]
    results = []
    for group in range(2 * nt):
        kind, tau = group // nt, group % nt
        right = select(far[which[tau], (1 - kind) * width : (2 - kind) * width, :], near_list, slots, width)
        zero = jnp.zeros_like(right)
        right_high, right_low = halves(
            jnp.concatenate([jnp.concatenate([right, zero], axis=1), jnp.concatenate([zero, right], axis=1)], axis=0)
        )

        rows_high, rows_low = halves(
            jnp.concatenate(
                [rows[pl.ds(group * pairs * share + at, pairs, stride=share), :] for at in range(share)], axis=0
            )
        )
        results.append(
            dot(
                jnp.concatenate([rows_high, rows_high, rows_low], axis=1),
                jnp.concatenate([right_high, right_low, right_high], axis=0),
            )
        )
    return results


def first(place, near, tensor, acc, token, rows, *, slots, width, share):
    token[...] = jnp.zeros_like(token)
    for group, result in enumerate(mix(place, near, near, tensor, rows, slots, width, share)):
        acc[group] = result


def second(place, near, acc, *refs, slots, width, share, others):
    refs, (sides, token, rows) = refs[: 2 * others], refs[-3:]
    tensors, fars = refs[: len(refs) // 2], refs[len(refs) // 2 :]
    token[...] = jnp.zeros_like(token)
    listed = slots * width
    groups, tall, _ = acc.shape
    pairs = tall // share
    total = [acc[group] for group in range(groups)]
    for tensor, far in zip(tensors, fars):
        term = mix(place, near, far, tensor, rows, slots, width, share)
        total = [x + y for x, y in zip(total, term)]
    for group in range(groups):
        height = groups * pairs
        high, low = halves(total[group])
        for odd in range(2):
            row = (2 * (group % (groups // 2)) + odd) * pairs + 2 * height * (group * 2 // groups)
            for at in range(share):
                for part, array in enumerate((high, low)):
                    sides[
                        part * height + row : part * height + row + pairs, at * listed : (at + 1) * listed
                    ] = array[at * pairs : (at + 1) * pairs, odd * listed : (odd + 1) * listed]


def relay(pieces, tensor):
    for i, parts in enumerate(pieces):
        at = 0
        for part in parts:
            per, half, listed = part.shape
            for inner in range(per):
                high, low = halves(part[inner])
                tensor[2 * i * half : (2 * i + 1) * half, at * listed : (at + 1) * listed] = high
                tensor[(2 * i + 1) * half : 2 * (i + 1) * half, at * listed : (at + 1) * listed] = low
                at += 1


def products(tensor, side, half):
    all_parts = dot_nt(tensor, side)
    width = side.shape[0] // 2
    rows = []
    for i in range(tensor.shape[0] // (2 * half)):
        block = all_parts[2 * i * half : (2 * i + 1) * half] + all_parts[(2 * i + 1) * half : 2 * (i + 1) * half]
        rows.append(block[:, :width] + block[:, width:])
    return jnp.concatenate(rows, axis=0)


def unfold(block, ordered, i):
    turned = block.T
    pairs = block.shape[0] // 4
    for group in range(turned.shape[0] // (2 * pairs)):
        for odd in range(2):
            at = (2 * group + odd) * pairs
            ordered[i, pl.ds(2 * group * pairs + odd, pairs, stride=2), :] = turned[at : at + pairs]


def at_sub(place, x, axis):
    zero = jnp.zeros_like(x)
    return by_sub(place, x, zero, axis)


def by_sub(place, own, other, axis):
    return jnp.where(
        place[2] == 0, jnp.concatenate([own, other], axis=axis), jnp.concatenate([other, own], axis=axis)
    )


def fold(place, own, other, ordered):
    unfold(by_sub(place, own, other, 0), ordered, 0)
    back = ordered[0, : own.shape[1], :].T
    half = own.shape[0]
    return jnp.concatenate([back[:half], back[half:]], axis=1)


def split(place, *refs):
    refs, tensor = refs[:-1], refs[-1]
    relay([refs[:1], refs[1:2]] + [refs[i : i + 2] for i in range(2, len(refs), 2)], tensor)


def meet_own(place, sides, ready, last, tensor, back, *refs):
    backs, ordered = refs[:-1], refs[-1]
    half = last.shape[1]
    some = tensor.shape[0] - 2 * half
    if some:
        tensor[:some, :] = ready[4 * half :, :]
    relay([[last]], tensor.at[some:, :])
    rest = products(tensor[...], sides[sides.shape[0] // 2 :, :], half)
    for i, back_ref in enumerate(backs):
        back_ref[...] = fold(
            place, rest[2 * i * half : (2 * i + 1) * half], rest[(2 * i + 1) * half : 2 * (i + 1) * half], ordered
        )
    back[...] = rest[-half:]


def meet_back(place, sides, own, piece, tensor, back_ref, ordered):
    half = piece.shape[1]
    relay([[piece]], tensor)
    other = products(tensor[...], sides[sides.shape[0] // 2 :, :], half)
    back_ref[...] = fold(place, own[...], other, ordered)


def meet_direct(place, sides, ready, own, last, out_ref, tensor, ordered, *, nt, naux):
    count = ordered.shape[0]
    block = ordered.shape[2]
    half = block // 2
    side = sides[: sides.shape[0] // 2, :]
    tensor[: 4 * half, :] = ready[: 4 * half, :]
    tensor[4 * half :, :] = last[...]
    some = products(tensor[...], side, half)
    own = jnp.concatenate([some[:block], products(own[...], side, half)], axis=0)
    other = some[block:]
    for i in range(count):
        first_half = own[i * block : i * block + half]
        second_half = own[i * block + half : (i + 1) * block] if i < count - 1 else other
        unfold(by_sub(place, first_half, second_half, 0), ordered, i)
    for tau in range(nt):
        here = [jnp.zeros((half, block), F32)] * naux
        for shift in range(count):
            here[(naux - shift) % naux] = ordered[shift, tau * half : (tau + 1) * half, :]
        out_ref[tau] = at_sub(place, jnp.concatenate(here, axis=1), 0)


def complete(place, early, *refs):
    backs, out_ref = refs[:-1], refs[-1]
    nt, block, wide = early.shape
    naux = wide // block
    half = block // 2
    for tau in range(nt):
        parts = [jnp.zeros((block, block), F32)] * naux
        for shift, ref in enumerate(backs, 1):
            upper = ref[:, tau * half : (tau + 1) * half]
            lower = ref[:, (nt + tau) * half : (nt + tau + 1) * half]
            parts[shift] = at_sub(place, jnp.concatenate([upper, lower], axis=0), 1)
        total = early[tau] + jnp.concatenate(parts, axis=1)
        out_ref[tau] = pltpu.roll(total, place[3] * block, 1)


def local(three_center, occupied_green, virtual_green, block_list, sizes):
    nt, naux, nob, nsub = sizes
    slots = three_center.shape[2]
    width = three_center.shape[3]
    columns = three_center.shape[4]
    rows_aux = columns // width
    block_aux = rows_aux * nsub
    norb = occupied_green.shape[1]
    listed = slots * width
    share = width // nt
    nauxf = naux * block_aux
    tensor = three_center.reshape(listed, columns)
    limit = 24 + 3 * max(nob - 2, 0)

    def call(kernel, outs, scratch, flops, *arguments, **options):
        shapes = [jax.ShapeDtypeStruct(shape, kind) for shape, kind in outs]
        size = sum(4 * math.prod(x.shape) for x in arguments)

        def here(*refs):
            kernel([lax.axis_index(axis) for axis in ("orb", "tau", "sub", "aux")], *refs, **options)

        return pl.pallas_call(
            here,
            out_shape=shapes,
            in_specs=[VMEM] * len(arguments),
            out_specs=[VMEM] * len(shapes),
            scratch_shapes=[pltpu.VMEM(shape, kind) for shape, kind in scratch],
            compiler_params=pltpu.CompilerParams(vmem_limit_bytes=limit * MIB),
            cost_estimate=pl.CostEstimate(flops=flops, bytes_accessed=size, transcendentals=0),
            name=kernel.__name__,
        )(*arguments)

    tensors = [lax.ppermute(tensor, "orb", ring(nob, shift)) for shift in range(1, nob)]
    mine, again = call(
        prepare, [((share, rows_aux, listed), F32)] * 2, [((columns + width, listed), F32)], 0, tensor, share=share
    )
    plan = shifts_of(naux)
    swap = ring(nsub, 1)
    small = jnp.concatenate(
        [
            occupied_green,
            virtual_green,
            jnp.pad(block_list.astype(F32), ((0, LIST_ROWS - 1), (0, norb - slots))),
        ]
    )
    near = jnp.stack([small] + [lax.ppermute(small, "tau", ring(nt, shift)) for shift in range(1, nt)])
    groups = 2 * nt
    work = 6 * groups * share * columns * listed * 3
    rows = groups * rows_aux
    depth = share * listed
    options = dict(slots=slots, width=width, share=share)
    acc, token = call(
        first,
        [((groups, rows_aux // 2 * share, 2 * listed), F32), ((8, 128), F32)],
        [((groups * rows_aux // 2 * share + share, 2 * width), F32)],
        0,
        near,
        tensor,
        **options,
    )
    mine_other = lax.ppermute(mine, "sub", swap)
    early = [mine_other]
    for pairs in plan[:-1]:
        parts = call(
            halve, [((share // 2, rows_aux, listed), F32)] * 2, [], 0, lax.ppermute(mine, "aux", pairs), token
        )
        early += [*parts, *(lax.ppermute(part, "sub", swap) for part in parts)]
    last = lax.ppermute(after(again, lax.ppermute(token, "sub", swap)), "aux", plan[-1])
    fars = []
    (ready,) = call(split, [((4 * len(plan) * rows_aux, share * listed), BF16)], [], 0, mine, *early)
    late_near = after(near, ready)
    for shift in range(1, nob):
        pairs = [(a * nsub + c, b * nsub + (c + 1) % nsub) for a, b in ring(nob, shift) for c in range(nsub)]
        fars.append(lax.ppermute(late_near, ("orb", "sub"), pairs))
    sides, token_late = call(
        second,
        [((2 * rows, depth), BF16), ((8, 128), F32)],
        [((groups * rows_aux // 2 * share + share, 2 * width), F32)],
        work,
        near,
        acc,
        *tensors,
        *fars,
        *early,
        others=nob - 1,
        **options,
    )
    last = after(last, token_late)
    last_other = lax.ppermute(last, "sub", swap)
    count = 1 + len(plan)
    work = 8 * rows * depth * rows_aux
    wide = nt * rows_aux
    shape = ((rows_aux, 2 * wide), F32)
    scratch = lambda count: ((count, wide + 8, block_aux), F32)
    own_rows = 2 * (2 * count - 3) * rows_aux
    own, back, *backs = call(
        meet_own,
        [((own_rows, depth), BF16), ((rows_aux, wide), F32)] + [shape] * (len(plan) - 1),
        [scratch(1)],
        work * (2 * count - 3),
        sides,
        ready,
        last,
    )
    tensor, *last_back = call(
        meet_back,
        [((2 * rows_aux, depth), BF16), shape],
        [scratch(1)],
        work,
        sides,
        back,
        last_other,
    )
    backs += last_back
    returned = [
        lax.ppermute(back, "aux", [(target, source) for source, target in pairs]) for back, pairs in zip(backs, plan)
    ]
    shape = ((nt, block_aux, nauxf), F32)
    (direct,) = call(
        meet_direct,
        [shape],
        [((6 * rows_aux, depth), BF16), scratch(count)],
        work * (2 * count),
        sides,
        ready,
        own,
        tensor,
        nt=nt,
        naux=naux,
    )
    (partial_chi,) = call(complete, [shape], [], 0, direct, *returned)
    owners = nt * nob * nsub
    received = lax.all_to_all(
        partial_chi.reshape(owners, nt * block_aux // owners, nauxf),
        ("tau", "orb", "sub"),
        split_axis=0,
        concat_axis=0,
        tiled=True,
    )
    return received.sum(axis=0) * (-2.0 / math.sqrt(norb * slots * width))


def solution(mesh):
    sizes = tuple(mesh.shape[axis] for axis in ("tau", "aux", "orb", "sub"))
    in_specs = (
        P("aux", "orb", None, None, "sub"),
        P(("tau", "orb"), None),
        P(("tau", "orb"), None),
        P("orb", None),
    )
    out_specs = P(("tau", "aux", "orb", "sub"), None)
    return jax.shard_map(
        functools.partial(local, sizes=sizes), mesh=mesh, in_specs=in_specs, out_specs=out_specs, check_vma=False
    )
```

```python
import functools
import math

import jax
import jax.numpy as jnp
from jax import lax
from jax.experimental import pallas as pl
from jax.experimental.pallas import tpu as pltpu
from jax.sharding import PartitionSpec as P

VMEM = pl.BlockSpec(memory_space=pltpu.VMEM)
ANY = pl.BlockSpec(memory_space=pl.ANY)
HBM = pl.BlockSpec(memory_space=pltpu.HBM)
F32 = jnp.float32
BF16 = jnp.bfloat16
LIST_ROWS = 8
MIB = 1024 * 1024


def halves(x):
    high = x.astype(BF16)
    return high, (x - high.astype(F32)).astype(BF16)


def dot(a, b):
    return lax.dot_general(a, b, (((1,), (0,)), ((), ())), preferred_element_type=F32)


def dot_nt(a, b):
    return lax.dot_general(a, b, (((1,), (1,)), ((), ())), preferred_element_type=F32)


def ring(count, shift):
    return [((target + shift) % count, target) for target in range(count)]


def prepare(place, tensor, mine, again, turned, *, share):
    some = mine.shape[1]
    columns = tensor.shape[1]
    turned[:columns, :] = tensor[...].T
    start = place[1] * share
    for at in range(share):
        rows = turned[pl.ds(start + at, some, stride=columns // some), :]
        mine[at] = rows
        again[at] = rows


def halve(place, block, token, *outs):
    some = outs[0].shape[0]
    for i, out in enumerate(outs):
        out[...] = block[i * some : (i + 1) * some]


def after(block, *tokens):
    return pl.pallas_call(
        lambda *refs: None,
        out_shape=jax.ShapeDtypeStruct(block.shape, block.dtype),
        in_specs=[ANY] * (1 + len(tokens)),
        out_specs=ANY,
        input_output_aliases={0: 0},
        compiler_params=pltpu.CompilerParams(vmem_limit_bytes=MIB),
        name="after",
    )(block, *tokens)


def shifts_of(naux):
    plan = []
    for shift in range(1, naux // 2 + 1):
        if 2 * shift < naux:
            plan.append([(source, (source + shift) % naux) for source in range(naux)])
        else:
            plan.append([(z, z + shift) if z % 2 else (z + shift, z) for z in range(shift)])
    return plan


def select(block, list_rows, slots, width):
    parts = []
    for slot in range(slots):
        entry = list_rows[:1, slot : slot + 1]
        chosen = jnp.zeros((block.shape[0], width), F32)
        for j in range(block.shape[1] // width):
            chosen = jnp.where(entry == float(j), block[:, j * width : (j + 1) * width], chosen)
        parts.append(chosen)
    return jnp.concatenate(parts, axis=1)


def mix(place, near, far, tensor, rows, slots, width, share):
    nt = near.shape[0]
    pairs = tensor.shape[1] // (2 * width)
    near_list, far_list = near[0, 2 * width :, :], far[0, 2 * width :, :]
    which = [lax.rem(tau + nt - place[1], nt) for tau in range(nt)]
    left = []
    for kind in range(2):
        for tau in range(nt):
            start = pl.multiple_of(kind * width + place[1] * share, share)
            left.append(select(near[which[tau], pl.ds(start, share), :], far_list, slots, width))
    left_high, left_low = halves(jnp.concatenate(left, axis=0))
    high, low = halves(tensor[...])
    middle = dot(
        jnp.concatenate([left_high, left_high, left_low], axis=1), jnp.concatenate([high, low, high], axis=0)
    )
    for group in range(2 * nt):
        for at in range(pairs):
            rows[(group * pairs + at) * share : (group * pairs + at + 1) * share, :] = middle[
                group * share : (group + 1) * share, 2 * width * at : 2 * width * (at + 1)
            ]
    results = []
    for group in range(2 * nt):
        kind, tau = group // nt, group % nt
        right = select(far[which[tau], (1 - kind) * width : (2 - kind) * width, :], near_list, slots, width)
        zero = jnp.zeros_like(right)
        right_high, right_low = halves(
            jnp.concatenate([jnp.concatenate([right, zero], axis=1), jnp.concatenate([zero, right], axis=1)], axis=0)
        )

        rows_high, rows_low = halves(
            jnp.concatenate(
                [rows[pl.ds(group * pairs * share + at, pairs, stride=share), :] for at in range(share)], axis=0
            )
        )
        results.append(
            dot(
                jnp.concatenate([rows_high, rows_high, rows_low], axis=1),
                jnp.concatenate([right_high, right_low, right_high], axis=0),
            )
        )
    return results


def first(place, near, tensor, acc, token, rows, *, slots, width, share):
    token[...] = jnp.zeros_like(token)
    for group, result in enumerate(mix(place, near, near, tensor, rows, slots, width, share)):
        acc[group] = result


def second(place, near, acc, *refs, slots, width, share, others):
    refs, (sides, token, rows) = refs[: 2 * others], refs[-3:]
    tensors, fars = refs[: len(refs) // 2], refs[len(refs) // 2 :]
    token[...] = jnp.zeros_like(token)
    listed = slots * width
    groups, tall, _ = acc.shape
    pairs = tall // share
    total = [acc[group] for group in range(groups)]
    for tensor, far in zip(tensors, fars):
        term = mix(place, near, far, tensor, rows, slots, width, share)
        total = [x + y for x, y in zip(total, term)]
    for group in range(groups):
        height = groups * pairs
        high, low = halves(total[group])
        for odd in range(2):
            row = (2 * (group % (groups // 2)) + odd) * pairs + 2 * height * (group * 2 // groups)
            for at in range(share):
                for part, array in enumerate((high, low)):
                    sides[
                        part * height + row : part * height + row + pairs, at * listed : (at + 1) * listed
                    ] = array[at * pairs : (at + 1) * pairs, odd * listed : (odd + 1) * listed]


def relay(pieces, tensor):
    for i, parts in enumerate(pieces):
        at = 0
        for part in parts:
            per, half, listed = part.shape
            for inner in range(per):
                high, low = halves(part[inner])
                tensor[2 * i * half : (2 * i + 1) * half, at * listed : (at + 1) * listed] = high
                tensor[(2 * i + 1) * half : 2 * (i + 1) * half, at * listed : (at + 1) * listed] = low
                at += 1


def products(tensor, side, half):
    all_parts = dot_nt(tensor, side)
    width = side.shape[0] // 2
    rows = []
    for i in range(tensor.shape[0] // (2 * half)):
        block = all_parts[2 * i * half : (2 * i + 1) * half] + all_parts[(2 * i + 1) * half : 2 * (i + 1) * half]
        rows.append(block[:, :width] + block[:, width:])
    return jnp.concatenate(rows, axis=0)


def unfold(block, ordered, i):
    turned = block.T
    pairs = block.shape[0] // 4
    for group in range(turned.shape[0] // (2 * pairs)):
        for odd in range(2):
            at = (2 * group + odd) * pairs
            ordered[i, pl.ds(2 * group * pairs + odd, pairs, stride=2), :] = turned[at : at + pairs]


def at_sub(place, x, axis):
    zero = jnp.zeros_like(x)
    return by_sub(place, x, zero, axis)


def by_sub(place, own, other, axis):
    return jnp.where(
        place[2] == 0, jnp.concatenate([own, other], axis=axis), jnp.concatenate([other, own], axis=axis)
    )


def fold(place, own, other, ordered):
    unfold(by_sub(place, own, other, 0), ordered, 0)
    back = ordered[0, : own.shape[1], :].T
    half = own.shape[0]
    return jnp.concatenate([back[:half], back[half:]], axis=1)


def meet_own(place, sides, *refs, count):
    refs, (tensor, back, *backs, ordered) = refs[: 4 * count - 3], refs[4 * count - 3 :]
    pieces = [refs[i : i + 2] for i in range(0, 4 * count - 4, 2)] + [refs[-1:]]
    half = refs[0].shape[1]
    relay(pieces, tensor)
    rest = products(tensor[...], sides[sides.shape[0] // 2 :, :], half)
    for i, back_ref in enumerate(backs):
        back_ref[...] = fold(
            place, rest[2 * i * half : (2 * i + 1) * half], rest[(2 * i + 1) * half : 2 * (i + 1) * half], ordered
        )
    back[...] = rest[-half:]


def meet_back(place, sides, own, piece, tensor, back_ref, ordered):
    half = piece.shape[1]
    relay([[piece]], tensor)
    other = products(tensor[...], sides[sides.shape[0] // 2 :, :], half)
    back_ref[...] = fold(place, own[...], other, ordered)


def meet_direct(place, sides, mine, mine_other, own, last, out_ref, tensor, ordered, *, nt, naux):
    count = ordered.shape[0]
    block = ordered.shape[2]
    half = block // 2
    side = sides[: sides.shape[0] // 2, :]
    relay([[mine], [mine_other]], tensor)
    tensor[4 * half :, :] = last[...]
    some = products(tensor[...], side, half)
    own = jnp.concatenate([some[:block], products(own[...], side, half)], axis=0)
    other = some[block:]
    for i in range(count):
        first_half = own[i * block : i * block + half]
        second_half = own[i * block + half : (i + 1) * block] if i < count - 1 else other
        unfold(by_sub(place, first_half, second_half, 0), ordered, i)
    for tau in range(nt):
        here = [jnp.zeros((half, block), F32)] * naux
        for shift in range(count):
            here[(naux - shift) % naux] = ordered[shift, tau * half : (tau + 1) * half, :]
        out_ref[tau] = at_sub(place, jnp.concatenate(here, axis=1), 0)


def complete(place, early, *refs, nsub):
    backs, out_ref = refs[:-1], refs[-1]
    nt, block, wide = early.shape
    naux = wide // block
    half = block // 2
    for tau in range(nt):
        parts = [jnp.zeros((block, block), F32)] * naux
        for shift, ref in enumerate(backs, 1):
            upper = ref[:, tau * half : (tau + 1) * half]
            lower = ref[:, (nt + tau) * half : (nt + tau + 1) * half]
            parts[shift] = at_sub(place, jnp.concatenate([upper, lower], axis=0), 1)
        total = early[tau] + jnp.concatenate(parts, axis=1)
        total = pltpu.roll(total, place[3] * block, 1)
        owners, rows, _ = out_ref.shape
        nob = owners // (nt * nsub)
        for i in range(nob * nsub):
            out_ref[((i % nsub) * nob + i // nsub) * nt + tau] = total[i * rows : (i + 1) * rows]


def local(three_center, occupied_green, virtual_green, block_list, sizes):
    nt, naux, nob, nsub = sizes
    slots = three_center.shape[2]
    width = three_center.shape[3]
    columns = three_center.shape[4]
    rows_aux = columns // width
    block_aux = rows_aux * nsub
    norb = occupied_green.shape[1]
    listed = slots * width
    share = width // nt
    nauxf = naux * block_aux
    tensor = three_center.reshape(listed, columns)
    limit = 24 + 3 * max(nob - 2, 0)

    def call(kernel, outs, scratch, flops, *arguments, **options):
        shapes = [jax.ShapeDtypeStruct(shape, kind) for shape, kind in outs]
        size = sum(4 * math.prod(x.shape) for x in arguments)

        def here(*refs):
            kernel([lax.axis_index(axis) for axis in ("orb", "tau", "sub", "aux")], *refs, **options)

        return pl.pallas_call(
            here,
            out_shape=shapes,
            in_specs=[VMEM] * len(arguments),
            out_specs=[VMEM] * len(shapes),
            scratch_shapes=[pltpu.VMEM(shape, kind) for shape, kind in scratch],
            compiler_params=pltpu.CompilerParams(vmem_limit_bytes=limit * MIB),
            cost_estimate=pl.CostEstimate(flops=flops, bytes_accessed=size, transcendentals=0),
            name=kernel.__name__,
        )(*arguments)

    tensors = [lax.ppermute(tensor, "orb", ring(nob, shift)) for shift in range(1, nob)]
    mine, again = call(
        prepare, [((share, rows_aux, listed), F32)] * 2, [((columns + width, listed), F32)], 0, tensor, share=share
    )
    plan = shifts_of(naux)
    swap = ring(nsub, 1)
    small = jnp.concatenate(
        [
            occupied_green,
            virtual_green,
            jnp.pad(block_list.astype(F32), ((0, LIST_ROWS - 1), (0, norb - slots))),
        ]
    )
    near = jnp.stack([small] + [lax.ppermute(small, "tau", ring(nt, shift)) for shift in range(1, nt)])
    groups = 2 * nt
    work = 6 * groups * share * columns * listed * 3
    rows = groups * rows_aux
    depth = share * listed
    options = dict(slots=slots, width=width, share=share)
    acc, token = call(
        first,
        [((groups, rows_aux // 2 * share, 2 * listed), F32), ((8, 128), F32)],
        [((groups * rows_aux // 2 * share + share, 2 * width), F32)],
        0,
        near,
        tensor,
        **options,
    )
    mine_other = lax.ppermute(mine, "sub", swap)
    early = [mine_other]
    for pairs in plan[:-1]:
        parts = call(
            halve, [((share // 2, rows_aux, listed), F32)] * 2, [], 0, lax.ppermute(mine, "aux", pairs), token
        )
        early += [*parts, *(lax.ppermute(part, "sub", swap) for part in parts)]
    last = lax.ppermute(after(again, lax.ppermute(token, "sub", swap)), "aux", plan[-1])
    fars = []
    late_near = after(near, *early)
    for shift in range(1, nob):
        pairs = [(a * nsub + c, b * nsub + (c + 1) % nsub) for a, b in ring(nob, shift) for c in range(nsub)]
        fars.append(lax.ppermute(late_near, ("orb", "sub"), pairs))
    sides, token_late = call(
        second,
        [((2 * rows, depth), BF16), ((8, 128), F32)],
        [((groups * rows_aux // 2 * share + share, 2 * width), F32)],
        work,
        near,
        acc,
        *tensors,
        *fars,
        *early,
        others=nob - 1,
        **options,
    )
    last = after(last, token_late)
    last_other = lax.ppermute(last, "sub", swap)
    count = 1 + len(plan)
    work = 8 * rows * depth * rows_aux
    wide = nt * rows_aux
    shape = ((rows_aux, 2 * wide), F32)
    scratch = lambda count: ((count, wide + 8, block_aux), F32)
    own_rows = 2 * (2 * count - 3) * rows_aux
    own, back, *backs = call(
        meet_own,
        [((own_rows, depth), BF16), ((rows_aux, wide), F32)] + [shape] * (len(plan) - 1),
        [scratch(1)],
        work * (2 * count - 3),
        sides,
        *early[1:],
        last,
        count=len(plan),
    )
    tensor, *last_back = call(
        meet_back,
        [((2 * rows_aux, depth), BF16), shape],
        [scratch(1)],
        work,
        sides,
        back,
        last_other,
    )
    backs += last_back
    returned = [
        lax.ppermute(back, "aux", [(target, source) for source, target in pairs]) for back, pairs in zip(backs, plan)
    ]
    shape = ((nt, block_aux, nauxf), F32)
    (direct,) = call(
        meet_direct,
        [shape],
        [((6 * rows_aux, depth), BF16), scratch(count)],
        work * (2 * count),
        sides,
        mine,
        mine_other,
        own,
        tensor,
        nt=nt,
        naux=naux,
    )
    owners = nt * nob * nsub
    shape = ((owners, nt * block_aux // owners, nauxf), F32)
    (partial_chi,) = call(complete, [shape], [], 0, direct, *returned, nsub=nsub)
    received = lax.all_to_all(partial_chi, ("sub", "orb", "tau"), split_axis=0, concat_axis=0, tiled=True)
    return received.sum(axis=0) * (-2.0 / math.sqrt(norb * slots * width))


def solution(mesh):
    sizes = tuple(mesh.shape[axis] for axis in ("tau", "aux", "orb", "sub"))
    in_specs = (
        P("aux", "orb", None, None, "sub"),
        P(("tau", "orb"), None),
        P(("tau", "orb"), None),
        P("orb", None),
    )
    out_specs = P(("tau", "aux", "orb", "sub"), None)
    return jax.shard_map(
        functools.partial(local, sizes=sizes), mesh=mesh, in_specs=in_specs, out_specs=out_specs, check_vma=False
    )
```
